32 devices in a mesh: parts: 2 (over y), dp: 16 (over z, x, core).
Axes of the slice: x: 2, y: 2, z: 4, core: 2. Of those that a mesh axis runs over, the one named last changes fastest.
Arguments:
- features: bfloat16 [16384, 256], P(('parts', 'dp')), parts along dimension 0, may hold values from -16 to 16
- kernel_map: int32 [16384, 27], P(('parts', 'dp')), parts along dimension 0, may hold values from 384 to 1536, as said below
- occupancy: int32 [32], P(('parts', 'dp')), parts along dimension 0, may hold values from 256 to 512, as said below
- weights: bfloat16 [27, 256, 256], replicated, may hold values from -0.1875 to 0.1875
- bn_gain: float32 [256], replicated, may hold values from 0.5 to 1.5
- bn_shift: float32 [256], replicated, may hold values from -3 to 3
- cotangent: bfloat16 [16384, 256], P(('parts', 'dp')), parts along dimension 0, may hold values from -6 to 6
Outputs:
- block_out: bfloat16 [16384, 256], P(('parts', 'dp')), parts along dimension 0
- grad_features: bfloat16 [16384, 256], P(('parts', 'dp')), parts along dimension 0
- grad_weights: bfloat16 [54, 256, 256], P('parts'), parts along dimension 0
- grad_gain: float32 [512], P('parts'), parts along dimension 0
- grad_shift: float32 [512], P('parts'), parts along dimension 0
The draws below stay inside these ranges and needn't reach their ends.
There are 2 independent parts, one for each index of `parts`. The reference program is written for one: setup_inputs(seed, part) draws one part's arguments, and reference() takes and returns one part's arrays. A program takes and returns all parts, laid end to end along the dimension named above; an argument that names none is the same for every part. Nothing has to cross between parts.
Inputs may be any that keep to these rules, and one draw needn't show every extreme that they name: `kernel_map`: entry [r, k] names, for an occupied row r of device d, its neighbour at offset k as a row of the rows of devices d - 1, d and d + 1 laid end to end, or 1536 for none; column 13 names r itself. A row in block b of its device (128 rows a block) names only rows of blocks b - 1, b and b + 1, counted in that concatenation around d's own rows; so neighbours on device d - 1 lie in its last 128 rows and are named only by the first 128 rows of d, and neighbours on d + 1 lie in its first 128 rows and are named only by the last 128 rows of d; the first and last device name none beyond the slab. Only occupied rows are named, and unoccupied rows name none. `occupancy`: a multiple of 128; a device's occupied rows are its first 128, its last 128, and the occupancy - 256 rows after its first 128.
All inputs are finite; a program needn't handle non-finite values.
Results may differ from the reference program's by a relative error of at most 0.0056.
Values may be sent and summed in bfloat16 or wider, within the bound.
No kernel may reach another device: no remote copies, remote signals or barrier semaphores. Data moves between devices by JAX's collectives and lax.ppermute only.
A program may use at most 64 MiB of HBM per device.

```python
import jax
import jax.numpy as jnp
from jax import lax

C = 256
K = 27
BLOCK = 128
VOX_DEV = 512
VOXELS = 8192


def occupied_counts(key):
    key = jax.random.fold_in(key, 11)
    device_count = VOXELS // VOX_DEV
    block_count = VOX_DEV // BLOCK
    left_key, right_key = jax.random.split(key)
    upper_bound = block_count - 1
    factor_one = jax.random.randint(left_key, (device_count,), 0, upper_bound)
    factor_two = jax.random.randint(right_key, (device_count,), 0, upper_bound)
    extra_blocks = factor_one * factor_two // max(block_count - 2, 1)
    block_total = 2 + extra_blocks
    device_index = jnp.arange(device_count)
    block_total = jnp.where(device_index == 0, block_count, jnp.where(device_index == 1, 2, block_total))
    return (block_total * BLOCK).astype(jnp.int32)


def draw_occupancy(key, part):
    counted = occupied_counts(key)
    return counted


def draw_kernel_map(key, part):
    counted = occupied_counts(key)
    key = jax.random.fold_in(key, 3)
    present_key, near_key = jax.random.split(key, 2)
    device_count = VOXELS // VOX_DEV
    position = jnp.arange(VOXELS, dtype=jnp.int32)
    device_index = (position // VOX_DEV)[:, None]
    column_inside = (position % VOX_DEV)[:, None]
    filled = counted[position // VOX_DEV][:, None]
    occupied = (column_inside < filled - BLOCK) | (column_inside >= VOX_DEV - BLOCK)
    present = jax.random.randint(present_key, (VOXELS, K), 0, 20) < 7
    block_start = column_inside // BLOCK * BLOCK
    candidate = block_start - BLOCK + jax.random.randint(near_key, (VOXELS, K), 0, 3 * BLOCK)
    below = candidate < 0
    above = candidate >= VOX_DEV
    own_ok = (candidate < filled - BLOCK) | (candidate >= VOX_DEV - BLOCK)
    valid = jnp.where(below, device_index > 0, jnp.where(above, device_index < device_count - 1, own_ok))
    linked = jnp.where(present & valid, VOX_DEV + candidate, 3 * VOX_DEV)
    middle = jnp.arange(K)[None, :] == K // 2
    linked = jnp.where(middle, VOX_DEV + column_inside, linked)
    return jnp.where(occupied, linked, 3 * VOX_DEV).astype(jnp.int32)


def draw_features(key, part):
    key = jax.random.fold_in(key, 5)
    device_count = VOXELS // VOX_DEV
    value_key = jax.random.fold_in(key, 0)
    position = jnp.arange(VOXELS)
    ramp_scale = 1.0 + 2.0 * (position // VOX_DEV).astype(jnp.float32) / max(device_count - 1, 1)
    values = jnp.clip(jax.random.normal(value_key, (VOXELS, C)), -4.0, 4.0)
    return (values * ramp_scale[:, None]).astype(jnp.bfloat16)


def block_levels(stream_key, extent, shards, smallest, high):
    level, own = 1.0, jax.random.fold_in(stream_key, 6)
    for axis_at, blocks in shards:
        draws = jnp.exp(jax.random.uniform(jax.random.fold_in(own, axis_at), (blocks,), jnp.float32, smallest / len(shards), high / len(shards)))
        level = level * jnp.repeat(draws, extent[axis_at] // blocks).reshape([-1 if axis == axis_at else 1 for axis in range(len(extent))])
    return level


def noise(key, shape, deviation, most, shards=(), held_as=jnp.bfloat16):
    array = jax.random.normal(key, shape, jnp.float32) * deviation
    if len(shards) > 0:
        array = block_levels(key, shape, shards, -0.22, 0.18) * array
    return jnp.clip(array, min=-most, max=most).astype(held_as)


def setup_inputs(seed: int = 0, part: int = 0) -> dict:
    keys = jax.random.split(jax.random.key(seed), 8)
    part_keys = jax.random.split(jax.random.fold_in(keys[7], part), 8)
    return {
        "features": draw_features(jax.random.fold_in(jax.random.fold_in(keys[7], part), 71), part),
        "kernel_map": draw_kernel_map(jax.random.fold_in(jax.random.fold_in(keys[7], part), 71), part),
        "occupancy": draw_occupancy(jax.random.fold_in(jax.random.fold_in(keys[7], part), 71), part),
        "weights": noise(keys[3], (K, C, C), (C * 4) ** -0.5, 0.1875),
        "bn_gain": jnp.clip(1.0 + 0.1 * jax.random.normal(keys[4], (C,), jnp.float32), 0.5, 1.5),
        "bn_shift": noise(keys[5], (C,), 0.5, 3.0, (), jnp.float32),
        "cotangent": noise(part_keys[6], (VOXELS, C), 1.0, 6.0, ((0, 16),)),
    }


EPSILON = 1e-05

def global_index(kernel_map):
    position = jnp.arange(VOXELS, dtype=jnp.int32)
    device_row = position // VOX_DEV * VOX_DEV
    shifted = device_row[:, None] + kernel_map - VOX_DEV
    return jnp.where(kernel_map >= 3 * VOX_DEV, VOXELS, shifted).astype(jnp.int32)

def active_rows(occupancy):
    position = jnp.arange(VOXELS, dtype=jnp.int32)
    filled = jnp.repeat(occupancy, VOX_DEV)
    inside = position % VOX_DEV
    return (inside < filled - BLOCK) | (inside >= VOX_DEV - BLOCK)

def reference(features, kernel_map, occupancy, weights, bn_gain, bn_shift, cotangent):
    lookup = global_index(kernel_map)
    occupied = active_rows(occupancy)[:, None]
    padded = jnp.concatenate([features, jnp.zeros((1, C), features.dtype)], axis=0)

    def forward_step(summed, inputs):
        column, kernel = inputs
        picked = jnp.take(padded, column, axis=0)
        return (summed + jnp.dot(picked, kernel, preferred_element_type=jnp.float32), None)
    conv, _ = lax.scan(forward_step, jnp.zeros((VOXELS, C), jnp.float32), (lookup.T, weights))
    total = jnp.sum(occupancy).astype(jnp.float32)
    center = lax.optimization_barrier(jnp.sum(jnp.where(occupied, conv, 0.0), axis=0)) / total
    spread = lax.optimization_barrier(jnp.sum(jnp.where(occupied, jnp.square(conv - center), 0.0), axis=0)) / total
    inverse = lax.rsqrt(spread + EPSILON)
    normed = (conv - center) * inverse
    affine = bn_gain * normed + bn_shift
    block_out = jnp.where(occupied, jnp.maximum(affine, 0.0) + features.astype(jnp.float32), 0.0).astype(jnp.bfloat16)
    upstream = jnp.where(occupied & (affine > 0.0), cotangent.astype(jnp.float32), 0.0)
    grad_gain = lax.optimization_barrier(jnp.sum(upstream * normed, axis=0))
    grad_shift = lax.optimization_barrier(jnp.sum(upstream, axis=0))
    grad_conv = jnp.where(occupied, bn_gain * inverse * (upstream - grad_shift / total - normed * grad_gain / total), 0.0).astype(jnp.bfloat16)

    def backward_step(sink, inputs):
        column, kernel = inputs
        picked = jnp.take(padded, column, axis=0)
        slice_grad = lax.dot_general(picked, grad_conv, (((0,), (0,)), ((), ())), preferred_element_type=jnp.float32)
        pushed = lax.dot_general(grad_conv, kernel, (((1,), (1,)), ((), ())), preferred_element_type=jnp.float32).astype(jnp.bfloat16)
        pushed = lax.optimization_barrier(pushed)
        return (sink.at[column].add(pushed.astype(jnp.float32)), slice_grad)
    sink, kernel_grads = lax.scan(backward_step, jnp.zeros((VOXELS + 1, C), jnp.float32), (lookup.T, weights))
    grad_features = (jnp.where(occupied, cotangent.astype(jnp.float32), 0.0) + sink[:VOXELS]).astype(jnp.bfloat16)
    return (block_out, grad_features, kernel_grads.astype(jnp.bfloat16), grad_gain, grad_shift)
```

```python
import functools

import jax
import jax.numpy as jnp
from jax import lax
from jax.experimental import pallas as pl
from jax.experimental.pallas import tpu as pltpu
from jax.sharding import PartitionSpec as P

K = 27
BLOCK = 128
GROUP = 3
K_ONE = 18
EPSILON = 1e-05
F32 = jnp.float32
BF16 = jnp.bfloat16
VMEM_LIMIT = 24 * 1024 * 1024


def dot(a, b, contract):
    return lax.dot_general(a, b, ((contract[0], contract[1]), ((), ())), preferred_element_type=F32)


def full(shape):
    return pl.BlockSpec(shape, lambda *_: (0,) * len(shape))


def params(**more):
    return pltpu.CompilerParams(vmem_limit_bytes=VMEM_LIMIT, **more)


def cost(flops, moved):
    return pl.CostEstimate(flops=int(flops), bytes_accessed=int(moved), transcendentals=0)


def occupied_rows(filled, rows):
    position = lax.broadcasted_iota(jnp.int32, (rows, 1), 0)
    return (position < filled - BLOCK) | (position >= rows - BLOCK)


def select_and_multiply(index_ref, tiles, weight_ref, conv_ref, picked_ref):
    step = pl.program_id(0)
    index = pltpu.roll(index_ref[...], lax.rem(BLOCK - step * GROUP, BLOCK), 1)
    slots = lax.broadcasted_iota(jnp.int32, (BLOCK, 3 * BLOCK), 1)
    for b, stacked in enumerate(tiles):
        rows = slice(b * BLOCK, (b + 1) * BLOCK)
        chosen = jnp.concatenate(
            [
                jnp.where(index[rows, j : j + 1] == slots, 1.0, 0.0).astype(BF16)
                for j in range(GROUP)
            ],
            axis=0,
        )
        picked = dot(chosen, stacked, ((1,), (0,))).astype(BF16)
        for j in range(GROUP):
            picked_ref[j, rows, :] = picked[j * BLOCK : (j + 1) * BLOCK]
    total = jnp.where(step == 0, 0.0, conv_ref[...])
    for j in range(GROUP):
        total = total + dot(picked_ref[j], weight_ref[j], ((1,), (0,)))
    conv_ref[...] = total


def inner_kernel(index_ref, own_ref, weight_ref, conv_ref, picked_ref):
    tiles = [own_ref[0 : 3 * BLOCK, :], own_ref[BLOCK : 4 * BLOCK, :]]
    select_and_multiply(index_ref, tiles, weight_ref, conv_ref, picked_ref)


def outer_kernel(
    filled_ref, index_ref, before_ref, own_ref, after_ref, inner_ref, weight_ref,
    conv_ref, picked_ref, stats_ref,
):
    tiles = [
        jnp.concatenate([before_ref[...], own_ref[0 : 2 * BLOCK, :]], axis=0),
        jnp.concatenate([own_ref[2 * BLOCK : 4 * BLOCK, :], after_ref[...]], axis=0),
    ]
    select_and_multiply(index_ref, tiles, weight_ref, conv_ref, picked_ref)

    @pl.when(pl.program_id(0) == pl.num_programs(0) - 1)
    def _():
        filled = filled_ref[0]
        count = filled.astype(F32)
        conv = jnp.concatenate([conv_ref[0:BLOCK, :], inner_ref[...], conv_ref[BLOCK:, :]], axis=0)
        occupied = occupied_rows(filled, conv.shape[0])
        sums = jnp.sum(jnp.where(occupied, conv, 0.0), axis=0, keepdims=True)
        off = jnp.where(occupied, conv - sums / count, 0.0)
        squares = jnp.sum(off * off, axis=0, keepdims=True)
        line = jnp.concatenate([sums, squares, jnp.full_like(sums, count)], axis=0)
        stats_ref[...] = jnp.broadcast_to(line[None], stats_ref.shape)


def moments(stats):
    sums, squares, counts = stats[:, 0, :], stats[:, 1, :], stats[:, 2, :]
    total = jnp.sum(counts, axis=0, keepdims=True)
    center = jnp.sum(sums, axis=0, keepdims=True) / total
    away = sums / counts - center
    spread = jnp.sum(squares + counts * away * away, axis=0, keepdims=True) / total
    return center, lax.rsqrt(spread + EPSILON), total


def normalised(filled, inner_ref, outer_ref, stats_ref, gain_ref, shift_ref, cotangent_ref):
    conv = jnp.concatenate([outer_ref[0:BLOCK, :], inner_ref[...], outer_ref[BLOCK:, :]], axis=0)
    center, inverse, total = moments(stats_ref[...])
    occupied = occupied_rows(filled, conv.shape[0])
    normed = (conv - center) * inverse
    affine = gain_ref[...] * normed + shift_ref[...]
    upstream = jnp.where(occupied & (affine > 0.0), cotangent_ref[...].astype(F32), 0.0)
    return occupied, normed, affine, upstream, inverse, total


def norm_kernel(
    filled_ref, inner_ref, outer_ref, stats_ref, gain_ref, shift_ref, cotangent_ref, feature_ref,
    out_ref, sums_ref,
):
    occupied, normed, affine, upstream, _, _ = normalised(
        filled_ref[0], inner_ref, outer_ref, stats_ref, gain_ref, shift_ref, cotangent_ref
    )
    out = jnp.maximum(affine, 0.0) + feature_ref[...].astype(F32)
    out_ref[...] = jnp.where(occupied, out, 0.0).astype(BF16)
    line = jnp.concatenate(
        [jnp.sum(upstream * normed, axis=0, keepdims=True), jnp.sum(upstream, axis=0, keepdims=True)],
        axis=0,
    )
    sums_ref[...] = jnp.broadcast_to(line[None], sums_ref.shape)


def kernel_gradient(place, inner_ref, outer_ref, grad_ref, product, keep_ref, send_ref):
    rows = product.shape[0] // 16
    half = keep_ref.shape[0]
    product[...] = dot(
        inner_ref[0], grad_ref[BLOCK : 3 * BLOCK, :], ((0,), (0,))
    ) + dot(
        outer_ref[0],
        jnp.concatenate([grad_ref[0:BLOCK, :], grad_ref[3 * BLOCK :, :]], axis=0),
        ((0,), (0,)),
    )
    for piece in range(16):
        start = pl.multiple_of(lax.bitwise_xor(jnp.int32(piece), place) * rows, rows)
        value = product[pl.ds(start, rows), :]
        if piece < half:
            keep_ref[piece, 0] = value
        else:
            send_ref[piece - half, 0] = value.astype(BF16)


def first_gradient_kernel(
    scalars_ref, inner_ref, outer_ref, stats_ref, grads_ref, gain_ref, shift_ref, cotangent_ref,
    picked_in_ref, picked_out_ref,
    keep_ref, send_ref, grad_ref, grad_gain_ref, grad_shift_ref, product,
):
    @pl.when(pl.program_id(0) == 0)
    def _():
        occupied, normed, _, upstream, inverse, total = normalised(
            scalars_ref[0], inner_ref, outer_ref, stats_ref, gain_ref, shift_ref, cotangent_ref
        )
        grads = grads_ref[...]
        grad_gain = jnp.sum(grads[:, 0, :], axis=0, keepdims=True)
        grad_shift = jnp.sum(grads[:, 1, :], axis=0, keepdims=True)
        grad_gain_ref[...] = grad_gain
        grad_shift_ref[...] = grad_shift
        grad_conv = gain_ref[...] * inverse * (
            upstream - grad_shift / total - normed * grad_gain / total
        )
        grad_ref[...] = jnp.where(occupied, grad_conv, 0.0).astype(BF16)

    kernel_gradient(
        scalars_ref[1], picked_in_ref, picked_out_ref, grad_ref, product, keep_ref, send_ref
    )


def second_gradient_kernel(
    scalars_ref, grad_ref, picked_in_ref, picked_out_ref, keep_ref, send_ref, product
):
    kernel_gradient(
        scalars_ref[1], picked_in_ref, picked_out_ref, grad_ref, product, keep_ref, send_ref
    )


def push_kernel(grad_ref, index_ref, weight_ref, before_ref, own_ref, after_ref, sink):
    step = pl.program_id(0)

    @pl.when(step == 0)
    def _():
        sink[...] = jnp.zeros_like(sink)

    blocks = grad_ref.shape[0] // BLOCK
    slots = lax.broadcasted_iota(jnp.int32, (3 * BLOCK, BLOCK), 0)
    pushed = [
        dot(grad_ref[...], weight_ref[j], ((1,), (1,))).astype(BF16) for j in range(GROUP)
    ]
    for b in range(blocks):
        rows = slice(b * BLOCK, (b + 1) * BLOCK)
        chosen = jnp.concatenate(
            [
                jnp.where(index_ref[step * GROUP + j, :][None, rows] == slots, 1.0, 0.0).astype(BF16)
                for j in range(GROUP)
            ],
            axis=1,
        )
        stacked = jnp.concatenate([pushed[j][rows] for j in range(GROUP)], axis=0)
        window = slice(b * BLOCK, (b + 3) * BLOCK)
        sink[window, :] = sink[window, :] + dot(chosen, stacked, ((1,), (0,)))

    @pl.when(step == pl.num_programs(0) - 1)
    def _():
        before_ref[...] = sink[0:BLOCK, :].astype(BF16)
        own_ref[...] = sink[BLOCK : (blocks + 1) * BLOCK, :]
        after_ref[...] = sink[(blocks + 1) * BLOCK :, :].astype(BF16)


def place_kernel(places_ref, own_one, other_one, own_two, other_two, out_ref, sems):
    rows = own_one.shape[2]
    half = own_one.shape[0]
    split = own_one.shape[1]
    copies = []
    for piece in range(16):
        for part, (own, other) in enumerate(((own_one, other_one), (own_two, other_two))):
            source = own if piece < half else other
            place = lax.bitwise_xor(jnp.int32(piece), places_ref[part])
            start = pl.multiple_of(place * rows, rows)
            first = 0 if part == 0 else split
            copies.append(
                pltpu.make_async_copy(
                    source.at[piece % half],
                    out_ref.at[pl.ds(first, source.shape[1]), pl.ds(start, rows), :],
                    sems.at[len(copies)],
                )
            )
    for copy in copies:
        copy.start()
    for copy in copies:
        copy.wait()


def swap(value, by):
    peers = lax.axis_size("dp")
    return lax.ppermute(value, "dp", [(i, i ^ by) for i in range(peers)])


STAGES = {"c": (1,), "x": (2,), "z": (4, 8, 12)}


def reduce_start(total, stage):
    partners = STAGES[stage]
    size = total.shape[0] // (len(partners) + 1)
    return [
        swap(total[(i + 1) * size : (i + 2) * size].astype(BF16), by)
        for i, by in enumerate(partners)
    ]


def reduce_end(total, received):
    size = received[0].shape[0]
    return functools.reduce(lambda a, b: a + b.astype(F32), received, total[:size])


def gather_start(piece, stage):
    return [swap(piece, by) for by in STAGES[stage]]


def lockstep(pieces, starts, ends):
    received = [start(piece) for piece, start in zip(pieces, starts)]
    received, pieces = lax.optimization_barrier((received, pieces))
    return [end(piece, got) for piece, got, end in zip(pieces, received, ends)]


def summed_over_devices(one, two):
    pieces = [keep + swap(send, 1).astype(F32) for keep, send in (one, two)]
    for stages in ("xz", "zx"):
        starts = [functools.partial(reduce_start, stage=stage) for stage in stages]
        pieces = lockstep(pieces, starts, [reduce_end] * 2)
    by = 16
    while by < lax.axis_size("dp"):
        pieces = [piece + swap(piece, by) for piece in pieces]
        by *= 2
    pieces = [piece.astype(BF16) for piece in pieces]

    def joined(piece, received):
        return jnp.concatenate([piece] + received, axis=0)

    for stages in ("zx", "xz"):
        starts = [functools.partial(gather_start, stage=stage) for stage in stages]
        pieces = lockstep(pieces, starts, [joined] * 2)
    return [(piece, swap(piece, 1)) for piece in pieces]


def per_device(features, kernel_map, occupancy, weights, bn_gain, bn_shift, cotangent):
    rows, channels = features.shape
    peers = lax.axis_size("dp")
    me = lax.axis_index("dp")
    blocks = rows // BLOCK
    inner_rows = rows - 2 * BLOCK
    steps = K // GROUP

    up = [(i, i + 1) for i in range(peers - 1)]
    down = [(i + 1, i) for i in range(peers - 1)]
    before = lax.ppermute(features[rows - BLOCK :], "dp", up)
    after = lax.ppermute(features[:BLOCK], "dp", down)

    block_of = lax.broadcasted_iota(jnp.int32, kernel_map.shape, 0) // BLOCK
    index = kernel_map - (rows - BLOCK) - block_of * BLOCK
    index_wide = jnp.pad(index, ((0, 0), (0, BLOCK - K)), constant_values=-1)
    index_flat = jnp.transpose(index)

    gain = bn_gain.reshape(1, channels)
    shift = bn_shift.reshape(1, channels)
    smem = pl.BlockSpec(memory_space=pltpu.SMEM)
    weight_spec = pl.BlockSpec((GROUP, channels, channels), lambda s: (s, 0, 0))
    picked_spec = pl.BlockSpec((GROUP, 2 * BLOCK, channels), lambda s: (s, 0, 0))
    half_conv = jax.ShapeDtypeStruct((2 * BLOCK, channels), F32)
    half_picked = jax.ShapeDtypeStruct((K, 2 * BLOCK, channels), BF16)
    work = K * 2 * BLOCK * channels * 2 * (3 * BLOCK + channels)
    moved = K * channels * channels * 2 * 2

    inner, picked_in = pl.pallas_call(
        inner_kernel,
        grid=(steps,),
        in_specs=[full((inner_rows, BLOCK)), full((rows, channels)), weight_spec],
        out_specs=[full((inner_rows, channels)), picked_spec],
        out_shape=[half_conv, half_picked],
        compiler_params=params(),
        cost_estimate=cost(work, moved),
        name="conv_inner",
    )(index_wide[BLOCK : rows - BLOCK], features, weights)

    index_outer = jnp.concatenate([index_wide[:BLOCK], index_wide[rows - BLOCK :]], axis=0)
    outer, picked_out, stats = pl.pallas_call(
        outer_kernel,
        grid=(steps,),
        in_specs=[
            smem,
            full((2 * BLOCK, BLOCK)),
            full((BLOCK, channels)),
            full((rows, channels)),
            full((BLOCK, channels)),
            full((inner_rows, channels)),
            weight_spec,
        ],
        out_specs=[full((2 * BLOCK, channels)), picked_spec, full((peers, 3, channels))],
        out_shape=[half_conv, half_picked, jax.ShapeDtypeStruct((peers, 3, channels), F32)],
        compiler_params=params(),
        cost_estimate=cost(work, moved),
        name="conv_outer",
    )(occupancy, index_outer, before, features, after, inner, weights)

    stats = lax.all_to_all(stats, "dp", 0, 0, tiled=True)

    block_out, sums = pl.pallas_call(
        norm_kernel,
        in_specs=[smem] + [pl.BlockSpec(memory_space=pltpu.VMEM)] * 7,
        out_shape=[
            jax.ShapeDtypeStruct((rows, channels), BF16),
            jax.ShapeDtypeStruct((peers, 2, channels), F32),
        ],
        compiler_params=params(),
        cost_estimate=cost(rows * channels * 20, rows * channels * 10),
        name="norm",
    )(occupancy, inner, outer, stats, gain, shift, cotangent, features)

    grads = lax.all_to_all(sums, "dp", 0, 0, tiled=True)

    core, lane, depth = me & 1, (me >> 1) & 1, (me >> 2) & 3
    place_one = core * 8 + lane * 4 + depth
    place_two = core * 8 + depth * 2 + lane
    piece_rows = channels // 16
    picked_one = pl.BlockSpec((1, 2 * BLOCK, channels), lambda s: (s, 0, 0))
    picked_two = pl.BlockSpec((1, 2 * BLOCK, channels), lambda s: (s + K_ONE, 0, 0))
    piece_spec = pl.BlockSpec((8, 1, piece_rows, channels), lambda s: (0, s, 0, 0))

    def pieces(count):
        shape = (8, count, piece_rows, channels)
        return [jax.ShapeDtypeStruct(shape, F32), jax.ShapeDtypeStruct(shape, BF16)]

    product = pltpu.VMEM((channels, channels), F32)
    line = jax.ShapeDtypeStruct((1, channels), F32)
    keep_one, send_one, grad_conv, grad_gain, grad_shift = pl.pallas_call(
        first_gradient_kernel,
        grid=(K_ONE,),
        in_specs=[
            smem,
            full((2 * BLOCK, channels)),
            full((2 * BLOCK, channels)),
            full((peers, 3, channels)),
            full((peers, 2, channels)),
            full((1, channels)),
            full((1, channels)),
            full((rows, channels)),
            picked_one,
            picked_one,
        ],
        out_specs=[
            piece_spec,
            piece_spec,
            full((rows, channels)),
            full((1, channels)),
            full((1, channels)),
        ],
        out_shape=pieces(K_ONE) + [jax.ShapeDtypeStruct((rows, channels), BF16), line, line],
        scratch_shapes=[product],
        compiler_params=params(),
        cost_estimate=cost(K_ONE * rows * channels * channels * 2, K_ONE * channels * channels * 8),
        name="weight_gradient_one",
    )(
        jnp.stack([occupancy[0], place_one]),
        inner, outer, stats, grads, gain, shift, cotangent, picked_in, picked_out,
    )

    keep_two, send_two = pl.pallas_call(
        second_gradient_kernel,
        grid=(K - K_ONE,),
        in_specs=[smem, full((rows, channels)), picked_two, picked_two],
        out_specs=[piece_spec, piece_spec],
        out_shape=pieces(K - K_ONE),
        scratch_shapes=[product],
        compiler_params=params(),
        cost_estimate=cost(
            (K - K_ONE) * rows * channels * channels * 2, (K - K_ONE) * channels * channels * 8
        ),
        name="weight_gradient_two",
    )(jnp.stack([occupancy[0], place_two]), grad_conv, picked_in, picked_out)

    (own_one, other_one), (own_two, other_two) = summed_over_devices(
        (keep_one, send_one), (keep_two, send_two)
    )
    anywhere = pl.BlockSpec(memory_space=pl.ANY)
    grad_weights = pl.pallas_call(
        place_kernel,
        in_specs=[smem] + [anywhere] * 4,
        out_specs=anywhere,
        out_shape=jax.ShapeDtypeStruct(weights.shape, BF16),
        scratch_shapes=[pltpu.SemaphoreType.DMA((32,))],
        compiler_params=params(),
        cost_estimate=cost(0, K * channels * channels * 4),
        name="place",
    )(jnp.stack([place_one, place_two]), own_one, other_one, own_two, other_two)

    sink_before, sink_own, sink_after = pl.pallas_call(
        push_kernel,
        grid=(steps,),
        in_specs=[full((rows, channels)), full((K, rows)), weight_spec],
        out_specs=[full((BLOCK, channels)), full((rows, channels)), full((BLOCK, channels))],
        out_shape=[
            jax.ShapeDtypeStruct((BLOCK, channels), BF16),
            jax.ShapeDtypeStruct((rows, channels), F32),
            jax.ShapeDtypeStruct((BLOCK, channels), BF16),
        ],
        scratch_shapes=[pltpu.VMEM((rows + 2 * BLOCK, channels), F32)],
        compiler_params=params(),
        cost_estimate=cost(2 * work, moved),
        name="push",
    )(grad_conv, index_flat, weights)
    from_next = lax.ppermute(sink_before, "dp", down).astype(F32)
    from_prev = lax.ppermute(sink_after, "dp", up).astype(F32)
    occupied = occupied_rows(occupancy[0], rows)
    received = jnp.concatenate(
        [
            sink_own[:BLOCK] + from_prev,
            sink_own[BLOCK : rows - BLOCK],
            sink_own[rows - BLOCK :] + from_next,
        ],
        axis=0,
    )
    grad_features = (jnp.where(occupied, cotangent.astype(F32), 0.0) + received).astype(BF16)
    return (
        block_out,
        grad_features,
        grad_weights,
        grad_gain.reshape(channels),
        grad_shift.reshape(channels),
    )


def solution(mesh):
    in_specs = (
        P(("parts", "dp"), None),
        P(("parts", "dp"), None),
        P(("parts", "dp")),
        P(),
        P(),
        P(),
        P(("parts", "dp"), None),
    )
    out_specs = (
        P(("parts", "dp"), None),
        P(("parts", "dp"), None),
        P("parts", None, None),
        P("parts"),
        P("parts"),
    )
    return jax.shard_map(
        per_device, mesh=mesh, in_specs=in_specs, out_specs=out_specs, check_vma=False
    )
```

```python
import functools

import jax
import jax.numpy as jnp
from jax import lax
from jax.experimental import pallas as pl
from jax.experimental.pallas import tpu as pltpu
from jax.sharding import PartitionSpec as P

K = 27
BLOCK = 128
GROUP = 9
K_ONE = 18
EPSILON = 1e-05
F32 = jnp.float32
BF16 = jnp.bfloat16
LARGE = 58 * 1024 * 1024
SMALL = 12 * 1024 * 1024


def dot(a, b, contract):
    return lax.dot_general(a, b, ((contract[0], contract[1]), ((), ())), preferred_element_type=F32)


def full(shape):
    return pl.BlockSpec(shape, lambda *_: (0,) * len(shape))


def params(limit):
    return pltpu.CompilerParams(vmem_limit_bytes=limit)


def cost(flops, moved):
    return pl.CostEstimate(flops=int(flops), bytes_accessed=int(moved), transcendentals=0)


def occupied_rows(filled, rows):
    position = lax.broadcasted_iota(jnp.int32, (rows, 1), 0)
    return (position < filled - BLOCK) | (position >= rows - BLOCK)


def convolve(blocks, map_ref, tiles, weight_hbm, conv_ref, picked_hbm, rows_of, scratch):
    weight, picked, index, weight_sem, picked_sem = scratch
    groups = K // GROUP

    def fetch(g):
        here = pl.ds(g * GROUP, GROUP)
        return pltpu.make_async_copy(weight_hbm.at[here], weight.at[here], weight_sem.at[g])

    def keep(g, b):
        here = pl.ds(g * GROUP, GROUP)
        return pltpu.make_async_copy(
            picked.at[here, pl.ds(b * BLOCK, BLOCK)],
            picked_hbm.at[here, pl.ds(rows_of[b], BLOCK)],
            picked_sem.at[g, b],
        )

    for g in range(groups):
        fetch(g).start()
    spare = jnp.zeros((BLOCK - K, blocks * BLOCK), jnp.int32)
    index[...] = jnp.transpose(jnp.concatenate([map_ref[...], spare], axis=0))
    conv_ref[...] = jnp.zeros_like(conv_ref)
    slots = lax.broadcasted_iota(jnp.int32, (BLOCK, 3 * BLOCK), 1)

    def group(g, carry):
        local = pltpu.roll(index[...], lax.rem(BLOCK - g * GROUP, BLOCK), 1)
        fetch(g).wait()
        for b in range(blocks):
            rows = slice(b * BLOCK, (b + 1) * BLOCK)
            here = local[rows] - (2 * BLOCK + rows_of[b] + BLOCK)
            for j in range(GROUP):
                chosen = jnp.where(here[:, j : j + 1] == slots, 1.0, 0.0).astype(BF16)
                picked[g * GROUP + j, rows, :] = dot(chosen, tiles[b][...], ((1,), (0,))).astype(BF16)
            keep(g, b).start()
        total = conv_ref[...]
        for j in range(GROUP):
            k = g * GROUP + j
            total = total + dot(picked[k], weight[k], ((1,), (0,)))
        conv_ref[...] = total
        return carry

    lax.fori_loop(0, groups, group, 0)

    def finish():
        for g in range(groups):
            for b in range(blocks):
                keep(g, b).wait()

    return finish


def inner_kernel(map_ref, own_ref, weight_hbm, conv_ref, picked_hbm, *scratch):
    tiles = [own_ref.at[0 : 3 * BLOCK], own_ref.at[BLOCK : 4 * BLOCK]]
    finish = convolve(
        2, map_ref, tiles, weight_hbm, conv_ref, picked_hbm, (BLOCK, 2 * BLOCK), scratch
    )
    finish()


def outer_kernel(
    filled_ref, map_ref, before_ref, own_ref, after_ref, inner_ref, weight_hbm, _,
    conv_ref, stats_ref, picked_hbm, first, last, *scratch,
):
    first[0:BLOCK, :] = before_ref[...]
    first[BLOCK:, :] = own_ref[0 : 2 * BLOCK, :]
    last[0 : 2 * BLOCK, :] = own_ref[2 * BLOCK :, :]
    last[2 * BLOCK :, :] = after_ref[...]
    finish = convolve(
        2, map_ref, [first, last], weight_hbm, conv_ref, picked_hbm, (0, 3 * BLOCK), scratch
    )
    filled = filled_ref[0]
    count = filled.astype(F32)
    conv = jnp.concatenate([conv_ref[0:BLOCK, :], inner_ref[...], conv_ref[BLOCK:, :]], axis=0)
    occupied = occupied_rows(filled, conv.shape[0])
    sums = jnp.sum(jnp.where(occupied, conv, 0.0), axis=0, keepdims=True)
    off = jnp.where(occupied, conv - sums / count, 0.0)
    squares = jnp.sum(off * off, axis=0, keepdims=True)
    stats_ref[...] = jnp.concatenate([sums, squares, jnp.full_like(sums, count)], axis=0)
    finish()


def normalised(filled, inner_ref, outer_ref, stats_ref, gain_ref, shift_ref, cotangent_ref):
    conv = jnp.concatenate([outer_ref[0:BLOCK, :], inner_ref[...], outer_ref[BLOCK:, :]], axis=0)
    total = stats_ref[2:3, :]
    center = stats_ref[0:1, :] / total
    inverse = lax.rsqrt(stats_ref[1:2, :] / total + EPSILON)
    occupied = occupied_rows(filled, conv.shape[0])
    normed = (conv - center) * inverse
    affine = gain_ref[...] * normed + shift_ref[...]
    upstream = jnp.where(occupied & (affine > 0.0), cotangent_ref[...].astype(F32), 0.0)
    return occupied, normed, affine, upstream, inverse, total


def norm_kernel(
    filled_ref, inner_ref, outer_ref, stats_ref, gain_ref, shift_ref, cotangent_ref, feature_ref,
    out_ref, sums_ref,
):
    occupied, normed, affine, upstream, _, _ = normalised(
        filled_ref[0], inner_ref, outer_ref, stats_ref, gain_ref, shift_ref, cotangent_ref
    )
    out = jnp.maximum(affine, 0.0) + feature_ref[...].astype(F32)
    out_ref[...] = jnp.where(occupied, out, 0.0).astype(BF16)
    sums_ref[...] = jnp.concatenate(
        [jnp.sum(upstream * normed, axis=0, keepdims=True), jnp.sum(upstream, axis=0, keepdims=True)],
        axis=0,
    )


def kernel_gradient(place, picked_ref, grad_ref, product, keep_ref, send_ref):
    rows = product.shape[1] // 16
    half = keep_ref.shape[0]
    for j in range(GROUP):
        product[j] = dot(picked_ref[j], grad_ref[...], ((0,), (0,)))
        for piece in range(16):
            start = pl.multiple_of(lax.bitwise_xor(jnp.int32(piece), place) * rows, rows)
            value = product[j, pl.ds(start, rows), :]
            if piece < half:
                keep_ref[piece, j] = value
            else:
                send_ref[piece - half, j] = value.astype(BF16)


def first_gradient_kernel(
    filled_ref, place_ref, inner_ref, outer_ref, stats_ref, grads_ref, gain_ref, shift_ref,
    cotangent_ref, picked_ref, keep_ref, send_ref, grad_ref, product,
):
    @pl.when(pl.program_id(0) == 0)
    def _():
        occupied, normed, _, upstream, inverse, total = normalised(
            filled_ref[0], inner_ref, outer_ref, stats_ref, gain_ref, shift_ref, cotangent_ref
        )
        grad_conv = gain_ref[...] * inverse * (
            upstream - grads_ref[1:2, :] / total - normed * grads_ref[0:1, :] / total
        )
        grad_ref[...] = jnp.where(occupied, grad_conv, 0.0).astype(BF16)

    kernel_gradient(place_ref[0], picked_ref, grad_ref, product, keep_ref, send_ref)


def second_gradient_kernel(place_ref, grad_ref, picked_ref, keep_ref, send_ref, product):
    kernel_gradient(place_ref[0], picked_ref, grad_ref, product, keep_ref, send_ref)


def push_kernel(grad_ref, index_ref, weight_ref, before_ref, own_ref, after_ref, sink):
    step = pl.program_id(0)

    @pl.when(step == 0)
    def _():
        sink[...] = jnp.zeros_like(sink)

    blocks = grad_ref.shape[0] // BLOCK
    here = jnp.concatenate([index_ref[step * GROUP + j, :][None] for j in range(GROUP)], axis=0)
    block_of = lax.broadcasted_iota(jnp.int32, here.shape, 1) // BLOCK
    local = here - (3 + block_of) * BLOCK
    slots = lax.broadcasted_iota(jnp.int32, (3 * BLOCK, BLOCK), 0)
    pushed = [
        dot(grad_ref[...], weight_ref[j], ((1,), (1,))).astype(BF16) for j in range(GROUP)
    ]
    for b in range(blocks):
        rows = slice(b * BLOCK, (b + 1) * BLOCK)
        chosen = jnp.concatenate(
            [
                jnp.where(local[j : j + 1, rows] == slots, 1.0, 0.0).astype(BF16)
                for j in range(GROUP)
            ],
            axis=1,
        )
        stacked = jnp.concatenate([pushed[j][rows] for j in range(GROUP)], axis=0)
        window = slice(b * BLOCK, (b + 3) * BLOCK)
        sink[window, :] = sink[window, :] + dot(chosen, stacked, ((1,), (0,)))

    @pl.when(step == pl.num_programs(0) - 1)
    def _():
        before_ref[...] = sink[0:BLOCK, :].astype(BF16)
        own_ref[...] = sink[BLOCK : (blocks + 1) * BLOCK, :]
        after_ref[...] = sink[(blocks + 1) * BLOCK :, :].astype(BF16)


def place_kernel(places_ref, own_one, other_one, own_two, other_two, out_ref, sems):
    rows = own_one.shape[2]
    half = own_one.shape[0]
    split = own_one.shape[1]
    copies = []
    for piece in range(16):
        for part, (own, other) in enumerate(((own_one, other_one), (own_two, other_two))):
            source = own if piece < half else other
            place = lax.bitwise_xor(jnp.int32(piece), places_ref[part])
            start = pl.multiple_of(place * rows, rows)
            first = 0 if part == 0 else split
            copies.append(
                pltpu.make_async_copy(
                    source.at[piece % half],
                    out_ref.at[pl.ds(first, source.shape[1]), pl.ds(start, rows), :],
                    sems.at[len(copies)],
                )
            )
    for copy in copies:
        copy.start()
    for copy in copies:
        copy.wait()


def swap(value, by):
    peers = lax.axis_size("dp")
    return lax.ppermute(value, "dp", [(i, i ^ by) for i in range(peers)])


STAGES = {"c": (1,), "x": (2,), "z": (4, 8, 12)}


def reduce_start(total, stage):
    partners = STAGES[stage]
    size = total.shape[0] // (len(partners) + 1)
    return [
        swap(total[(i + 1) * size : (i + 2) * size].astype(BF16), by)
        for i, by in enumerate(partners)
    ]


def reduce_end(total, received):
    size = received[0].shape[0]
    return functools.reduce(lambda a, b: a + b.astype(F32), received, total[:size])


def gather_start(piece, stage):
    return [swap(piece, by) for by in STAGES[stage]]


def summed_over_devices(one, two, grad_conv, push):
    pieces = [keep + swap(send, 1).astype(F32) for keep, send in (one, two)]
    pieces, grad_conv = lax.optimization_barrier((pieces, grad_conv))
    beside = push(grad_conv)
    for stages in ("xz", "zx"):
        received = [reduce_start(piece, stage) for piece, stage in zip(pieces, stages)]
        received, pieces, beside = lax.optimization_barrier((received, pieces, beside))
        pieces = [reduce_end(piece, got) for piece, got in zip(pieces, received)]
    by = 16
    while by < lax.axis_size("dp"):
        pieces = [piece + swap(piece, by) for piece in pieces]
        by *= 2
    pieces = [piece.astype(BF16) for piece in pieces]
    for stages in ("zx", "xz"):
        received = [gather_start(piece, stage) for piece, stage in zip(pieces, stages)]
        received, pieces = lax.optimization_barrier((received, pieces))
        pieces = [
            jnp.concatenate([piece] + got, axis=0) for piece, got in zip(pieces, received)
        ]
    return [(piece, swap(piece, 1)) for piece in pieces], beside


def exchanged(value, merge):
    for partners in ((1, 2, 3), (4, 8, 12)):
        received = [swap(value, by) for by in partners]
        received, value = lax.optimization_barrier((received, value))
        value = merge(merge(value, received[0]), merge(received[1], received[2]))
    by = 16
    while by < lax.axis_size("dp"):
        value = merge(value, swap(value, by))
        by *= 2
    return value


def merged_moments(one, two):
    (sum_one, square_one, count_one), (sum_two, square_two, count_two) = one, two
    away = sum_one / count_one - sum_two / count_two
    count = count_one + count_two
    square = (square_one + square_two) + away * away * (count_one * count_two / count)
    return jnp.stack([sum_one + sum_two, square, count])


def per_device(features, kernel_map, occupancy, weights, bn_gain, bn_shift, cotangent):
    rows, channels = features.shape
    peers = lax.axis_size("dp")
    me = lax.axis_index("dp")
    blocks = rows // BLOCK
    inner_rows = rows - 2 * BLOCK
    steps = K // GROUP

    up = [(i, i + 1) for i in range(peers - 1)]
    down = [(i + 1, i) for i in range(peers - 1)]
    before = lax.ppermute(features[rows - BLOCK :], "dp", up)
    after = lax.ppermute(features[:BLOCK], "dp", down)

    map_rows = jnp.transpose(kernel_map)
    map_outer = jnp.concatenate([map_rows[:, :BLOCK], map_rows[:, rows - BLOCK :]], axis=1)

    gain = bn_gain.reshape(1, channels)
    shift = bn_shift.reshape(1, channels)
    smem = pl.BlockSpec(memory_space=pltpu.SMEM)
    vmem = pl.BlockSpec(memory_space=pltpu.VMEM)
    hbm = pl.BlockSpec(memory_space=pltpu.HBM)
    groups = K // GROUP
    half_conv = jax.ShapeDtypeStruct((2 * BLOCK, channels), F32)
    all_picked = jax.ShapeDtypeStruct((K, rows, channels), BF16)
    work = K * 2 * BLOCK * channels * 2 * (3 * BLOCK + channels)
    moved = K * channels * channels * 2 * 2
    scratch = [
        pltpu.VMEM((K, channels, channels), BF16),
        pltpu.VMEM((K, 2 * BLOCK, channels), BF16),
        pltpu.VMEM((2 * BLOCK, BLOCK), jnp.int32),
        pltpu.SemaphoreType.DMA((groups,)),
        pltpu.SemaphoreType.DMA((groups, 2)),
    ]

    inner, picked = pl.pallas_call(
        inner_kernel,
        in_specs=[vmem, vmem, hbm],
        out_specs=[vmem, hbm],
        out_shape=[half_conv, all_picked],
        scratch_shapes=scratch,
        compiler_params=params(LARGE),
        cost_estimate=cost(work, moved),
        name="conv_inner",
    )(map_rows[:, BLOCK : rows - BLOCK], features, weights)

    outer, stats, picked = pl.pallas_call(
        outer_kernel,
        in_specs=[smem, vmem, vmem, vmem, vmem, vmem, hbm, hbm],
        out_specs=[vmem, vmem, hbm],
        out_shape=[half_conv, jax.ShapeDtypeStruct((3, channels), F32), all_picked],
        scratch_shapes=[pltpu.VMEM((3 * BLOCK, channels), BF16)] * 2 + scratch,
        input_output_aliases={7: 2},
        compiler_params=params(LARGE),
        cost_estimate=cost(work, moved),
        name="conv_outer",
    )(occupancy, map_outer, before, features, after, inner, weights, picked)

    stats = exchanged(stats, merged_moments)

    block_out, sums = pl.pallas_call(
        norm_kernel,
        in_specs=[smem] + [vmem] * 7,
        out_shape=[
            jax.ShapeDtypeStruct((rows, channels), BF16),
            jax.ShapeDtypeStruct((2, channels), F32),
        ],
        compiler_params=params(LARGE),
        cost_estimate=cost(rows * channels * 20, rows * channels * 10),
        name="norm",
    )(occupancy, inner, outer, stats, gain, shift, cotangent, features)

    grads = exchanged(sums, jnp.add)

    core, lane, depth = me & 1, (me >> 1) & 1, (me >> 2) & 3
    place_one = (core * 8 + lane * 4 + depth).reshape(1)
    place_two = (core * 8 + depth * 2 + lane).reshape(1)
    piece_rows = channels // 16
    piece_spec = pl.BlockSpec((8, GROUP, piece_rows, channels), lambda s: (0, s, 0, 0))

    def picked_spec(first):
        return pl.BlockSpec((GROUP, rows, channels), lambda s: (s + first // GROUP, 0, 0))

    def pieces(count):
        shape = (8, count, piece_rows, channels)
        return [jax.ShapeDtypeStruct(shape, F32), jax.ShapeDtypeStruct(shape, BF16)]

    product = pltpu.VMEM((GROUP, channels, channels), F32)
    keep_one, send_one, grad_conv = pl.pallas_call(
        first_gradient_kernel,
        grid=(K_ONE // GROUP,),
        in_specs=[
            smem,
            smem,
            full((2 * BLOCK, channels)),
            full((2 * BLOCK, channels)),
            full((3, channels)),
            full((2, channels)),
            full((1, channels)),
            full((1, channels)),
            full((rows, channels)),
            picked_spec(0),
        ],
        out_specs=[piece_spec, piece_spec, full((rows, channels))],
        out_shape=pieces(K_ONE) + [jax.ShapeDtypeStruct((rows, channels), BF16)],
        scratch_shapes=[product],
        compiler_params=params(LARGE),
        cost_estimate=cost(K_ONE * rows * channels * channels * 2, K_ONE * channels * channels * 8),
        name="weight_gradient_one",
    )(occupancy, place_one, inner, outer, stats, grads, gain, shift, cotangent, picked)

    keep_two, send_two = pl.pallas_call(
        second_gradient_kernel,
        grid=((K - K_ONE) // GROUP,),
        in_specs=[smem, full((rows, channels)), picked_spec(K_ONE)],
        out_specs=[piece_spec, piece_spec],
        out_shape=pieces(K - K_ONE),
        scratch_shapes=[product],
        compiler_params=params(LARGE),
        cost_estimate=cost(
            (K - K_ONE) * rows * channels * channels * 2, (K - K_ONE) * channels * channels * 8
        ),
        name="weight_gradient_two",
    )(place_two, grad_conv, picked)

    weight_spec = pl.BlockSpec((GROUP, channels, channels), lambda s: (s, 0, 0))

    def push(grad_conv):
        sink_before, sink_own, sink_after = pl.pallas_call(
            push_kernel,
            grid=(groups,),
            in_specs=[full((rows, channels)), full((K, rows)), weight_spec],
            out_specs=[full((BLOCK, channels)), full((rows, channels)), full((BLOCK, channels))],
            out_shape=[
                jax.ShapeDtypeStruct((BLOCK, channels), BF16),
                jax.ShapeDtypeStruct((rows, channels), F32),
                jax.ShapeDtypeStruct((BLOCK, channels), BF16),
            ],
            scratch_shapes=[pltpu.VMEM((rows + 2 * BLOCK, channels), F32)],
            compiler_params=params(SMALL),
            cost_estimate=cost(2 * work, moved),
            name="push",
        )(grad_conv, map_rows, weights)
        return sink_before, sink_own, sink_after

    ((own_one, other_one), (own_two, other_two)), (sink_before, sink_own, sink_after) = (
        summed_over_devices((keep_one, send_one), (keep_two, send_two), grad_conv, push)
    )
    anywhere = pl.BlockSpec(memory_space=pl.ANY)
    grad_weights = pl.pallas_call(
        place_kernel,
        in_specs=[smem] + [anywhere] * 4,
        out_specs=anywhere,
        out_shape=jax.ShapeDtypeStruct(weights.shape, BF16),
        scratch_shapes=[pltpu.SemaphoreType.DMA((32,))],
        compiler_params=params(SMALL),
        cost_estimate=cost(0, K * channels * channels * 4),
        name="place",
    )(jnp.concatenate([place_one, place_two]), own_one, other_one, own_two, other_two)

    from_next = lax.ppermute(sink_before, "dp", down).astype(F32)
    from_prev = lax.ppermute(sink_after, "dp", up).astype(F32)
    occupied = occupied_rows(occupancy[0], rows)
    received = jnp.concatenate(
        [
            sink_own[:BLOCK] + from_prev,
            sink_own[BLOCK : rows - BLOCK],
            sink_own[rows - BLOCK :] + from_next,
        ],
        axis=0,
    )
    grad_features = (jnp.where(occupied, cotangent.astype(F32), 0.0) + received).astype(BF16)
    return (
        block_out,
        grad_features,
        grad_weights,
        grads[0],
        grads[1],
    )


def solution(mesh):
    in_specs = (
        P(("parts", "dp"), None),
        P(("parts", "dp"), None),
        P(("parts", "dp")),
        P(),
        P(),
        P(),
        P(("parts", "dp"), None),
    )
    out_specs = (
        P(("parts", "dp"), None),
        P(("parts", "dp"), None),
        P("parts", None, None),
        P("parts"),
        P("parts"),
    )
    return jax.shard_map(
        per_device, mesh=mesh, in_specs=in_specs, out_specs=out_specs, check_vma=False
    )
```

```python
import functools

import jax
import jax.numpy as jnp
from jax import lax
from jax.experimental import pallas as pl
from jax.experimental.pallas import tpu as pltpu
from jax.sharding import PartitionSpec as P

K = 27
BLOCK = 128
GROUP = 9
PART = 3
EPSILON = 1e-05
F32 = jnp.float32
BF16 = jnp.bfloat16
LIMIT = 24 * 1024 * 1024


def dot(a, b, contract):
    return lax.dot_general(a, b, ((contract[0], contract[1]), ((), ())), preferred_element_type=F32)


def full(shape):
    return pl.BlockSpec(shape, lambda *_: (0,) * len(shape))


def params(limit):
    return pltpu.CompilerParams(vmem_limit_bytes=limit)


def cost(flops, moved):
    return pl.CostEstimate(flops=int(flops), bytes_accessed=int(moved), transcendentals=0)


def occupied_rows(filled, rows):
    position = lax.broadcasted_iota(jnp.int32, (rows, 1), 0)
    return (position < filled - BLOCK) | (position >= rows - BLOCK)


def convolve(map_ref, tiles, weight_hbm, conv_ref, picked_any, scratch):
    weight, picked, index, weight_sem, picked_sem = scratch
    groups = K // GROUP
    rows = conv_ref.shape[0]

    def fetch(g):
        here = pl.ds(g * GROUP, GROUP)
        return pltpu.make_async_copy(weight_hbm.at[here], weight.at[here], weight_sem.at[g])

    def keep(g):
        here = pl.ds(g * GROUP, GROUP)
        return pltpu.make_async_copy(picked.at[here], picked_any.at[here], picked_sem.at[g])

    for g in range(groups):
        fetch(g).start()
    spare = jnp.zeros((BLOCK - K, rows), jnp.int32)
    index[...] = jnp.transpose(jnp.concatenate([map_ref[...], spare], axis=0))
    conv_ref[...] = jnp.zeros_like(conv_ref)
    slots = lax.broadcasted_iota(jnp.int32, (BLOCK, 3 * BLOCK), 1)

    def group(g, carry):
        local = pltpu.roll(index[...], lax.rem(BLOCK - g * GROUP, BLOCK), 1)
        fetch(g).wait()
        for b, tile in enumerate(tiles):
            here = slice(b * BLOCK, (b + 1) * BLOCK)
            slot = local[here] - (rows - BLOCK + b * BLOCK)
            for j in range(GROUP):
                chosen = jnp.where(slot[:, j : j + 1] == slots, 1.0, 0.0).astype(BF16)
                picked[g * GROUP + j, here, :] = dot(chosen, tile[...], ((1,), (0,))).astype(BF16)
        keep(g).start()
        total = conv_ref[...]
        for j in range(GROUP):
            k = g * GROUP + j
            total = total + dot(picked[k], weight[k], ((1,), (0,)))
        conv_ref[...] = total
        return carry

    lax.fori_loop(0, groups, group, 0)

    def finish():
        for g in range(groups):
            keep(g).wait()

    return finish


def conv_kernel(
    filled_ref, odd_ref, map_ref, own_ref, even_ref, other_ref, weight_hbm,
    conv_ref, stats_ref, picked_any, first, last, *scratch,
):
    rows = own_ref.shape[0]
    odd = odd_ref[0] == 1
    first[0:BLOCK, :] = jnp.where(odd, even_ref[...], other_ref[...])
    first[BLOCK:, :] = own_ref[0 : 2 * BLOCK, :]
    last[0 : 2 * BLOCK, :] = own_ref[rows - 2 * BLOCK :, :]
    last[2 * BLOCK :, :] = jnp.where(odd, other_ref[...], even_ref[...])
    middle = [
        own_ref.at[b * BLOCK : (b + 3) * BLOCK] for b in range(rows // BLOCK - 2)
    ]
    tiles = [first] + middle + [last]
    finish = convolve(map_ref, tiles, weight_hbm, conv_ref, picked_any, scratch)
    filled = filled_ref[0]
    count = filled.astype(F32)
    conv = conv_ref[...]
    occupied = occupied_rows(filled, rows)
    sums = jnp.sum(jnp.where(occupied, conv, 0.0), axis=0, keepdims=True)
    off = jnp.where(occupied, conv - sums / count, 0.0)
    squares = jnp.sum(off * off, axis=0, keepdims=True)
    stats_ref[...] = jnp.concatenate([sums, squares, jnp.full_like(sums, count)], axis=0)
    finish()


def normalised(filled, conv_ref, stats_ref, gain_ref, shift_ref, cotangent_ref):
    conv = conv_ref[...]
    total = stats_ref[2:3, :]
    center = stats_ref[0:1, :] / total
    inverse = lax.rsqrt(stats_ref[1:2, :] / total + EPSILON)
    occupied = occupied_rows(filled, conv.shape[0])
    normed = (conv - center) * inverse
    affine = gain_ref[...] * normed + shift_ref[...]
    upstream = jnp.where(occupied & (affine > 0.0), cotangent_ref[...].astype(F32), 0.0)
    return occupied, normed, affine, upstream, inverse, total


def norm_kernel(
    filled_ref, conv_ref, stats_ref, gain_ref, shift_ref, cotangent_ref, feature_ref,
    out_ref, sums_ref,
):
    occupied, normed, affine, upstream, _, _ = normalised(
        filled_ref[0], conv_ref, stats_ref, gain_ref, shift_ref, cotangent_ref
    )
    out = jnp.maximum(affine, 0.0) + feature_ref[...].astype(F32)
    out_ref[...] = jnp.where(occupied, out, 0.0).astype(BF16)
    sums_ref[...] = jnp.concatenate(
        [jnp.sum(upstream * normed, axis=0, keepdims=True), jnp.sum(upstream, axis=0, keepdims=True)],
        axis=0,
    )


def kernel_gradient(first, place, picked_any, grad, keep_any, send_any, scratch):
    picked, product, keep, send, in_sem, out_sem = scratch
    rows = product.shape[1] // 16
    half = keep.shape[0]

    def fetch(j):
        return pltpu.make_async_copy(picked_any.at[first + j], picked.at[j], in_sem.at[j])

    def store(t):
        here = pl.ds(t * PART, PART)
        return [
            pltpu.make_async_copy(keep.at[:, here], keep_any.at[:, here], out_sem.at[0, t]),
            pltpu.make_async_copy(send.at[:, here], send_any.at[:, here], out_sem.at[1, t]),
        ]

    for j in range(GROUP):
        fetch(j).start()
    grad = grad()
    for j in range(GROUP):
        fetch(j).wait()
        product[j] = dot(picked[j], grad, ((0,), (0,)))
        for piece in range(16):
            start = pl.multiple_of(lax.bitwise_xor(jnp.int32(piece), place) * rows, rows)
            value = product[j, pl.ds(start, rows), :]
            if piece < half:
                keep[piece, j] = value
            else:
                send[piece - half, j] = value.astype(BF16)
        if j % PART == PART - 1:
            for copy in store(j // PART):
                copy.start()
    for t in range(GROUP // PART):
        for copy in store(t):
            copy.wait()


def first_gradient_kernel(
    filled_ref, place_ref, conv_ref, stats_ref, grads_ref, gain_ref, shift_ref, cotangent_ref,
    picked_any, grad_ref, keep_any, send_any, *scratch,
):
    def grad():
        occupied, normed, _, upstream, inverse, total = normalised(
            filled_ref[0], conv_ref, stats_ref, gain_ref, shift_ref, cotangent_ref
        )
        grad_conv = gain_ref[...] * inverse * (
            upstream - grads_ref[1:2, :] / total - normed * grads_ref[0:1, :] / total
        )
        value = jnp.where(occupied, grad_conv, 0.0).astype(BF16)
        grad_ref[...] = value
        return value

    kernel_gradient(0, place_ref[0], picked_any, grad, keep_any, send_any, scratch)


def later_gradient_kernel(
    first, place_ref, grad_ref, picked_any, keep_any, send_any, *scratch
):
    def grad():
        return grad_ref[...]

    kernel_gradient(first, place_ref[0], picked_any, grad, keep_any, send_any, scratch)


def push_kernel(grad_ref, index_ref, weight_ref, before_ref, own_ref, after_ref, sink):
    step = pl.program_id(0)

    @pl.when(step == 0)
    def _():
        sink[...] = jnp.zeros_like(sink)

    blocks = grad_ref.shape[0] // BLOCK
    here = jnp.concatenate([index_ref[step * GROUP + j, :][None] for j in range(GROUP)], axis=0)
    block_of = lax.broadcasted_iota(jnp.int32, here.shape, 1) // BLOCK
    local = here - (3 + block_of) * BLOCK
    slots = lax.broadcasted_iota(jnp.int32, (3 * BLOCK, BLOCK), 0)
    pushed = [
        dot(grad_ref[...], weight_ref[j], ((1,), (1,))).astype(BF16) for j in range(GROUP)
    ]
    for b in range(blocks):
        rows = slice(b * BLOCK, (b + 1) * BLOCK)
        chosen = jnp.concatenate(
            [
                jnp.where(local[j : j + 1, rows] == slots, 1.0, 0.0).astype(BF16)
                for j in range(GROUP)
            ],
            axis=1,
        )
        stacked = jnp.concatenate([pushed[j][rows] for j in range(GROUP)], axis=0)
        window = slice(b * BLOCK, (b + 3) * BLOCK)
        sink[window, :] = sink[window, :] + dot(chosen, stacked, ((1,), (0,)))

    @pl.when(step == pl.num_programs(0) - 1)
    def _():
        before_ref[...] = sink[0:BLOCK, :].astype(BF16)
        own_ref[...] = sink[BLOCK : (blocks + 1) * BLOCK, :]
        after_ref[...] = sink[(blocks + 1) * BLOCK :, :].astype(BF16)


def place_kernel(other, places_ref, one, two, *refs):
    out_ref, sems = refs[-2:]
    half, split, rows = two.shape[:3]
    copies = []
    for piece in range(half):
        for part, source in enumerate((one, two)):
            relative = jnp.int32(piece + half * other)
            place = lax.bitwise_xor(relative, places_ref[part])
            start = pl.multiple_of(place * rows, rows)
            first = split if part == 0 else 0
            copies.append(
                pltpu.make_async_copy(
                    source.at[piece],
                    out_ref.at[pl.ds(first, source.shape[1]), pl.ds(start, rows), :],
                    sems.at[len(copies)],
                )
            )
    for copy in copies:
        copy.start()
    for copy in copies:
        copy.wait()


def swap(value, by):
    peers = lax.axis_size("dp")
    return lax.ppermute(value, "dp", [(i, i ^ by) for i in range(peers)])


STAGES = {"c": (1,), "x": (2,), "z": (4, 8, 12)}


def reduce_start(total, stage):
    partners = STAGES[stage]
    size = total.shape[0] // (len(partners) + 1)
    return [
        swap(total[(i + 1) * size : (i + 2) * size].astype(BF16), by)
        for i, by in enumerate(partners)
    ]


def reduce_end(total, received):
    size = received[0].shape[0]
    return functools.reduce(lambda a, b: a + b.astype(F32), received, total[:size])


def gather_start(piece, stage):
    return [swap(piece, by) for by in STAGES[stage]]


def core_reduced(keep, send):
    return keep + swap(send, 1).astype(F32)


def summed_over_devices(one, two, beside, then):
    pieces = [one, two]
    for stages, work in (("xz", beside), ("zx", then)):
        received = [reduce_start(piece, stage) for piece, stage in zip(pieces, stages)]
        received, pieces, result = lax.optimization_barrier((received, pieces, work()))
        pieces = [reduce_end(piece, got) for piece, got in zip(pieces, received)]
    by = 16
    while by < lax.axis_size("dp"):
        pieces = [piece + swap(piece, by) for piece in pieces]
        by *= 2
    pieces = [piece.astype(BF16) for piece in pieces]
    for stages in ("zx", "xz"):
        received = [gather_start(piece, stage) for piece, stage in zip(pieces, stages)]
        received, pieces = lax.optimization_barrier((received, pieces))
        pieces = [
            jnp.concatenate([piece] + got, axis=0) for piece, got in zip(pieces, received)
        ]
    return pieces, result


def exchanged(value, merge):
    for partners in ((1, 2, 3), (4, 8, 12)):
        received = [swap(value, by) for by in partners]
        received, value = lax.optimization_barrier((received, value))
        value = merge(merge(value, received[0]), merge(received[1], received[2]))
    by = 16
    while by < lax.axis_size("dp"):
        value = merge(value, swap(value, by))
        by *= 2
    return value


def merged_moments(one, two):
    (sum_one, square_one, count_one), (sum_two, square_two, count_two) = one, two
    away = sum_one / count_one - sum_two / count_two
    count = count_one + count_two
    square = (square_one + square_two) + away * away * (count_one * count_two / count)
    return jnp.stack([sum_one + sum_two, square, count])


def per_device(features, kernel_map, occupancy, weights, bn_gain, bn_shift, cotangent):
    rows, channels = features.shape
    peers = lax.axis_size("dp")
    me = lax.axis_index("dp")
    blocks = rows // BLOCK
    inner_rows = rows - 2 * BLOCK
    steps = K // GROUP

    odd = me & 1
    even_pairs = [(i, i ^ 1) for i in range(peers)]
    other_pairs = [(i, ((i + 1) ^ 1) - 1) for i in range(1, peers - 1)]

    def neighbours_swap(to_before, to_after):
        even = lax.ppermute(jnp.where(odd == 1, to_before, to_after), "dp", even_pairs)
        other = lax.ppermute(jnp.where(odd == 1, to_after, to_before), "dp", other_pairs)
        return even, other

    even, other = neighbours_swap(features[:BLOCK], features[rows - BLOCK :])
    map_rows = jnp.transpose(kernel_map)
    odd_flag = odd.reshape(1)

    gain = bn_gain.reshape(1, channels)
    shift = bn_shift.reshape(1, channels)
    smem = pl.BlockSpec(memory_space=pltpu.SMEM)
    vmem = pl.BlockSpec(memory_space=pltpu.VMEM)
    hbm = pl.BlockSpec(memory_space=pltpu.HBM)
    anywhere = pl.BlockSpec(memory_space=pl.ANY)
    groups = K // GROUP
    work = K * rows * channels * 2 * (3 * BLOCK + channels)
    moved = K * channels * channels * 2 * 3

    conv, stats, picked = pl.pallas_call(
        conv_kernel,
        in_specs=[smem, smem, vmem, vmem, vmem, vmem, hbm],
        out_specs=[vmem, vmem, anywhere],
        out_shape=[
            jax.ShapeDtypeStruct((rows, channels), F32),
            jax.ShapeDtypeStruct((3, channels), F32),
            jax.ShapeDtypeStruct((K, rows, channels), BF16),
        ],
        scratch_shapes=[pltpu.VMEM((3 * BLOCK, channels), BF16)] * 2
        + [
            pltpu.VMEM((K, channels, channels), BF16),
            pltpu.VMEM((K, rows, channels), BF16),
            pltpu.VMEM((rows, BLOCK), jnp.int32),
            pltpu.SemaphoreType.DMA((groups,)),
            pltpu.SemaphoreType.DMA((groups,)),
        ],
        compiler_params=params(LIMIT),
        cost_estimate=cost(work, moved),
        name="conv",
    )(occupancy, odd_flag, map_rows, features, even, other, weights)

    stats = exchanged(stats, merged_moments)

    block_out, sums = pl.pallas_call(
        norm_kernel,
        in_specs=[smem] + [vmem] * 6,
        out_shape=[
            jax.ShapeDtypeStruct((rows, channels), BF16),
            jax.ShapeDtypeStruct((2, channels), F32),
        ],
        compiler_params=params(LIMIT),
        cost_estimate=cost(rows * channels * 20, rows * channels * 10),
        name="norm",
    )(occupancy, conv, stats, gain, shift, cotangent, features)

    grads = exchanged(sums, jnp.add)

    core, lane, depth = me & 1, (me >> 1) & 1, (me >> 2) & 3
    place_one = (core * 8 + lane * 4 + depth).reshape(1)
    place_two = (core * 8 + depth * 2 + lane).reshape(1)
    piece_rows = channels // 16
    piece_shape = (8, GROUP, piece_rows, channels)
    piece_types = [
        jax.ShapeDtypeStruct(piece_shape, F32),
        jax.ShapeDtypeStruct(piece_shape, BF16),
    ]
    gradient_scratch = [
        pltpu.VMEM((GROUP, rows, channels), BF16),
        pltpu.VMEM((GROUP, channels, channels), F32),
        pltpu.VMEM(piece_shape, F32),
        pltpu.VMEM(piece_shape, BF16),
        pltpu.SemaphoreType.DMA((GROUP,)),
        pltpu.SemaphoreType.DMA((2, GROUP // PART)),
    ]
    gradient_cost = cost(
        GROUP * rows * channels * channels * 2, GROUP * channels * (channels * 5 + rows * 2)
    )
    grad_conv, *pair_two = pl.pallas_call(
        first_gradient_kernel,
        in_specs=[smem, smem] + [vmem] * 6 + [anywhere],
        out_specs=[vmem, anywhere, anywhere],
        out_shape=[jax.ShapeDtypeStruct((rows, channels), BF16)] + piece_types,
        scratch_shapes=gradient_scratch,
        compiler_params=params(LIMIT),
        cost_estimate=gradient_cost,
        name="weight_gradient_first",
    )(occupancy, place_two, conv, stats, grads, gain, shift, cotangent, picked)
    two = core_reduced(*pair_two)

    def later_gradient(first):
        return pl.pallas_call(
            functools.partial(later_gradient_kernel, first),
            in_specs=[smem, vmem, anywhere],
            out_specs=[anywhere, anywhere],
            out_shape=piece_types,
            scratch_shapes=gradient_scratch,
            compiler_params=params(LIMIT),
            cost_estimate=gradient_cost,
            name="weight_gradient_later",
        )(place_one, grad_conv, picked)

    one = [core_reduced(*later_gradient(first)) for first in (GROUP, 2 * GROUP)]
    one = jnp.concatenate(one, axis=1)

    weight_spec = pl.BlockSpec((GROUP, channels, channels), lambda s: (s, 0, 0))
    one, grad_conv_later = lax.optimization_barrier((one, grad_conv))
    sink_before, sink_own, sink_after = pl.pallas_call(
        push_kernel,
        grid=(groups,),
        in_specs=[full((rows, channels)), full((K, rows)), weight_spec],
        out_specs=[full((BLOCK, channels)), full((rows, channels)), full((BLOCK, channels))],
        out_shape=[
            jax.ShapeDtypeStruct((BLOCK, channels), BF16),
            jax.ShapeDtypeStruct((rows, channels), F32),
            jax.ShapeDtypeStruct((BLOCK, channels), BF16),
        ],
        scratch_shapes=[pltpu.VMEM((rows + 2 * BLOCK, channels), F32)],
        compiler_params=params(LIMIT),
        cost_estimate=cost(work, moved),
        name="push",
    )(grad_conv_later, map_rows, weights)

    def spread_gradient():
        even, other = neighbours_swap(sink_before, sink_after)
        from_prev = jnp.where(odd == 1, even, other).astype(F32)
        from_next = jnp.where(odd == 1, other, even).astype(F32)
        occupied = occupied_rows(occupancy[0], rows)
        received = jnp.concatenate(
            [
                sink_own[:BLOCK] + from_prev,
                sink_own[BLOCK : rows - BLOCK],
                sink_own[rows - BLOCK :] + from_next,
            ],
            axis=0,
        )
        return (jnp.where(occupied, cotangent.astype(F32), 0.0) + received).astype(BF16)

    (own_one, own_two), grad_features = summed_over_devices(
        one, two, lambda: (sink_before, sink_own, sink_after), spread_gradient
    )
    places = jnp.concatenate([place_one, place_two])

    def placed(other, sources, *into):
        return pl.pallas_call(
            functools.partial(place_kernel, other),
            in_specs=[smem, anywhere, anywhere] + [hbm] * len(into),
            out_specs=hbm,
            out_shape=jax.ShapeDtypeStruct(weights.shape, BF16),
            scratch_shapes=[pltpu.SemaphoreType.DMA((16,))],
            input_output_aliases={3: 0} if into else {},
            compiler_params=params(LIMIT),
            cost_estimate=cost(0, K * channels * channels * 2),
            name="place",
        )(places, *sources, *into)

    others = [swap(own_one, 1), swap(own_two, 1)]
    grad_weights = placed(1, others, placed(0, (own_one, own_two)))
    return block_out, grad_features, grad_weights, grads[0], grads[1]


def solution(mesh):
    in_specs = (
        P(("parts", "dp"), None),
        P(("parts", "dp"), None),
        P(("parts", "dp")),
        P(),
        P(),
        P(),
        P(("parts", "dp"), None),
    )
    out_specs = (
        P(("parts", "dp"), None),
        P(("parts", "dp"), None),
        P("parts", None, None),
        P("parts"),
        P("parts"),
    )
    return jax.shard_map(
        per_device, mesh=mesh, in_specs=in_specs, out_specs=out_specs, check_vma=False
    )
```

```python
import functools

import jax
import jax.numpy as jnp
from jax import lax
from jax.experimental import pallas as pl
from jax.experimental.pallas import tpu as pltpu
from jax.sharding import PartitionSpec as P

K = 27
BLOCK = 128
GROUP = 9
K_ONE = 18
EPSILON = 1e-05
F32 = jnp.float32
BF16 = jnp.bfloat16
LARGE = 58 * 1024 * 1024
SMALL = 24 * 1024 * 1024


def merged(merge, values):
    return merge(merge(values[0], values[1]), merge(values[2], values[3]))


def merged_moments(one, two):
    (sum_one, square_one, count_one), (sum_two, square_two, count_two) = one, two
    away = sum_one / count_one - sum_two / count_two
    count = count_one + count_two
    square = (square_one + square_two) + away * away * (count_one * count_two / count)
    return sum_one + sum_two, square, count


def dot(a, b, contract):
    return lax.dot_general(a, b, ((contract[0], contract[1]), ((), ())), preferred_element_type=F32)


def full(shape):
    return pl.BlockSpec(shape, lambda *_: (0,) * len(shape))


def params(limit):
    return pltpu.CompilerParams(vmem_limit_bytes=limit)


def cost(flops, moved):
    return pl.CostEstimate(flops=int(flops), bytes_accessed=int(moved), transcendentals=0)


def occupied_rows(filled, rows):
    position = lax.broadcasted_iota(jnp.int32, (rows, 1), 0)
    return (position < filled - BLOCK) | (position >= rows - BLOCK)


def chosen_slots(slot, slots):
    return jnp.where(slot == slots, 1.0, 0.0).astype(BF16)


def transposed_map(map_ref):
    spare = jnp.zeros((BLOCK - K, map_ref.shape[1]), jnp.int32)
    return jnp.transpose(jnp.concatenate([map_ref[...], spare], axis=0))


def convolve(map_ref, tiles, first_slots, weight_hbm, conv_ref, scratch):
    weight, picked, index, weight_sem = scratch
    groups = K // GROUP

    def fetch(g):
        here = pl.ds(g * GROUP, GROUP)
        return pltpu.make_async_copy(weight_hbm.at[here], weight.at[here], weight_sem.at[g])

    for g in range(groups):
        fetch(g).start()
    index[...] = transposed_map(map_ref)
    conv_ref[...] = jnp.zeros_like(conv_ref)
    slots = lax.broadcasted_iota(jnp.int32, (BLOCK, 3 * BLOCK), 1)

    def group(g, carry):
        local = pltpu.roll(index[...], lax.rem(BLOCK - g * GROUP, BLOCK), 1)
        for b, tile in enumerate(tiles):
            here = slice(b * BLOCK, (b + 1) * BLOCK)
            slot = local[here] - first_slots[b]
            for j in range(GROUP):
                chosen = chosen_slots(slot[:, j : j + 1], slots)
                picked[j, here, :] = dot(chosen, tile[...], ((1,), (0,))).astype(BF16)
        fetch(g).wait()
        total = conv_ref[...]
        for j in range(GROUP):
            total = total + dot(picked[j], weight[g * GROUP + j], ((1,), (0,)))
        conv_ref[...] = total
        return carry

    lax.fori_loop(0, groups, group, 0)


def inner_kernel(map_ref, own_ref, weight_hbm, conv_ref, chosen_map, *scratch):
    rows = own_ref.shape[0]
    chosen_map[...] = map_ref[:, BLOCK : rows - BLOCK]
    blocks = range(1, rows // BLOCK - 1)
    tiles = [own_ref.at[(b - 1) * BLOCK : (b + 2) * BLOCK] for b in blocks]
    first_slots = [rows - BLOCK + b * BLOCK for b in blocks]
    convolve(chosen_map, tiles, first_slots, weight_hbm, conv_ref, scratch)


def outer_kernel(
    filled_ref, odd_ref, map_ref, own_ref, even_ref, other_ref, inner_ref, weight_hbm,
    conv_ref, stats_ref, window_ref, chosen_map, *scratch,
):
    rows = own_ref.shape[0]
    odd = odd_ref[0] == 1
    window_ref[0:BLOCK, :] = jnp.where(odd, even_ref[...], other_ref[...])
    window_ref[BLOCK : rows + BLOCK, :] = own_ref[...]
    window_ref[rows + BLOCK :, :] = jnp.where(odd, other_ref[...], even_ref[...])
    chosen_map[:, 0:BLOCK] = map_ref[:, 0:BLOCK]
    chosen_map[:, BLOCK:] = map_ref[:, rows - BLOCK :]
    tiles = [window_ref.at[0 : 3 * BLOCK], window_ref.at[rows - BLOCK :]]
    first_slots = [rows - BLOCK, 2 * rows - 2 * BLOCK]
    convolve(chosen_map, tiles, first_slots, weight_hbm, conv_ref, scratch)
    filled = filled_ref[0]
    count = filled.astype(F32)
    conv = whole(inner_ref, conv_ref)
    occupied = occupied_rows(filled, rows)
    sums = jnp.sum(jnp.where(occupied, conv, 0.0), axis=0, keepdims=True)
    off = jnp.where(occupied, conv - sums / count, 0.0)
    squares = jnp.sum(off * off, axis=0, keepdims=True)
    stats_ref[...] = jnp.concatenate([sums, squares, jnp.full_like(sums, count)], axis=0)


def whole(inner_ref, outer_ref):
    return jnp.concatenate([outer_ref[0:BLOCK, :], inner_ref[...], outer_ref[BLOCK:, :]], axis=0)


def normalised(filled, inner_ref, outer_ref, stats_refs, gain_ref, shift_ref, cotangent_ref):
    conv = whole(inner_ref, outer_ref)
    sums, squares, total = merged(
        merged_moments, [[ref[i : i + 1, :] for i in range(3)] for ref in stats_refs]
    )
    center = sums / total
    inverse = lax.rsqrt(squares / total + EPSILON)
    occupied = occupied_rows(filled, conv.shape[0])
    normed = (conv - center) * inverse
    affine = gain_ref[...] * normed + shift_ref[...]
    upstream = jnp.where(occupied & (affine > 0.0), cotangent_ref[...].astype(F32), 0.0)
    return occupied, normed, affine, upstream, inverse, total


def norm_kernel(
    filled_ref, inner_ref, outer_ref, gain_ref, shift_ref, cotangent_ref, feature_ref, *refs
):
    *stats_refs, out_ref, sums_ref = refs
    occupied, normed, affine, upstream, _, _ = normalised(
        filled_ref[0], inner_ref, outer_ref, stats_refs, gain_ref, shift_ref, cotangent_ref
    )
    out = jnp.maximum(affine, 0.0) + feature_ref[...].astype(F32)
    out_ref[...] = jnp.where(occupied, out, 0.0).astype(BF16)
    sums_ref[...] = jnp.concatenate(
        [jnp.sum(upstream * normed, axis=0, keepdims=True), jnp.sum(upstream, axis=0, keepdims=True)],
        axis=0,
    )


def kernel_gradient(first, place, map_ref, window_ref, grad, keep_any, send_any, scratch):
    index, picked, product, keep, send, out_sem = scratch
    half, count, rows = keep.shape[:3]
    index[...] = transposed_map(map_ref)
    slots = lax.broadcasted_iota(jnp.int32, (BLOCK, 3 * BLOCK), 1)

    def store(g):
        here = pl.ds(g * GROUP, GROUP)
        return [
            pltpu.make_async_copy(keep.at[:, here], keep_any.at[:, here], out_sem.at[0, g]),
            pltpu.make_async_copy(send.at[:, here], send_any.at[:, here], out_sem.at[1, g]),
        ]

    def group(g, carry):
        local = pltpu.roll(index[...], lax.rem(BLOCK - first - g * GROUP, BLOCK), 1)
        for j in range(GROUP):
            for b in range(grad.shape[0] // BLOCK):
                here = slice(b * BLOCK, (b + 1) * BLOCK)
                slot = local[here, j : j + 1] - (grad.shape[0] + (b - 1) * BLOCK)
                tile = window_ref[b * BLOCK : (b + 3) * BLOCK, :]
                chosen = chosen_slots(slot, slots)
                picked[j, here, :] = dot(chosen, tile, ((1,), (0,))).astype(BF16)
        for j in range(GROUP):
            product[j] = dot(picked[j], grad[...], ((0,), (0,)))
            for piece in range(16):
                start = pl.multiple_of(lax.bitwise_xor(jnp.int32(piece), place) * rows, rows)
                value = product[j, pl.ds(start, rows), :]
                if piece < half:
                    keep[piece, g * GROUP + j] = value
                else:
                    send[piece - half, g * GROUP + j] = value.astype(BF16)
        for copy in store(g):
            copy.start()
        return carry

    lax.fori_loop(0, count // GROUP, group, 0)
    for g in range(count // GROUP):
        for copy in store(g):
            copy.wait()


def first_gradient_kernel(
    parts, filled_ref, place_ref, inner_ref, outer_ref, gain_ref, shift_ref, cotangent_ref,
    map_ref, window_ref, *refs,
):
    stats_refs, grads_refs, refs = refs[:parts], refs[parts : 2 * parts], refs[2 * parts :]
    grad_ref, sums_ref, keep_any, send_any, *scratch = refs
    occupied, normed, _, upstream, inverse, total = normalised(
        filled_ref[0], inner_ref, outer_ref, stats_refs, gain_ref, shift_ref, cotangent_ref
    )
    sums = merged(jnp.add, [ref[...] for ref in grads_refs])
    sums_ref[...] = sums
    grad_conv = gain_ref[...] * inverse * (
        upstream - sums[1:2, :] / total - normed * sums[0:1, :] / total
    )
    grad_ref[...] = jnp.where(occupied, grad_conv, 0.0).astype(BF16)
    kernel_gradient(0, place_ref[0], map_ref, window_ref, grad_ref, keep_any, send_any, scratch)


def second_gradient_kernel(
    place_ref, grad_ref, map_ref, window_ref, keep_any, send_any, *scratch
):
    kernel_gradient(
        K_ONE, place_ref[0], map_ref, window_ref, grad_ref, keep_any, send_any, scratch
    )


def push_kernel(grad_ref, index_ref, weight_ref, before_ref, own_ref, after_ref, sink):
    step = pl.program_id(0)

    @pl.when(step == 0)
    def _():
        sink[...] = jnp.zeros_like(sink)

    blocks = grad_ref.shape[0] // BLOCK
    here = jnp.concatenate([index_ref[step * GROUP + j, :][None] for j in range(GROUP)], axis=0)
    block_of = lax.broadcasted_iota(jnp.int32, here.shape, 1) // BLOCK
    local = here - (3 + block_of) * BLOCK
    slots = lax.broadcasted_iota(jnp.int32, (3 * BLOCK, BLOCK), 0)
    pushed = [
        dot(grad_ref[...], weight_ref[j], ((1,), (1,))).astype(BF16) for j in range(GROUP)
    ]
    for b in range(blocks):
        rows = slice(b * BLOCK, (b + 1) * BLOCK)
        chosen = jnp.concatenate(
            [
                jnp.where(local[j : j + 1, rows] == slots, 1.0, 0.0).astype(BF16)
                for j in range(GROUP)
            ],
            axis=1,
        )
        stacked = jnp.concatenate([pushed[j][rows] for j in range(GROUP)], axis=0)
        window = slice(b * BLOCK, (b + 3) * BLOCK)
        sink[window, :] = sink[window, :] + dot(chosen, stacked, ((1,), (0,)))

    @pl.when(step == pl.num_programs(0) - 1)
    def _():
        before_ref[...] = sink[0:BLOCK, :].astype(BF16)
        own_ref[...] = sink[BLOCK : (blocks + 1) * BLOCK, :]
        after_ref[...] = sink[(blocks + 1) * BLOCK :, :].astype(BF16)


def place_kernel(other, places_ref, one, two, *refs):
    out_ref, sems = refs[-2:]
    half, split, rows = one.shape[:3]
    copies = []
    for piece in range(half):
        for part, source in enumerate((one, two)):
            relative = jnp.int32(piece + half * other)
            place = lax.bitwise_xor(relative, places_ref[part])
            start = pl.multiple_of(place * rows, rows)
            first = 0 if part == 0 else split
            copies.append(
                pltpu.make_async_copy(
                    source.at[piece],
                    out_ref.at[pl.ds(first, source.shape[1]), pl.ds(start, rows), :],
                    sems.at[len(copies)],
                )
            )
    for copy in copies:
        copy.start()
    for copy in copies:
        copy.wait()


def swap(value, by):
    peers = lax.axis_size("dp")
    return lax.ppermute(value, "dp", [(i, i ^ by) for i in range(peers)])


STAGES = {"c": (1,), "x": (2,), "z": (4, 8, 12)}


def split(total, stage):
    size = total.shape[0] // (len(STAGES[stage]) + 1)
    sends = [
        total[(i + 1) * size : (i + 2) * size].astype(BF16) for i in range(len(STAGES[stage]))
    ]
    return total[:size], sends


def swapped(sends, stage):
    return [swap(send, by) for send, by in zip(sends, STAGES[stage])]


def added(kept, received):
    return functools.reduce(lambda a, b: a + b.astype(F32), received, kept)


def gather_start(piece, stage):
    return [swap(piece, by) for by in STAGES[stage]]


def core_reduced(keep, send):
    return keep + swap(send, 1).astype(F32)


def summed_over_devices(one, two, grad_conv, push, spread):
    parts = [split(one, "x"), split(two, "z")]
    parts, grad_conv = lax.optimization_barrier((parts, grad_conv))
    received = [swapped(sends, stage) for (_, sends), stage in zip(parts, "xz")]
    received, sinks = lax.optimization_barrier((received, push(grad_conv)))
    pieces = [added(kept, got) for (kept, _), got in zip(parts, received)]
    parts = [split(piece, stage) for piece, stage in zip(pieces, "zx")]
    received = [swapped(sends, stage) for (_, sends), stage in zip(parts, "zx")]
    received, result = lax.optimization_barrier((received, spread(*sinks)))
    pieces = [added(kept, got) for (kept, _), got in zip(parts, received)]
    by = 16
    while by < lax.axis_size("dp"):
        pieces = [piece + swap(piece, by) for piece in pieces]
        by *= 2
    pieces = [piece.astype(BF16) for piece in pieces]
    for stages in ("zx", "xz"):
        received = [gather_start(piece, stage) for piece, stage in zip(pieces, stages)]
        received, pieces = lax.optimization_barrier((received, pieces))
        pieces = [
            jnp.concatenate([piece] + got, axis=0) for piece, got in zip(pieces, received)
        ]
    return pieces, result


def exchanged(value, merge):
    received = [swap(value, by) for by in (1, 2, 3)]
    value = merged(merge, [value] + received)
    by = 16
    while by < lax.axis_size("dp"):
        value = merge(value, swap(value, by))
        by *= 2
    return [value] + [swap(value, by) for by in (4, 8, 12)]


def stacked_moments(one, two):
    return jnp.stack(merged_moments(one, two))


def per_device(features, kernel_map, occupancy, weights, bn_gain, bn_shift, cotangent):
    rows, channels = features.shape
    peers = lax.axis_size("dp")
    me = lax.axis_index("dp")
    blocks = rows // BLOCK
    inner_rows = rows - 2 * BLOCK
    steps = K // GROUP

    odd = me & 1
    even_pairs = [(i, i ^ 1) for i in range(peers)]
    other_pairs = [(i, ((i + 1) ^ 1) - 1) for i in range(1, peers - 1)]

    def neighbours_swap(to_before, to_after):
        even = lax.ppermute(jnp.where(odd == 1, to_before, to_after), "dp", even_pairs)
        other = lax.ppermute(jnp.where(odd == 1, to_after, to_before), "dp", other_pairs)
        return even, other

    even, other = neighbours_swap(features[:BLOCK], features[rows - BLOCK :])
    map_rows = jnp.transpose(kernel_map)
    odd_flag = odd.reshape(1)

    gain = bn_gain.reshape(1, channels)
    shift = bn_shift.reshape(1, channels)
    smem = pl.BlockSpec(memory_space=pltpu.SMEM)
    vmem = pl.BlockSpec(memory_space=pltpu.VMEM)
    hbm = pl.BlockSpec(memory_space=pltpu.HBM)
    anywhere = pl.BlockSpec(memory_space=pl.ANY)
    groups = K // GROUP
    work = K * rows * channels * 2 * (3 * BLOCK + channels)
    moved = K * channels * channels * 2 * 3

    half_conv = jax.ShapeDtypeStruct((2 * BLOCK, channels), F32)
    scratch = [
        pltpu.VMEM((K, 2 * BLOCK), jnp.int32),
        pltpu.VMEM((K, channels, channels), BF16),
        pltpu.VMEM((GROUP, 2 * BLOCK, channels), BF16),
        pltpu.VMEM((2 * BLOCK, BLOCK), jnp.int32),
        pltpu.SemaphoreType.DMA((groups,)),
    ]

    inner = pl.pallas_call(
        inner_kernel,
        in_specs=[vmem, vmem, hbm],
        out_specs=vmem,
        out_shape=half_conv,
        scratch_shapes=scratch,
        compiler_params=params(LARGE),
        cost_estimate=cost(work / 2, moved),
        name="conv_inner",
    )(map_rows, features, weights)

    outer, stats, window = pl.pallas_call(
        outer_kernel,
        in_specs=[smem, smem, vmem, vmem, vmem, vmem, vmem, hbm],
        out_specs=[vmem, vmem, vmem],
        out_shape=[
            half_conv,
            jax.ShapeDtypeStruct((3, channels), F32),
            jax.ShapeDtypeStruct((rows + 2 * BLOCK, channels), BF16),
        ],
        scratch_shapes=scratch,
        compiler_params=params(LARGE),
        cost_estimate=cost(work / 2, moved),
        name="conv_outer",
    )(occupancy, odd_flag, map_rows, features, even, other, inner, weights)

    stats = exchanged(stats, stacked_moments)

    block_out, sums = pl.pallas_call(
        norm_kernel,
        in_specs=[smem] + [vmem] * 10,
        out_shape=[
            jax.ShapeDtypeStruct((rows, channels), BF16),
            jax.ShapeDtypeStruct((2, channels), F32),
        ],
        compiler_params=params(SMALL),
        cost_estimate=cost(rows * channels * 20, rows * channels * 10),
        name="norm",
    )(occupancy, inner, outer, gain, shift, cotangent, features, *stats)

    grads = exchanged(sums, jnp.add)

    core, lane, depth = me & 1, (me >> 1) & 1, (me >> 2) & 3
    place_one = (core * 8 + lane * 4 + depth).reshape(1)
    place_two = (core * 8 + depth * 2 + lane).reshape(1)
    piece_rows = channels // 16

    def gradient(kernel, count, in_specs, out_specs, out_shape, name):
        shape = (8, count, piece_rows, channels)
        return pl.pallas_call(
            kernel,
            in_specs=in_specs,
            out_specs=out_specs + [anywhere, anywhere],
            out_shape=out_shape
            + [jax.ShapeDtypeStruct(shape, F32), jax.ShapeDtypeStruct(shape, BF16)],
            scratch_shapes=[
                pltpu.VMEM((rows, BLOCK), jnp.int32),
                pltpu.VMEM((GROUP, rows, channels), BF16),
                pltpu.VMEM((GROUP, channels, channels), F32),
                pltpu.VMEM(shape, F32),
                pltpu.VMEM(shape, BF16),
                pltpu.SemaphoreType.DMA((2, count // GROUP)),
            ],
            compiler_params=params(SMALL),
            cost_estimate=cost(work * count / K, count * channels * channels * 6),
            name=name,
        )

    grad_conv, sums, *pair_one = gradient(
        functools.partial(first_gradient_kernel, len(stats)),
        K_ONE,
        [smem, smem] + [vmem] * 15,
        [vmem, vmem],
        [
            jax.ShapeDtypeStruct((rows, channels), BF16),
            jax.ShapeDtypeStruct((2, channels), F32),
        ],
        "weight_gradient_one",
    )(
        occupancy, place_one, inner, outer, gain, shift, cotangent, map_rows, window,
        *stats, *grads,
    )
    one = core_reduced(*pair_one)
    pair_two = gradient(
        second_gradient_kernel, K - K_ONE, [smem] + [vmem] * 3, [], [], "weight_gradient_two"
    )(place_two, grad_conv, map_rows, window)
    two = core_reduced(*pair_two)

    weight_spec = pl.BlockSpec((GROUP, channels, channels), lambda s: (s, 0, 0))

    def push(grad_conv):
        return pl.pallas_call(
            push_kernel,
            grid=(groups,),
            in_specs=[full((rows, channels)), full((K, rows)), weight_spec],
            out_specs=[full((BLOCK, channels)), full((rows, channels)), full((BLOCK, channels))],
            out_shape=[
                jax.ShapeDtypeStruct((BLOCK, channels), BF16),
                jax.ShapeDtypeStruct((rows, channels), F32),
                jax.ShapeDtypeStruct((BLOCK, channels), BF16),
            ],
            scratch_shapes=[pltpu.VMEM((rows + 2 * BLOCK, channels), F32)],
            compiler_params=params(SMALL),
            cost_estimate=cost(work, moved),
            name="push",
        )(grad_conv, map_rows, weights)

    def spread_gradient(sink_before, sink_own, sink_after):
        even, other = neighbours_swap(sink_before, sink_after)
        from_prev = jnp.where(odd == 1, even, other).astype(F32)
        from_next = jnp.where(odd == 1, other, even).astype(F32)
        occupied = occupied_rows(occupancy[0], rows)
        received = jnp.concatenate(
            [
                sink_own[:BLOCK] + from_prev,
                sink_own[BLOCK : rows - BLOCK],
                sink_own[rows - BLOCK :] + from_next,
            ],
            axis=0,
        )
        return (jnp.where(occupied, cotangent.astype(F32), 0.0) + received).astype(BF16)

    (own_one, own_two), grad_features = summed_over_devices(
        one, two, grad_conv, push, spread_gradient
    )
    places = jnp.concatenate([place_one, place_two])

    def placed(other, sources, *into):
        return pl.pallas_call(
            functools.partial(place_kernel, other),
            in_specs=[smem, anywhere, anywhere] + [hbm] * len(into),
            out_specs=hbm,
            out_shape=jax.ShapeDtypeStruct(weights.shape, BF16),
            scratch_shapes=[pltpu.SemaphoreType.DMA((16,))],
            input_output_aliases={3: 0} if into else {},
            compiler_params=params(SMALL),
            cost_estimate=cost(0, K * channels * channels * 2),
            name="place",
        )(places, *sources, *into)

    others = [swap(own_one, 1), swap(own_two, 1)]
    grad_weights = placed(1, others, placed(0, (own_one, own_two)))
    return block_out, grad_features, grad_weights, sums[0], sums[1]


def solution(mesh):
    in_specs = (
        P(("parts", "dp"), None),
        P(("parts", "dp"), None),
        P(("parts", "dp")),
        P(),
        P(),
        P(),
        P(("parts", "dp"), None),
    )
    out_specs = (
        P(("parts", "dp"), None),
        P(("parts", "dp"), None),
        P("parts", None, None),
        P("parts"),
        P("parts"),
    )
    return jax.shard_map(
        per_device, mesh=mesh, in_specs=in_specs, out_specs=out_specs, check_vma=False
    )
```

```python
import functools

import jax
import jax.numpy as jnp
from jax import lax
from jax.experimental import pallas as pl
from jax.experimental.pallas import tpu as pltpu
from jax.sharding import PartitionSpec as P

K = 27
BLOCK = 128
GROUP = 9
K_ONE = 18
EPSILON = 1e-05
F32 = jnp.float32
BF16 = jnp.bfloat16
LIMIT = 24 * 1024 * 1024


def merged(merge, values):
    return merge(merge(values[0], values[1]), merge(values[2], values[3]))


def merged_moments(one, two):
    (sum_one, square_one, count_one), (sum_two, square_two, count_two) = one, two
    away = sum_one / count_one - sum_two / count_two
    count = count_one + count_two
    square = (square_one + square_two) + away * away * (count_one * count_two / count)
    return sum_one + sum_two, square, count


def dot(a, b, contract):
    return lax.dot_general(a, b, ((contract[0], contract[1]), ((), ())), preferred_element_type=F32)


def full(shape):
    return pl.BlockSpec(shape, lambda *_: (0,) * len(shape))


def params(limit):
    return pltpu.CompilerParams(vmem_limit_bytes=limit)


def cost(flops, moved):
    return pl.CostEstimate(flops=int(flops), bytes_accessed=int(moved), transcendentals=0)


def occupied_rows(filled, rows):
    position = lax.broadcasted_iota(jnp.int32, (rows, 1), 0)
    return (position < filled - BLOCK) | (position >= rows - BLOCK)


def chosen_slots(slot, slots):
    return jnp.where(slot == slots, 1.0, 0.0).astype(BF16)


def transposed_map(map_ref):
    spare = jnp.zeros((BLOCK - K, map_ref.shape[1]), jnp.int32)
    return jnp.transpose(jnp.concatenate([map_ref[...], spare], axis=0))


def convolve(map_ref, tiles, first_slots, weight_hbm, conv_ref, scratch):
    weight, picked, index, weight_sem = scratch
    groups = K // GROUP

    def fetch(g):
        here = pl.ds(g * GROUP, GROUP)
        return pltpu.make_async_copy(weight_hbm.at[here], weight.at[here], weight_sem.at[g])

    for g in range(groups):
        fetch(g).start()
    index[...] = transposed_map(map_ref)
    conv_ref[...] = jnp.zeros_like(conv_ref)
    slots = lax.broadcasted_iota(jnp.int32, (BLOCK, 3 * BLOCK), 1)

    def group(g, carry):
        local = pltpu.roll(index[...], lax.rem(BLOCK - g * GROUP, BLOCK), 1)
        for b, tile in enumerate(tiles):
            here = slice(b * BLOCK, (b + 1) * BLOCK)
            slot = local[here] - first_slots[b]
            for j in range(GROUP):
                chosen = chosen_slots(slot[:, j : j + 1], slots)
                picked[j, here, :] = dot(chosen, tile[...], ((1,), (0,))).astype(BF16)
        fetch(g).wait()
        total = conv_ref[...]
        for j in range(GROUP):
            total = total + dot(picked[j], weight[g * GROUP + j], ((1,), (0,)))
        conv_ref[...] = total
        return carry

    lax.fori_loop(0, groups, group, 0)


def inner_kernel(map_ref, own_ref, weight_hbm, conv_ref, chosen_map, *scratch):
    rows = own_ref.shape[0]
    chosen_map[...] = map_ref[:, BLOCK : rows - BLOCK]
    blocks = range(1, rows // BLOCK - 1)
    tiles = [own_ref.at[(b - 1) * BLOCK : (b + 2) * BLOCK] for b in blocks]
    first_slots = [rows - BLOCK + b * BLOCK for b in blocks]
    convolve(chosen_map, tiles, first_slots, weight_hbm, conv_ref, scratch)


def outer_kernel(
    filled_ref, odd_ref, map_ref, own_ref, even_ref, other_ref, inner_ref, weight_hbm,
    conv_ref, stats_ref, window_ref, chosen_map, *scratch,
):
    rows = own_ref.shape[0]
    odd = odd_ref[0] == 1
    window_ref[0:BLOCK, :] = jnp.where(odd, even_ref[...], other_ref[...])
    window_ref[BLOCK : rows + BLOCK, :] = own_ref[...]
    window_ref[rows + BLOCK :, :] = jnp.where(odd, other_ref[...], even_ref[...])
    chosen_map[:, 0:BLOCK] = map_ref[:, 0:BLOCK]
    chosen_map[:, BLOCK:] = map_ref[:, rows - BLOCK :]
    tiles = [window_ref.at[0 : 3 * BLOCK], window_ref.at[rows - BLOCK :]]
    first_slots = [rows - BLOCK, 2 * rows - 2 * BLOCK]
    convolve(chosen_map, tiles, first_slots, weight_hbm, conv_ref, scratch)
    filled = filled_ref[0]
    count = filled.astype(F32)
    conv = whole(inner_ref, conv_ref)
    occupied = occupied_rows(filled, rows)
    sums = jnp.sum(jnp.where(occupied, conv, 0.0), axis=0, keepdims=True)
    off = jnp.where(occupied, conv - sums / count, 0.0)
    squares = jnp.sum(off * off, axis=0, keepdims=True)
    stats_ref[...] = jnp.concatenate([sums, squares, jnp.full_like(sums, count)], axis=0)


def whole(inner_ref, outer_ref):
    return jnp.concatenate([outer_ref[0:BLOCK, :], inner_ref[...], outer_ref[BLOCK:, :]], axis=0)


def normalised(filled, inner_ref, outer_ref, stats_refs, gain_ref, shift_ref, cotangent_ref):
    conv = whole(inner_ref, outer_ref)
    sums, squares, total = merged(
        merged_moments, [[ref[i : i + 1, :] for i in range(3)] for ref in stats_refs]
    )
    center = sums / total
    inverse = lax.rsqrt(squares / total + EPSILON)
    occupied = occupied_rows(filled, conv.shape[0])
    normed = (conv - center) * inverse
    affine = gain_ref[...] * normed + shift_ref[...]
    upstream = jnp.where(occupied & (affine > 0.0), cotangent_ref[...].astype(F32), 0.0)
    return occupied, normed, affine, upstream, inverse, total


def norm_kernel(
    filled_ref, inner_ref, outer_ref, gain_ref, shift_ref, cotangent_ref, feature_ref, *refs
):
    *stats_refs, out_ref, sums_ref = refs
    occupied, normed, affine, upstream, _, _ = normalised(
        filled_ref[0], inner_ref, outer_ref, stats_refs, gain_ref, shift_ref, cotangent_ref
    )
    out = jnp.maximum(affine, 0.0) + feature_ref[...].astype(F32)
    out_ref[...] = jnp.where(occupied, out, 0.0).astype(BF16)
    sums_ref[...] = jnp.concatenate(
        [jnp.sum(upstream * normed, axis=0, keepdims=True), jnp.sum(upstream, axis=0, keepdims=True)],
        axis=0,
    )


def kernel_gradient(first, place, map_ref, window_ref, grad, keep_any, send_any, scratch):
    index, picked, product, keep, send, out_sem = scratch
    half, count, rows = keep.shape[:3]
    index[...] = transposed_map(map_ref)
    slots = lax.broadcasted_iota(jnp.int32, (BLOCK, 3 * BLOCK), 1)

    def store(g):
        here = pl.ds(g * GROUP, GROUP)
        return [
            pltpu.make_async_copy(keep.at[:, here], keep_any.at[:, here], out_sem.at[0, g]),
            pltpu.make_async_copy(send.at[:, here], send_any.at[:, here], out_sem.at[1, g]),
        ]

    def group(g, carry):
        local = pltpu.roll(index[...], lax.rem(BLOCK - first - g * GROUP, BLOCK), 1)
        for j in range(GROUP):
            for b in range(grad.shape[0] // BLOCK):
                here = slice(b * BLOCK, (b + 1) * BLOCK)
                slot = local[here, j : j + 1] - (grad.shape[0] + (b - 1) * BLOCK)
                tile = window_ref[b * BLOCK : (b + 3) * BLOCK, :]
                chosen = chosen_slots(slot, slots)
                picked[j, here, :] = dot(chosen, tile, ((1,), (0,))).astype(BF16)
        for j in range(GROUP):
            product[j] = dot(picked[j], grad[...], ((0,), (0,)))
            for piece in range(16):
                start = pl.multiple_of(lax.bitwise_xor(jnp.int32(piece), place) * rows, rows)
                value = product[j, pl.ds(start, rows), :]
                if piece < half:
                    keep[piece, g * GROUP + j] = value
                else:
                    send[piece - half, g * GROUP + j] = value.astype(BF16)
        for copy in store(g):
            copy.start()
        return carry

    lax.fori_loop(0, count // GROUP, group, 0)
    for g in range(count // GROUP):
        for copy in store(g):
            copy.wait()


def first_gradient_kernel(
    parts, filled_ref, place_ref, inner_ref, outer_ref, gain_ref, shift_ref, cotangent_ref,
    map_ref, window_ref, *refs,
):
    stats_refs, grads_refs, refs = refs[:parts], refs[parts : 2 * parts], refs[2 * parts :]
    grad_ref, sums_ref, keep_any, send_any, *scratch = refs
    occupied, normed, _, upstream, inverse, total = normalised(
        filled_ref[0], inner_ref, outer_ref, stats_refs, gain_ref, shift_ref, cotangent_ref
    )
    sums = merged(jnp.add, [ref[...] for ref in grads_refs])
    sums_ref[...] = sums
    grad_conv = gain_ref[...] * inverse * (
        upstream - sums[1:2, :] / total - normed * sums[0:1, :] / total
    )
    grad_ref[...] = jnp.where(occupied, grad_conv, 0.0).astype(BF16)
    kernel_gradient(0, place_ref[0], map_ref, window_ref, grad_ref, keep_any, send_any, scratch)


def second_gradient_kernel(
    place_ref, grad_ref, map_ref, window_ref, keep_any, send_any, *scratch
):
    kernel_gradient(
        K_ONE, place_ref[0], map_ref, window_ref, grad_ref, keep_any, send_any, scratch
    )


def push_kernel(grad_ref, index_ref, weight_ref, before_ref, own_ref, after_ref, sink):
    step = pl.program_id(0)

    @pl.when(step == 0)
    def _():
        sink[...] = jnp.zeros_like(sink)

    blocks = grad_ref.shape[0] // BLOCK
    here = jnp.concatenate([index_ref[step * GROUP + j, :][None] for j in range(GROUP)], axis=0)
    block_of = lax.broadcasted_iota(jnp.int32, here.shape, 1) // BLOCK
    local = here - (3 + block_of) * BLOCK
    slots = lax.broadcasted_iota(jnp.int32, (3 * BLOCK, BLOCK), 0)
    pushed = [
        dot(grad_ref[...], weight_ref[j], ((1,), (1,))).astype(BF16) for j in range(GROUP)
    ]
    for b in range(blocks):
        rows = slice(b * BLOCK, (b + 1) * BLOCK)
        chosen = jnp.concatenate(
            [
                jnp.where(local[j : j + 1, rows] == slots, 1.0, 0.0).astype(BF16)
                for j in range(GROUP)
            ],
            axis=1,
        )
        stacked = jnp.concatenate([pushed[j][rows] for j in range(GROUP)], axis=0)
        window = slice(b * BLOCK, (b + 3) * BLOCK)
        sink[window, :] = sink[window, :] + dot(chosen, stacked, ((1,), (0,)))

    @pl.when(step == pl.num_programs(0) - 1)
    def _():
        before_ref[...] = sink[0:BLOCK, :].astype(BF16)
        own_ref[...] = sink[BLOCK : (blocks + 1) * BLOCK, :]
        after_ref[...] = sink[(blocks + 1) * BLOCK :, :].astype(BF16)


def place_kernel(other, places_ref, one, two, *refs):
    out_ref, sems = refs[-2:]
    half, split, rows = one.shape[:3]
    copies = []
    for piece in range(half):
        for part, source in enumerate((one, two)):
            relative = jnp.int32(piece + half * other)
            place = lax.bitwise_xor(relative, places_ref[part])
            start = pl.multiple_of(place * rows, rows)
            first = 0 if part == 0 else split
            copies.append(
                pltpu.make_async_copy(
                    source.at[piece],
                    out_ref.at[pl.ds(first, source.shape[1]), pl.ds(start, rows), :],
                    sems.at[len(copies)],
                )
            )
    for copy in copies:
        copy.start()
    for copy in copies:
        copy.wait()


def swap(value, by):
    peers = lax.axis_size("dp")
    return lax.ppermute(value, "dp", [(i, i ^ by) for i in range(peers)])


STAGES = {"c": (1,), "x": (2,), "z": (4, 8, 12)}


def part(terms, first, size):
    return functools.reduce(
        jnp.add, [term[first : first + size].astype(F32) for term in terms]
    )


def split(terms, stage):
    partners = STAGES[stage]
    size = terms[0].shape[0] // (len(partners) + 1)
    sends = [part(terms, (i + 1) * size, size).astype(BF16) for i in range(len(partners))]
    return part(terms, 0, size), sends


def swapped(sends, stage):
    return [swap(send, by) for send, by in zip(sends, STAGES[stage])]


def gather_start(piece, stage):
    return [swap(piece, by) for by in STAGES[stage]]


def summed_over_devices(one, two, grad_conv, push, spread):
    parts = [split(one, "x"), split(two, "z")]
    parts, grad_conv = lax.optimization_barrier((parts, grad_conv))
    received = [swapped(sends, stage) for (_, sends), stage in zip(parts, "xz")]
    received, sinks = lax.optimization_barrier((received, push(grad_conv)))
    parts = [
        split([kept] + got, stage) for (kept, _), got, stage in zip(parts, received, "zx")
    ]
    parts, sinks = lax.optimization_barrier((parts, sinks))
    received = [swapped(sends, stage) for (_, sends), stage in zip(parts, "zx")]
    halo = spread(sinks)
    received, halo = lax.optimization_barrier((received, halo))
    pieces = [part([kept] + got, 0, 1) for (kept, _), got in zip(parts, received)]
    by = 16
    while by < lax.axis_size("dp"):
        pieces = [piece + swap(piece, by) for piece in pieces]
        by *= 2
    pieces = [piece.astype(BF16) for piece in pieces]
    for stages in ("zx", "xz"):
        received = [gather_start(piece, stage) for piece, stage in zip(pieces, stages)]
        received, pieces = lax.optimization_barrier((received, pieces))
        pieces = [
            jnp.concatenate([piece] + got, axis=0) for piece, got in zip(pieces, received)
        ]
    return pieces, halo


def exchanged(value, merge):
    received = [swap(value, by) for by in (1, 2, 3)]
    value = merged(merge, [value] + received)
    by = 16
    while by < lax.axis_size("dp"):
        value = merge(value, swap(value, by))
        by *= 2
    return [value] + [swap(value, by) for by in (4, 8, 12)]


def stacked_moments(one, two):
    return jnp.stack(merged_moments(one, two))


def per_device(features, kernel_map, occupancy, weights, bn_gain, bn_shift, cotangent):
    rows, channels = features.shape
    peers = lax.axis_size("dp")
    me = lax.axis_index("dp")
    blocks = rows // BLOCK
    inner_rows = rows - 2 * BLOCK
    steps = K // GROUP

    odd = me & 1
    even_pairs = [(i, i ^ 1) for i in range(peers)]
    other_pairs = [(i, ((i + 1) ^ 1) - 1) for i in range(1, peers - 1)]

    def neighbours_swap(to_before, to_after):
        even = lax.ppermute(jnp.where(odd == 1, to_before, to_after), "dp", even_pairs)
        other = lax.ppermute(jnp.where(odd == 1, to_after, to_before), "dp", other_pairs)
        return even, other

    even, other = neighbours_swap(features[:BLOCK], features[rows - BLOCK :])
    map_rows = jnp.transpose(kernel_map)
    odd_flag = odd.reshape(1)

    gain = bn_gain.reshape(1, channels)
    shift = bn_shift.reshape(1, channels)
    smem = pl.BlockSpec(memory_space=pltpu.SMEM)
    vmem = pl.BlockSpec(memory_space=pltpu.VMEM)
    hbm = pl.BlockSpec(memory_space=pltpu.HBM)
    anywhere = pl.BlockSpec(memory_space=pl.ANY)
    groups = K // GROUP
    work = K * rows * channels * 2 * (3 * BLOCK + channels)
    moved = K * channels * channels * 2 * 3

    half_conv = jax.ShapeDtypeStruct((2 * BLOCK, channels), F32)
    scratch = [
        pltpu.VMEM((K, 2 * BLOCK), jnp.int32),
        pltpu.VMEM((K, channels, channels), BF16),
        pltpu.VMEM((GROUP, 2 * BLOCK, channels), BF16),
        pltpu.VMEM((2 * BLOCK, BLOCK), jnp.int32),
        pltpu.SemaphoreType.DMA((groups,)),
    ]

    def in_hbm(value):
        return pltpu.with_memory_space_constraint(value, pltpu.HBM)

    inner = pl.pallas_call(
        inner_kernel,
        in_specs=[vmem, vmem, hbm],
        out_specs=vmem,
        out_shape=half_conv,
        scratch_shapes=scratch,
        compiler_params=params(LIMIT),
        cost_estimate=cost(work / 2, moved),
        name="conv_inner",
    )(in_hbm(map_rows), in_hbm(features), in_hbm(weights))

    outer, stats, window = pl.pallas_call(
        outer_kernel,
        in_specs=[smem, smem, vmem, vmem, vmem, vmem, vmem, hbm],
        out_specs=[vmem, vmem, vmem],
        out_shape=[
            half_conv,
            jax.ShapeDtypeStruct((3, channels), F32),
            jax.ShapeDtypeStruct((rows + 2 * BLOCK, channels), BF16),
        ],
        scratch_shapes=scratch,
        compiler_params=params(LIMIT),
        cost_estimate=cost(work / 2, moved),
        name="conv_outer",
    )(occupancy, odd_flag, map_rows, features, even, other, inner, in_hbm(weights))

    stats = exchanged(stats, stacked_moments)

    block_out, sums = pl.pallas_call(
        norm_kernel,
        in_specs=[smem] + [vmem] * 10,
        out_shape=[
            jax.ShapeDtypeStruct((rows, channels), BF16),
            jax.ShapeDtypeStruct((2, channels), F32),
        ],
        compiler_params=params(LIMIT),
        cost_estimate=cost(rows * channels * 20, rows * channels * 10),
        name="norm",
    )(occupancy, inner, outer, gain, shift, cotangent, features, *stats)

    grads = exchanged(sums, jnp.add)

    core, lane, depth = me & 1, (me >> 1) & 1, (me >> 2) & 3
    place_one = (core * 8 + lane * 4 + depth).reshape(1)
    place_two = (core * 8 + depth * 2 + lane).reshape(1)
    piece_rows = channels // 16

    def gradient(kernel, count, in_specs, out_specs, out_shape, name):
        shape = (8, count, piece_rows, channels)
        return pl.pallas_call(
            kernel,
            in_specs=in_specs,
            out_specs=out_specs + [anywhere, anywhere],
            out_shape=out_shape
            + [jax.ShapeDtypeStruct(shape, F32), jax.ShapeDtypeStruct(shape, BF16)],
            scratch_shapes=[
                pltpu.VMEM((rows, BLOCK), jnp.int32),
                pltpu.VMEM((GROUP, rows, channels), BF16),
                pltpu.VMEM((GROUP, channels, channels), F32),
                pltpu.VMEM(shape, F32),
                pltpu.VMEM(shape, BF16),
                pltpu.SemaphoreType.DMA((2, count // GROUP)),
            ],
            compiler_params=params(LIMIT),
            cost_estimate=cost(work * count / K, count * channels * channels * 6),
            name=name,
        )

    grad_conv, sums, *pair_one = gradient(
        functools.partial(first_gradient_kernel, len(stats)),
        K_ONE,
        [smem, smem] + [vmem] * 15,
        [vmem, vmem],
        [
            jax.ShapeDtypeStruct((rows, channels), BF16),
            jax.ShapeDtypeStruct((2, channels), F32),
        ],
        "weight_gradient_one",
    )(
        occupancy, place_one, inner, outer, gain, shift, cotangent, map_rows, window,
        *stats, *grads,
    )
    one = [pair_one[0], swap(pair_one[1], 1)]
    pair_two = gradient(
        second_gradient_kernel, K - K_ONE, [smem] + [vmem] * 3, [], [], "weight_gradient_two"
    )(place_two, grad_conv, map_rows, window)
    two = [pair_two[0], swap(pair_two[1], 1)]

    weight_spec = pl.BlockSpec((GROUP, channels, channels), lambda s: (s, 0, 0))

    def push(grad_conv):
        return pl.pallas_call(
            push_kernel,
            grid=(groups,),
            in_specs=[full((rows, channels)), full((K, rows)), weight_spec],
            out_specs=[full((BLOCK, channels)), full((rows, channels)), full((BLOCK, channels))],
            out_shape=[
                jax.ShapeDtypeStruct((BLOCK, channels), BF16),
                jax.ShapeDtypeStruct((rows, channels), F32),
                jax.ShapeDtypeStruct((BLOCK, channels), BF16),
            ],
            scratch_shapes=[pltpu.VMEM((rows + 2 * BLOCK, channels), F32)],
            compiler_params=params(LIMIT),
            cost_estimate=cost(1000, 1000),
            name="push",
        )(grad_conv, map_rows, weights)

    def spread_gradient(sinks):
        sink_before, sink_own, sink_after = sinks
        return neighbours_swap(sink_before, sink_after), sink_own

    (own_one, own_two), ((even, other), sink_own) = summed_over_devices(
        one, two, grad_conv, push, spread_gradient
    )
    from_prev = jnp.where(odd == 1, even, other).astype(F32)
    from_next = jnp.where(odd == 1, other, even).astype(F32)
    occupied = occupied_rows(occupancy[0], rows)
    received = jnp.concatenate(
        [
            sink_own[:BLOCK] + from_prev,
            sink_own[BLOCK : rows - BLOCK],
            sink_own[rows - BLOCK :] + from_next,
        ],
        axis=0,
    )
    grad_features = (jnp.where(occupied, cotangent.astype(F32), 0.0) + received).astype(BF16)
    places = jnp.concatenate([place_one, place_two])

    def placed(other, sources, *into):
        return pl.pallas_call(
            functools.partial(place_kernel, other),
            in_specs=[smem, anywhere, anywhere] + [hbm] * len(into),
            out_specs=hbm,
            out_shape=jax.ShapeDtypeStruct(weights.shape, BF16),
            scratch_shapes=[pltpu.SemaphoreType.DMA((16,))],
            input_output_aliases={3: 0} if into else {},
            compiler_params=params(LIMIT),
            cost_estimate=cost(0, K * channels * channels * 2),
            name="place",
        )(places, *sources, *into)

    others = [swap(own_one, 1), swap(own_two, 1)]
    grad_weights = placed(1, others, placed(0, (own_one, own_two)))
    return block_out, grad_features, grad_weights, sums[0], sums[1]


def solution(mesh):
    in_specs = (
        P(("parts", "dp"), None),
        P(("parts", "dp"), None),
        P(("parts", "dp")),
        P(),
        P(),
        P(),
        P(("parts", "dp"), None),
    )
    out_specs = (
        P(("parts", "dp"), None),
        P(("parts", "dp"), None),
        P("parts", None, None),
        P("parts"),
        P("parts"),
    )
    return jax.shard_map(
        per_device, mesh=mesh, in_specs=in_specs, out_specs=out_specs, check_vma=False
    )
```

```python
import functools

import jax
import jax.numpy as jnp
from jax import lax
from jax.experimental import pallas as pl
from jax.experimental.pallas import tpu as pltpu
from jax.sharding import PartitionSpec as P

K = 27
BLOCK = 128
GROUP = 9
HALF = 13
K_ONE = 9
EPSILON = 1e-05
F32 = jnp.float32
BF16 = jnp.bfloat16
LIMIT = 24 * 1024 * 1024


def merged(merge, values):
    return merge(merge(values[0], values[1]), merge(values[2], values[3]))


def merged_moments(one, two):
    (sum_one, square_one, count_one), (sum_two, square_two, count_two) = one, two
    away = sum_one / count_one - sum_two / count_two
    count = count_one + count_two
    square = (square_one + square_two) + away * away * (count_one * count_two / count)
    return sum_one + sum_two, square, count


def dot(a, b, contract):
    return lax.dot_general(a, b, ((contract[0], contract[1]), ((), ())), preferred_element_type=F32)


def full(shape):
    return pl.BlockSpec(shape, lambda *_: (0,) * len(shape))


def params(limit):
    return pltpu.CompilerParams(vmem_limit_bytes=limit)


def cost(flops, moved):
    return pl.CostEstimate(flops=int(flops), bytes_accessed=int(moved), transcendentals=0)


def occupied_rows(filled, rows):
    position = lax.broadcasted_iota(jnp.int32, (rows, 1), 0)
    return (position < filled - BLOCK) | (position >= rows - BLOCK)


def chosen_slots(slot, slots):
    return jnp.where(slot == slots, 1.0, 0.0).astype(BF16)


def transposed_map(map_ref):
    spare = jnp.zeros((BLOCK - K, map_ref.shape[1]), jnp.int32)
    return jnp.transpose(jnp.concatenate([map_ref[...], spare], axis=0))


def convolve(map_ref, tiles, first_slots, weight_hbm, conv_ref, scratch):
    weight, picked, index, weight_sem = scratch
    groups = K // GROUP

    def fetch(g):
        here = pl.ds(g * GROUP, GROUP)
        return pltpu.make_async_copy(weight_hbm.at[here], weight.at[here], weight_sem.at[g])

    for g in range(groups):
        fetch(g).start()
    index[...] = transposed_map(map_ref)
    conv_ref[...] = jnp.zeros_like(conv_ref)
    slots = lax.broadcasted_iota(jnp.int32, (BLOCK, 3 * BLOCK), 1)

    def group(g, carry):
        local = pltpu.roll(index[...], lax.rem(BLOCK - g * GROUP, BLOCK), 1)
        for b, tile in enumerate(tiles):
            here = slice(b * BLOCK, (b + 1) * BLOCK)
            slot = local[here] - first_slots[b]
            for j in range(GROUP):
                chosen = chosen_slots(slot[:, j : j + 1], slots)
                picked[j, here, :] = dot(chosen, tile[...], ((1,), (0,))).astype(BF16)
        fetch(g).wait()
        total = conv_ref[...]
        for j in range(GROUP):
            total = total + dot(picked[j], weight[g * GROUP + j], ((1,), (0,)))
        conv_ref[...] = total
        return carry

    lax.fori_loop(0, groups, group, 0)


def inner_kernel(map_ref, own_ref, weight_hbm, conv_ref, chosen_map, *scratch):
    rows = own_ref.shape[0]
    chosen_map[...] = map_ref[:, BLOCK : rows - BLOCK]
    blocks = range(1, rows // BLOCK - 1)
    tiles = [own_ref.at[(b - 1) * BLOCK : (b + 2) * BLOCK] for b in blocks]
    first_slots = [rows - BLOCK + b * BLOCK for b in blocks]
    convolve(chosen_map, tiles, first_slots, weight_hbm, conv_ref, scratch)


def outer_kernel(
    filled_ref, odd_ref, map_ref, own_ref, even_ref, other_ref, inner_ref, weight_hbm,
    conv_ref, stats_ref, window_ref, chosen_map, *scratch,
):
    rows = own_ref.shape[0]
    odd = odd_ref[0] == 1
    window_ref[0:BLOCK, :] = jnp.where(odd, even_ref[...], other_ref[...])
    window_ref[BLOCK : rows + BLOCK, :] = own_ref[...]
    window_ref[rows + BLOCK :, :] = jnp.where(odd, other_ref[...], even_ref[...])
    chosen_map[:, 0:BLOCK] = map_ref[:, 0:BLOCK]
    chosen_map[:, BLOCK:] = map_ref[:, rows - BLOCK :]
    tiles = [window_ref.at[0 : 3 * BLOCK], window_ref.at[rows - BLOCK :]]
    first_slots = [rows - BLOCK, 2 * rows - 2 * BLOCK]
    convolve(chosen_map, tiles, first_slots, weight_hbm, conv_ref, scratch)
    filled = filled_ref[0]
    count = filled.astype(F32)
    conv = whole(inner_ref, conv_ref)
    occupied = occupied_rows(filled, rows)
    sums = jnp.sum(jnp.where(occupied, conv, 0.0), axis=0, keepdims=True)
    off = jnp.where(occupied, conv - sums / count, 0.0)
    squares = jnp.sum(off * off, axis=0, keepdims=True)
    stats_ref[...] = jnp.concatenate([sums, squares, jnp.full_like(sums, count)], axis=0)


def whole(inner_ref, outer_ref):
    return jnp.concatenate([outer_ref[0:BLOCK, :], inner_ref[...], outer_ref[BLOCK:, :]], axis=0)


def normalised(filled, inner_ref, outer_ref, stats_refs, gain_ref, shift_ref, cotangent_ref):
    conv = whole(inner_ref, outer_ref)
    sums, squares, total = merged(
        merged_moments, [[ref[i : i + 1, :] for i in range(3)] for ref in stats_refs]
    )
    center = sums / total
    inverse = lax.rsqrt(squares / total + EPSILON)
    occupied = occupied_rows(filled, conv.shape[0])
    normed = (conv - center) * inverse
    affine = gain_ref[...] * normed + shift_ref[...]
    upstream = jnp.where(occupied & (affine > 0.0), cotangent_ref[...].astype(F32), 0.0)
    return occupied, normed, affine, upstream, inverse, total


def norm_kernel(
    filled_ref, inner_ref, outer_ref, gain_ref, shift_ref, cotangent_ref, feature_ref, *refs
):
    *stats_refs, out_ref, sums_ref = refs
    occupied, normed, affine, upstream, _, _ = normalised(
        filled_ref[0], inner_ref, outer_ref, stats_refs, gain_ref, shift_ref, cotangent_ref
    )
    out = jnp.maximum(affine, 0.0) + feature_ref[...].astype(F32)
    out_ref[...] = jnp.where(occupied, out, 0.0).astype(BF16)
    sums_ref[...] = jnp.concatenate(
        [jnp.sum(upstream * normed, axis=0, keepdims=True), jnp.sum(upstream, axis=0, keepdims=True)],
        axis=0,
    )


def grad_conv_kernel(
    parts, filled_ref, inner_ref, outer_ref, gain_ref, shift_ref, cotangent_ref, *refs
):
    stats_refs, grads_refs, (grad_ref, sums_ref) = refs[:parts], refs[parts:-2], refs[-2:]
    occupied, normed, _, upstream, inverse, total = normalised(
        filled_ref[0], inner_ref, outer_ref, stats_refs, gain_ref, shift_ref, cotangent_ref
    )
    sums = merged(jnp.add, [ref[...] for ref in grads_refs])
    sums_ref[...] = sums
    grad_conv = gain_ref[...] * inverse * (
        upstream - sums[1:2, :] / total - normed * sums[0:1, :] / total
    )
    grad_ref[...] = jnp.where(occupied, grad_conv, 0.0).astype(BF16)


def gradient_kernel(
    place_ref, grad_own, grad_mate, map_own, map_mate, window_own, window_mate, *refs
):
    outs, scratch = refs[:6], refs[6:]
    index, picked, grad, product, *staged, out_sem = scratch
    keep_one, send_one, keep_two, *sends_two = staged
    rows, channels = grad_own.shape
    core = place_ref[0]
    slots = lax.broadcasted_iota(jnp.int32, (BLOCK, 3 * BLOCK), 1)
    sides = ((map_own, window_own), (map_mate, window_mate))
    grad[0:rows, :] = grad_own[...]
    grad[rows:, :] = grad_mate[...]
    for side, (map_ref, _) in enumerate(sides):
        index[side] = transposed_map(map_ref)

    def gradient(j, slot_of):
        for side, (_, window) in enumerate(sides):
            for b in range(rows // BLOCK):
                here = slice(b * BLOCK, (b + 1) * BLOCK)
                chosen = chosen_slots(slot_of(side)[here] - (rows + (b - 1) * BLOCK), slots)
                tile = window[b * BLOCK : (b + 3) * BLOCK, :]
                at = slice(side * rows + b * BLOCK, side * rows + (b + 1) * BLOCK)
                picked[j, at, :] = dot(chosen, tile, ((1,), (0,))).astype(BF16)
        product[j] = dot(picked[j], grad[...], ((0,), (0,)))

    def stored(staged, out, n):
        return pltpu.make_async_copy(staged, out, out_sem.at[n])

    shift = lax.rem(BLOCK - core * (HALF + 1), BLOCK)
    local = [pltpu.roll(index[side], shift, 1) for side in range(2)]
    size = channels // 8

    def rows_of(piece, place, size, first):
        at = lax.bitwise_xor(jnp.int32(piece), place) * size + first
        return pl.ds(pl.multiple_of(at, 16), size)

    for j in range(K_ONE):
        gradient(j, lambda side: local[side][:, j : j + 1])
        here = slice(j * size, (j + 1) * size)
        for piece in range(8):
            value = product[j, rows_of(piece, place_ref[1], size, 0), :]
            if piece < 4:
                keep_one[piece, here, :] = value
            else:
                send_one[piece - 4, here, :] = value.astype(BF16)
    copies = [stored(keep_one, outs[0], 0), stored(send_one, outs[1], 1)]
    for copy in copies:
        copy.start()
    for j in range(HALF - K_ONE + 1):
        whole_offset = j < HALF - K_ONE
        if whole_offset:
            gradient(j, lambda side: local[side][:, K_ONE + j : K_ONE + j + 1])
        else:
            gradient(j, lambda side: index[side][:, HALF : HALF + 1])
        count = size if whole_offset else size // 2
        first = 0 if whole_offset else core * (channels // 2)
        here = slice(j * size, j * size + count)
        for piece in range(8):
            value = product[j, rows_of(piece, place_ref[2], count, first), :]
            if piece < 2:
                keep_two[piece, here, :] = value
            else:
                sends_two[piece // 2 - 1][piece % 2, here, :] = value.astype(BF16)
    late = [stored(keep_two, outs[2], 2)]
    late += [stored(sends_two[n], outs[3 + n], 3 + n) for n in range(3)]
    for copy in late:
        copy.start()
    for copy in copies + late:
        copy.wait()


def push_kernel(grad_ref, index_ref, weight_ref, before_ref, own_ref, after_ref, sink):
    step = pl.program_id(0)

    @pl.when(step == 0)
    def _():
        sink[...] = jnp.zeros_like(sink)

    blocks = grad_ref.shape[0] // BLOCK
    here = jnp.concatenate([index_ref[step * GROUP + j, :][None] for j in range(GROUP)], axis=0)
    block_of = lax.broadcasted_iota(jnp.int32, here.shape, 1) // BLOCK
    local = here - (3 + block_of) * BLOCK
    slots = lax.broadcasted_iota(jnp.int32, (3 * BLOCK, BLOCK), 0)
    pushed = [
        dot(grad_ref[...], weight_ref[j], ((1,), (1,))).astype(BF16) for j in range(GROUP)
    ]
    for b in range(blocks):
        rows = slice(b * BLOCK, (b + 1) * BLOCK)
        chosen = jnp.concatenate(
            [
                jnp.where(local[j : j + 1, rows] == slots, 1.0, 0.0).astype(BF16)
                for j in range(GROUP)
            ],
            axis=1,
        )
        stacked = jnp.concatenate([pushed[j][rows] for j in range(GROUP)], axis=0)
        window = slice(b * BLOCK, (b + 3) * BLOCK)
        sink[window, :] = sink[window, :] + dot(chosen, stacked, ((1,), (0,)))

    @pl.when(step == pl.num_programs(0) - 1)
    def _():
        before_ref[...] = sink[0:BLOCK, :].astype(BF16)
        own_ref[...] = sink[BLOCK : (blocks + 1) * BLOCK, :]
        after_ref[...] = sink[(blocks + 1) * BLOCK :, :].astype(BF16)


def place_kernel(other, places_ref, one, two, *refs):
    out_ref, sems = refs[-2:]
    core = lax.bitwise_xor(places_ref[0], jnp.int32(other))
    first = core * (HALF + 1)
    size = out_ref.shape[1] // 8
    copies = []

    def put(source, out, part, piece, count, base):
        at = lax.bitwise_xor(jnp.int32(piece), places_ref[part]) * count + base
        here = pl.ds(pl.multiple_of(at, 16), count)
        copies.append(pltpu.make_async_copy(source, out.at[:, here, :], sems.at[len(copies)]))

    for piece in range(8):
        put(one.at[piece], out_ref.at[pl.ds(first, K_ONE)], 1, piece, size, 0)
        for j in range(HALF - K_ONE):
            source = two.at[pl.ds(piece, 1), pl.ds(j * size, size)]
            put(source, out_ref.at[pl.ds(first + K_ONE + j, 1)], 2, piece, size, 0)
        source = two.at[pl.ds(piece, 1), pl.ds((HALF - K_ONE) * size, size // 2)]
        base = core * (out_ref.shape[1] // 2)
        put(source, out_ref.at[pl.ds(HALF, 1)], 2, piece, size // 2, base)
    for copy in copies:
        copy.start()
    for copy in copies:
        copy.wait()


def swap(value, by):
    peers = lax.axis_size("dp")
    return lax.ppermute(value, "dp", [(i, i ^ by) for i in range(peers)])


STAGES = {"c": (1,), "x": (2,), "z": (4, 8, 12)}


def part(terms, first, size):
    return functools.reduce(
        jnp.add, [term[first : first + size].astype(F32) for term in terms]
    )


def split(terms, stage):
    partners = STAGES[stage]
    size = terms[0].shape[0] // (len(partners) + 1)
    sends = [part(terms, (i + 1) * size, size).astype(BF16) for i in range(len(partners))]
    return part(terms, 0, size), sends


def swapped(sends, stage):
    return [swap(send, by) for send, by in zip(sends, STAGES[stage])]


def gather_start(piece, stage):
    return [swap(piece, by) for by in STAGES[stage]]


def summed_over_devices(one, two, grad_conv, push, spread):
    parts, grad_conv = lax.optimization_barrier(((one, two), grad_conv))
    received = [swapped(sends, stage) for (_, sends), stage in zip(parts, "xz")]
    received, sinks = lax.optimization_barrier((received, push(grad_conv)))
    parts = [
        split([kept] + got, stage) for (kept, _), got, stage in zip(parts, received, "zx")
    ]
    parts, sinks = lax.optimization_barrier((parts, sinks))
    received = [swapped(sends, stage) for (_, sends), stage in zip(parts, "zx")]
    halo = spread(sinks)
    received, halo = lax.optimization_barrier((received, halo))
    pieces = [part([kept] + got, 0, 1) for (kept, _), got in zip(parts, received)]
    by = 16
    while by < lax.axis_size("dp"):
        pieces = [piece + swap(piece, by) for piece in pieces]
        by *= 2
    pieces = [piece.astype(BF16) for piece in pieces]
    for stages in ("zx", "xz"):
        received = [gather_start(piece, stage) for piece, stage in zip(pieces, stages)]
        received, pieces = lax.optimization_barrier((received, pieces))
        pieces = [
            jnp.concatenate([piece] + got, axis=0) for piece, got in zip(pieces, received)
        ]
    return pieces, halo


def exchanged(value, merge):
    received = [swap(value, by) for by in (1, 2, 3)]
    value = merged(merge, [value] + received)
    by = 16
    while by < lax.axis_size("dp"):
        value = merge(value, swap(value, by))
        by *= 2
    return [value] + [swap(value, by) for by in (4, 8, 12)]


def stacked_moments(one, two):
    return jnp.stack(merged_moments(one, two))


def per_device(features, kernel_map, occupancy, weights, bn_gain, bn_shift, cotangent):
    rows, channels = features.shape
    peers = lax.axis_size("dp")
    me = lax.axis_index("dp")
    blocks = rows // BLOCK
    inner_rows = rows - 2 * BLOCK
    steps = K // GROUP

    odd = me & 1
    even_pairs = [(i, i ^ 1) for i in range(peers)]
    other_pairs = [(i, ((i + 1) ^ 1) - 1) for i in range(1, peers - 1)]

    def neighbours_swap(to_before, to_after):
        even = lax.ppermute(jnp.where(odd == 1, to_before, to_after), "dp", even_pairs)
        other = lax.ppermute(jnp.where(odd == 1, to_after, to_before), "dp", other_pairs)
        return even, other

    even, other = neighbours_swap(features[:BLOCK], features[rows - BLOCK :])
    map_rows = jnp.transpose(kernel_map)
    map_mate = swap(map_rows, 1)
    odd_flag = odd.reshape(1)

    gain = bn_gain.reshape(1, channels)
    shift = bn_shift.reshape(1, channels)
    smem = pl.BlockSpec(memory_space=pltpu.SMEM)
    vmem = pl.BlockSpec(memory_space=pltpu.VMEM)
    hbm = pl.BlockSpec(memory_space=pltpu.HBM)
    anywhere = pl.BlockSpec(memory_space=pl.ANY)
    groups = K // GROUP
    work = K * rows * channels * 2 * (3 * BLOCK + channels)
    moved = K * channels * channels * 2 * 3

    half_conv = jax.ShapeDtypeStruct((2 * BLOCK, channels), F32)
    scratch = [
        pltpu.VMEM((K, 2 * BLOCK), jnp.int32),
        pltpu.VMEM((K, channels, channels), BF16),
        pltpu.VMEM((GROUP, 2 * BLOCK, channels), BF16),
        pltpu.VMEM((2 * BLOCK, BLOCK), jnp.int32),
        pltpu.SemaphoreType.DMA((groups,)),
    ]

    def in_hbm(value):
        return pltpu.with_memory_space_constraint(value, pltpu.HBM)

    inner = pl.pallas_call(
        inner_kernel,
        in_specs=[vmem, vmem, hbm],
        out_specs=vmem,
        out_shape=half_conv,
        scratch_shapes=scratch,
        compiler_params=params(LIMIT),
        cost_estimate=cost(work / 2, moved),
        name="conv_inner",
    )(in_hbm(map_rows), in_hbm(features), in_hbm(weights))

    outer, stats, window = pl.pallas_call(
        outer_kernel,
        in_specs=[smem, smem, vmem, vmem, vmem, vmem, vmem, hbm],
        out_specs=[vmem, vmem, vmem],
        out_shape=[
            half_conv,
            jax.ShapeDtypeStruct((3, channels), F32),
            jax.ShapeDtypeStruct((rows + 2 * BLOCK, channels), BF16),
        ],
        scratch_shapes=scratch,
        compiler_params=params(LIMIT),
        cost_estimate=cost(work / 2, moved),
        name="conv_outer",
    )(occupancy, odd_flag, map_rows, features, even, other, inner, in_hbm(weights))

    window_mate = swap(window, 1)
    stats = exchanged(stats, stacked_moments)

    block_out, sums = pl.pallas_call(
        norm_kernel,
        in_specs=[smem] + [vmem] * 10,
        out_shape=[
            jax.ShapeDtypeStruct((rows, channels), BF16),
            jax.ShapeDtypeStruct((2, channels), F32),
        ],
        compiler_params=params(LIMIT),
        cost_estimate=cost(rows * channels * 20, rows * channels * 10),
        name="norm",
    )(occupancy, inner, outer, gain, shift, cotangent, features, *stats)

    grads = exchanged(sums, jnp.add)

    grad_conv, sums = pl.pallas_call(
        functools.partial(grad_conv_kernel, len(stats)),
        in_specs=[smem] + [vmem] * 13,
        out_shape=[
            jax.ShapeDtypeStruct((rows, channels), BF16),
            jax.ShapeDtypeStruct((2, channels), F32),
        ],
        compiler_params=params(LIMIT),
        cost_estimate=cost(rows * channels * 20, rows * channels * 8),
        name="grad_conv",
    )(occupancy, inner, outer, gain, shift, cotangent, *stats, *grads)
    grad_mate = swap(grad_conv, 1)

    core, lane, depth = me & 1, (me >> 1) & 1, (me >> 2) & 3
    places = jnp.stack([core, lane * 4 + depth, depth * 2 + lane])
    size = channels // 8
    rows_one, rows_two = K_ONE * size, (HALF - K_ONE) * size + size // 2
    shapes = [((4, rows_one, channels), F32), ((4, rows_one, channels), BF16)]
    shapes += [((2, rows_two, channels), F32)] + [((2, rows_two, channels), BF16)] * 3
    keep_one, send_one, keep_two, *sends_two = pl.pallas_call(
        gradient_kernel,
        in_specs=[smem] + [vmem] * 6,
        out_specs=[anywhere] * 6,
        out_shape=[jax.ShapeDtypeStruct(*shape) for shape in shapes],
        scratch_shapes=[
            pltpu.VMEM((2, rows, BLOCK), jnp.int32),
            pltpu.VMEM((K_ONE, 2 * rows, channels), BF16),
            pltpu.VMEM((2 * rows, channels), BF16),
            pltpu.VMEM((K_ONE, channels, channels), F32),
        ]
        + [pltpu.VMEM(*shape) for shape in shapes]
        + [pltpu.SemaphoreType.DMA((6,))],
        compiler_params=params(LIMIT),
        cost_estimate=cost(work, K * channels * channels * 6),
        name="weight_gradient",
    )(places, grad_conv, grad_mate, map_rows, map_mate, window, window_mate)
    one, two = (keep_one, [send_one]), (keep_two, sends_two)

    weight_spec = pl.BlockSpec((GROUP, channels, channels), lambda s: (s, 0, 0))

    def push(grad_conv):
        return pl.pallas_call(
            push_kernel,
            grid=(groups,),
            in_specs=[full((rows, channels)), full((K, rows)), weight_spec],
            out_specs=[full((BLOCK, channels)), full((rows, channels)), full((BLOCK, channels))],
            out_shape=[
                jax.ShapeDtypeStruct((BLOCK, channels), BF16),
                jax.ShapeDtypeStruct((rows, channels), F32),
                jax.ShapeDtypeStruct((BLOCK, channels), BF16),
            ],
            scratch_shapes=[pltpu.VMEM((rows + 2 * BLOCK, channels), F32)],
            compiler_params=params(LIMIT),
            cost_estimate=cost(1000, 1000),
            name="push",
        )(grad_conv, map_rows, weights)

    def spread_gradient(sinks):
        sink_before, sink_own, sink_after = sinks
        return neighbours_swap(sink_before, sink_after), sink_own

    (own_one, own_two), ((even, other), sink_own) = summed_over_devices(
        one, two, grad_conv, push, spread_gradient
    )
    from_prev = jnp.where(odd == 1, even, other).astype(F32)
    from_next = jnp.where(odd == 1, other, even).astype(F32)
    occupied = occupied_rows(occupancy[0], rows)
    received = jnp.concatenate(
        [
            sink_own[:BLOCK] + from_prev,
            sink_own[BLOCK : rows - BLOCK],
            sink_own[rows - BLOCK :] + from_next,
        ],
        axis=0,
    )
    grad_features = (jnp.where(occupied, cotangent.astype(F32), 0.0) + received).astype(BF16)

    def placed(other, sources, *into):
        return pl.pallas_call(
            functools.partial(place_kernel, other),
            in_specs=[smem, anywhere, anywhere] + [hbm] * len(into),
            out_specs=hbm,
            out_shape=jax.ShapeDtypeStruct(weights.shape, BF16),
            scratch_shapes=[pltpu.SemaphoreType.DMA((8 * (HALF - K_ONE + 2),))],
            input_output_aliases={3: 0} if into else {},
            compiler_params=params(LIMIT),
            cost_estimate=cost(0, K * channels * channels * 2),
            name="place",
        )(places, sources[0].reshape(8, K_ONE, size, channels), sources[1], *into)

    others = [swap(own_one, 1), swap(own_two, 1)]
    grad_weights = placed(1, others, placed(0, (own_one, own_two)))
    return block_out, grad_features, grad_weights, sums[0], sums[1]


def solution(mesh):
    in_specs = (
        P(("parts", "dp"), None),
        P(("parts", "dp"), None),
        P(("parts", "dp")),
        P(),
        P(),
        P(),
        P(("parts", "dp"), None),
    )
    out_specs = (
        P(("parts", "dp"), None),
        P(("parts", "dp"), None),
        P("parts", None, None),
        P("parts"),
        P("parts"),
    )
    return jax.shard_map(
        per_device, mesh=mesh, in_specs=in_specs, out_specs=out_specs, check_vma=False
    )
```

```python
import functools

import jax
import jax.numpy as jnp
from jax import lax
from jax.experimental import pallas as pl
from jax.experimental.pallas import tpu as pltpu
from jax.sharding import PartitionSpec as P

K = 27
BLOCK = 128
GROUP = 9
HALF = 13
K_ONE = 9
EPSILON = 1e-05
F32 = jnp.float32
BF16 = jnp.bfloat16
LIMIT = 24 * 1024 * 1024


def merged(merge, values):
    return merge(merge(values[0], values[1]), merge(values[2], values[3]))


def merged_moments(one, two):
    (sum_one, square_one, count_one), (sum_two, square_two, count_two) = one, two
    away = sum_one / count_one - sum_two / count_two
    count = count_one + count_two
    square = (square_one + square_two) + away * away * (count_one * count_two / count)
    return sum_one + sum_two, square, count


def dot(a, b, contract):
    return lax.dot_general(a, b, ((contract[0], contract[1]), ((), ())), preferred_element_type=F32)


def full(shape):
    return pl.BlockSpec(shape, lambda *_: (0,) * len(shape))


def params(limit):
    return pltpu.CompilerParams(vmem_limit_bytes=limit)


def cost(flops, moved):
    return pl.CostEstimate(flops=int(flops), bytes_accessed=int(moved), transcendentals=0)


def occupied_rows(filled, rows):
    position = lax.broadcasted_iota(jnp.int32, (rows, 1), 0)
    return (position < filled - BLOCK) | (position >= rows - BLOCK)


def chosen_slots(slot, slots):
    return jnp.where(slot == slots, 1.0, 0.0).astype(BF16)


def transposed_map(map_ref):
    spare = jnp.zeros((BLOCK - K, map_ref.shape[1]), jnp.int32)
    return jnp.transpose(jnp.concatenate([map_ref[...], spare], axis=0))


def convolve(map_ref, tiles, first_slots, weight_hbm, conv_ref, scratch):
    weight, picked, index, weight_sem = scratch
    groups = K // GROUP

    def fetch(g):
        here = pl.ds(g * GROUP, GROUP)
        return pltpu.make_async_copy(weight_hbm.at[here], weight.at[here], weight_sem.at[g])

    for g in range(groups):
        fetch(g).start()
    index[...] = transposed_map(map_ref)
    conv_ref[...] = jnp.zeros_like(conv_ref)
    slots = lax.broadcasted_iota(jnp.int32, (BLOCK, 3 * BLOCK), 1)

    def group(g, carry):
        local = pltpu.roll(index[...], lax.rem(BLOCK - g * GROUP, BLOCK), 1)
        for b, tile in enumerate(tiles):
            here = slice(b * BLOCK, (b + 1) * BLOCK)
            slot = local[here] - first_slots[b]
            for j in range(GROUP):
                chosen = chosen_slots(slot[:, j : j + 1], slots)
                picked[j, here, :] = dot(chosen, tile[...], ((1,), (0,))).astype(BF16)
        fetch(g).wait()
        total = conv_ref[...]
        for j in range(GROUP):
            total = total + dot(picked[j], weight[g * GROUP + j], ((1,), (0,)))
        conv_ref[...] = total
        return carry

    lax.fori_loop(0, groups, group, 0)


def inner_kernel(map_ref, own_ref, weight_hbm, conv_ref, chosen_map, *scratch):
    rows = own_ref.shape[0]
    chosen_map[...] = map_ref[:, BLOCK : rows - BLOCK]
    blocks = range(1, rows // BLOCK - 1)
    tiles = [own_ref.at[(b - 1) * BLOCK : (b + 2) * BLOCK] for b in blocks]
    first_slots = [rows - BLOCK + b * BLOCK for b in blocks]
    convolve(chosen_map, tiles, first_slots, weight_hbm, conv_ref, scratch)


def outer_kernel(
    filled_ref, odd_ref, map_ref, own_ref, even_ref, other_ref, inner_ref, weight_hbm,
    conv_ref, stats_ref, window_ref, chosen_map, *scratch,
):
    rows = own_ref.shape[0]
    odd = odd_ref[0] == 1
    window_ref[0:BLOCK, :] = jnp.where(odd, even_ref[...], other_ref[...])
    window_ref[BLOCK : rows + BLOCK, :] = own_ref[...]
    window_ref[rows + BLOCK :, :] = jnp.where(odd, other_ref[...], even_ref[...])
    chosen_map[:, 0:BLOCK] = map_ref[:, 0:BLOCK]
    chosen_map[:, BLOCK:] = map_ref[:, rows - BLOCK :]
    tiles = [window_ref.at[0 : 3 * BLOCK], window_ref.at[rows - BLOCK :]]
    first_slots = [rows - BLOCK, 2 * rows - 2 * BLOCK]
    convolve(chosen_map, tiles, first_slots, weight_hbm, conv_ref, scratch)
    filled = filled_ref[0]
    count = filled.astype(F32)
    conv = whole(inner_ref, conv_ref)
    occupied = occupied_rows(filled, rows)
    sums = jnp.sum(jnp.where(occupied, conv, 0.0), axis=0, keepdims=True)
    off = jnp.where(occupied, conv - sums / count, 0.0)
    squares = jnp.sum(off * off, axis=0, keepdims=True)
    stats_ref[...] = jnp.concatenate([sums, squares, jnp.full_like(sums, count)], axis=0)


def whole(inner_ref, outer_ref):
    return jnp.concatenate([outer_ref[0:BLOCK, :], inner_ref[...], outer_ref[BLOCK:, :]], axis=0)


def normalised(filled, inner_ref, outer_ref, stats_refs, gain_ref, shift_ref, cotangent_ref):
    conv = whole(inner_ref, outer_ref)
    sums, squares, total = merged(
        merged_moments, [[ref[i : i + 1, :] for i in range(3)] for ref in stats_refs]
    )
    center = sums / total
    inverse = lax.rsqrt(squares / total + EPSILON)
    occupied = occupied_rows(filled, conv.shape[0])
    normed = (conv - center) * inverse
    affine = gain_ref[...] * normed + shift_ref[...]
    upstream = jnp.where(occupied & (affine > 0.0), cotangent_ref[...].astype(F32), 0.0)
    return occupied, normed, affine, upstream, inverse, total


def norm_kernel(
    filled_ref, inner_ref, outer_ref, gain_ref, shift_ref, cotangent_ref, feature_ref, *refs
):
    *stats_refs, out_ref, sums_ref = refs
    occupied, normed, affine, upstream, _, _ = normalised(
        filled_ref[0], inner_ref, outer_ref, stats_refs, gain_ref, shift_ref, cotangent_ref
    )
    out = jnp.maximum(affine, 0.0) + feature_ref[...].astype(F32)
    out_ref[...] = jnp.where(occupied, out, 0.0).astype(BF16)
    sums_ref[...] = jnp.concatenate(
        [jnp.sum(upstream * normed, axis=0, keepdims=True), jnp.sum(upstream, axis=0, keepdims=True)],
        axis=0,
    )


def grad_conv_kernel(
    parts, filled_ref, inner_ref, outer_ref, gain_ref, shift_ref, cotangent_ref, *refs
):
    stats_refs, grads_refs, (grad_ref, sums_ref) = refs[:parts], refs[parts:-2], refs[-2:]
    occupied, normed, _, upstream, inverse, total = normalised(
        filled_ref[0], inner_ref, outer_ref, stats_refs, gain_ref, shift_ref, cotangent_ref
    )
    sums = merged(jnp.add, [ref[...] for ref in grads_refs])
    sums_ref[...] = sums
    grad_conv = gain_ref[...] * inverse * (
        upstream - sums[1:2, :] / total - normed * sums[0:1, :] / total
    )
    grad_ref[...] = jnp.where(occupied, grad_conv, 0.0).astype(BF16)


def gradient_kernel(
    place_ref, grad_own, grad_mate, map_own, map_mate, window_own, window_mate, *refs
):
    outs, scratch = refs[:6], refs[6:]
    index, picked, grad, product, *staged, out_sem = scratch
    keep_one, send_one, keep_two, *sends_two = staged
    rows, channels = grad_own.shape
    core = place_ref[0]
    slots = lax.broadcasted_iota(jnp.int32, (BLOCK, 3 * BLOCK), 1)
    sides = ((map_own, window_own), (map_mate, window_mate))
    grad[0:rows, :] = grad_own[...]
    grad[rows:, :] = grad_mate[...]
    for side, (map_ref, _) in enumerate(sides):
        index[side] = transposed_map(map_ref)

    def gradient(j, slot_of):
        for side, (_, window) in enumerate(sides):
            for b in range(rows // BLOCK):
                here = slice(b * BLOCK, (b + 1) * BLOCK)
                chosen = chosen_slots(slot_of(side)[here] - (rows + (b - 1) * BLOCK), slots)
                tile = window[b * BLOCK : (b + 3) * BLOCK, :]
                at = slice(side * rows + b * BLOCK, side * rows + (b + 1) * BLOCK)
                picked[j, at, :] = dot(chosen, tile, ((1,), (0,))).astype(BF16)
        product[j] = dot(picked[j], grad[...], ((0,), (0,)))

    def stored(staged, out, n):
        return pltpu.make_async_copy(staged, out, out_sem.at[n])

    shift = lax.rem(BLOCK - core * (HALF + 1), BLOCK)
    local = [pltpu.roll(index[side], shift, 1) for side in range(2)]
    size = channels // 8

    def rows_of(piece, place, size, first):
        at = lax.bitwise_xor(jnp.int32(piece), place) * size + first
        return pl.ds(pl.multiple_of(at, 16), size)

    for j in range(K_ONE):
        gradient(j, lambda side: local[side][:, j : j + 1])
        here = slice(j * size, (j + 1) * size)
        for piece in range(8):
            value = product[j, rows_of(piece, place_ref[1], size, 0), :]
            if piece < 4:
                keep_one[piece, here, :] = value
            else:
                send_one[piece - 4, here, :] = value.astype(BF16)
    copies = [stored(keep_one, outs[0], 0), stored(send_one, outs[1], 1)]
    for copy in copies:
        copy.start()
    for j in range(HALF - K_ONE + 1):
        whole_offset = j < HALF - K_ONE
        if whole_offset:
            gradient(j, lambda side: local[side][:, K_ONE + j : K_ONE + j + 1])
        else:
            gradient(j, lambda side: index[side][:, HALF : HALF + 1])
        count = size if whole_offset else size // 2
        first = 0 if whole_offset else core * (channels // 2)
        here = slice(j * size, j * size + count)
        for piece in range(8):
            value = product[j, rows_of(piece, place_ref[2], count, first), :]
            if piece < 2:
                keep_two[piece, here, :] = value
            else:
                sends_two[piece // 2 - 1][piece % 2, here, :] = value.astype(BF16)
    late = [stored(keep_two, outs[2], 2)]
    late += [stored(sends_two[n], outs[3 + n], 3 + n) for n in range(3)]
    for copy in late:
        copy.start()
    for copy in copies + late:
        copy.wait()


def scatter(step, grad_ref, first_row, map_ref, weight_ref, windows):
    pushed = [dot(grad_ref[...], weight_ref[j], ((1,), (1,))).astype(BF16) for j in range(GROUP)]
    named = [map_ref[step * GROUP + j, :][None] for j in range(GROUP)]
    for b, first_slot, sink in windows:
        rows = slice(b * BLOCK, (b + 1) * BLOCK)
        at = slice(first_row(b), first_row(b) + BLOCK)
        slots = lax.broadcasted_iota(jnp.int32, (sink.shape[0], BLOCK), 0) + first_slot
        chosen = jnp.concatenate(
            [chosen_slots(named[j][:, at], slots) for j in range(GROUP)],
            axis=1,
        )
        stacked = jnp.concatenate([pushed[j][rows] for j in range(GROUP)], axis=0)
        sink[...] = sink[...] + dot(chosen, stacked, ((1,), (0,)))


def edge_push_kernel(grad_ref, map_ref, weight_ref, before_ref, after_ref, before, after):
    step = pl.program_id(0)
    rows = map_ref.shape[1]

    @pl.when(step == 0)
    def _():
        before[...] = jnp.zeros_like(before)
        after[...] = jnp.zeros_like(after)

    def first_row(b):
        return b * (rows - BLOCK)

    windows = [(0, rows - BLOCK, before), (1, 2 * rows, after)]
    scatter(step, grad_ref, first_row, map_ref, weight_ref, windows)

    @pl.when(step == pl.num_programs(0) - 1)
    def _():
        before_ref[...] = before[...].astype(BF16)
        after_ref[...] = after[...].astype(BF16)


def push_kernel(grad_ref, map_ref, weight_ref, own_ref):
    step = pl.program_id(0)
    rows = map_ref.shape[1]

    @pl.when(step == 0)
    def _():
        own_ref[...] = jnp.zeros_like(own_ref)

    windows = []
    for b in range(rows // BLOCK):
        start, stop = max(b - 1, 0) * BLOCK, min((b + 2) * BLOCK, rows)
        windows.append((b, rows + start, own_ref.at[start:stop]))
    scatter(step, grad_ref, lambda b: b * BLOCK, map_ref, weight_ref, windows)


def place_kernel(layout, places_ref, *refs):
    out_ref, sems = refs[-2:]
    size = out_ref.shape[1] // 8
    copies = []

    def put(source, out, part, piece, count, base):
        at = lax.bitwise_xor(jnp.int32(piece), places_ref[part]) * count + base
        here = pl.ds(pl.multiple_of(at, 16), count)
        copies.append(pltpu.make_async_copy(source, out.at[:, here, :], sems.at[len(copies)]))

    for n, (other, first_one, first_two) in enumerate(layout):
        one, two = refs[2 * n : 2 * n + 2]
        core = lax.bitwise_xor(places_ref[0], jnp.int32(other))
        first = core * (HALF + 1)
        for i in range(one.shape[0]):
            put(one.at[i], out_ref.at[pl.ds(first, K_ONE)], 1, first_one + i, size, 0)
        for i in range(two.shape[0]):
            piece = first_two + i
            for j in range(HALF - K_ONE):
                source = two.at[pl.ds(i, 1), pl.ds(j * size, size)]
                put(source, out_ref.at[pl.ds(first + K_ONE + j, 1)], 2, piece, size, 0)
            source = two.at[pl.ds(i, 1), pl.ds((HALF - K_ONE) * size, size // 2)]
            base = core * (out_ref.shape[1] // 2)
            put(source, out_ref.at[pl.ds(HALF, 1)], 2, piece, size // 2, base)
    for copy in copies:
        copy.start()
    for copy in copies:
        copy.wait()


def swap(value, by):
    peers = lax.axis_size("dp")
    return lax.ppermute(value, "dp", [(i, i ^ by) for i in range(peers)])


STAGES = {"c": (1,), "x": (2,), "z": (4, 8, 12)}


def part(terms, first, size):
    return functools.reduce(
        jnp.add, [term[first : first + size].astype(F32) for term in terms]
    )


def split(terms, stage):
    partners = STAGES[stage]
    size = terms[0].shape[0] // (len(partners) + 1)
    sends = [part(terms, (i + 1) * size, size).astype(BF16) for i in range(len(partners))]
    return part(terms, 0, size), sends


def swapped(sends, stage):
    return [swap(send, by) for send, by in zip(sends, STAGES[stage])]


def gather_start(piece, stage):
    return [swap(piece, by) for by in STAGES[stage]]


def summed_over_devices(one, two, grad_conv, edge_push, push, spread, finish, place):
    parts, grad_conv = lax.optimization_barrier(((one, two), grad_conv))
    received = [swapped(sends, stage) for (_, sends), stage in zip(parts, "xz")]
    received[1][0], edge_grad = lax.optimization_barrier((received[1][0], grad_conv))
    halo = spread(*edge_push(edge_grad))
    received, halo = lax.optimization_barrier((received, halo))
    parts = [
        split([kept] + got, stage) for (kept, _), got, stage in zip(parts, received, "zx")
    ]
    parts, grad_conv = lax.optimization_barrier((parts, grad_conv))
    received = [swapped(sends, stage) for (_, sends), stage in zip(parts, "zx")]
    received, sink = lax.optimization_barrier((received, push(grad_conv)))
    pieces = [part([kept] + got, 0, 1) for (kept, _), got in zip(parts, received)]
    by = 16
    while by < lax.axis_size("dp"):
        pieces = [piece + swap(piece, by) for piece in pieces]
        by *= 2
    pieces = [piece.astype(BF16) for piece in pieces]
    pieces, sink = lax.optimization_barrier((pieces, sink))
    results = finish(sink, halo)
    received = [gather_start(piece, stage) for piece, stage in zip(pieces, "zx")]
    received, pieces, results = lax.optimization_barrier((received, pieces, results))
    early = [jnp.concatenate([piece] + got, axis=0) for piece, got in zip(pieces, received)]
    early_other = [swap(piece, 1) for piece in early]
    received = [gather_start(piece, stage) for piece, stage in zip(early, "xz")]
    received, results = lax.optimization_barrier((received, (results, place(early, early_other))))
    late = [jnp.concatenate(got, axis=0) for got in received]
    late_other = [swap(piece, 1) for piece in late]
    return late, late_other, results


def exchanged(value, merge):
    received = [swap(value, by) for by in (1, 2, 3)]
    value = merged(merge, [value] + received)
    by = 16
    while by < lax.axis_size("dp"):
        value = merge(value, swap(value, by))
        by *= 2
    return [value] + [swap(value, by) for by in (4, 8, 12)]


def stacked_moments(one, two):
    return jnp.stack(merged_moments(one, two))


def per_device(features, kernel_map, occupancy, weights, bn_gain, bn_shift, cotangent):
    rows, channels = features.shape
    peers = lax.axis_size("dp")
    me = lax.axis_index("dp")
    blocks = rows // BLOCK
    inner_rows = rows - 2 * BLOCK
    steps = K // GROUP

    odd = me & 1
    even_pairs = [(i, i ^ 1) for i in range(peers)]
    other_pairs = [(i, ((i + 1) ^ 1) - 1) for i in range(1, peers - 1)]

    def neighbours_swap(to_before, to_after):
        even = lax.ppermute(jnp.where(odd == 1, to_before, to_after), "dp", even_pairs)
        other = lax.ppermute(jnp.where(odd == 1, to_after, to_before), "dp", other_pairs)
        return even, other

    even, other = neighbours_swap(features[:BLOCK], features[rows - BLOCK :])
    map_rows = jnp.transpose(kernel_map)
    map_mate = swap(map_rows, 1)
    odd_flag = odd.reshape(1)

    gain = bn_gain.reshape(1, channels)
    shift = bn_shift.reshape(1, channels)
    smem = pl.BlockSpec(memory_space=pltpu.SMEM)
    vmem = pl.BlockSpec(memory_space=pltpu.VMEM)
    hbm = pl.BlockSpec(memory_space=pltpu.HBM)
    anywhere = pl.BlockSpec(memory_space=pl.ANY)
    groups = K // GROUP
    work = K * rows * channels * 2 * (3 * BLOCK + channels)
    moved = K * channels * channels * 2 * 3

    half_conv = jax.ShapeDtypeStruct((2 * BLOCK, channels), F32)
    scratch = [
        pltpu.VMEM((K, 2 * BLOCK), jnp.int32),
        pltpu.VMEM((K, channels, channels), BF16),
        pltpu.VMEM((GROUP, 2 * BLOCK, channels), BF16),
        pltpu.VMEM((2 * BLOCK, BLOCK), jnp.int32),
        pltpu.SemaphoreType.DMA((groups,)),
    ]

    def in_hbm(value):
        return pltpu.with_memory_space_constraint(value, pltpu.HBM)

    inner = pl.pallas_call(
        inner_kernel,
        in_specs=[vmem, vmem, hbm],
        out_specs=vmem,
        out_shape=half_conv,
        scratch_shapes=scratch,
        compiler_params=params(LIMIT),
        cost_estimate=cost(work / 2, moved),
        name="conv_inner",
    )(in_hbm(map_rows), in_hbm(features), in_hbm(weights))

    outer, stats, window = pl.pallas_call(
        outer_kernel,
        in_specs=[smem, smem, vmem, vmem, vmem, vmem, vmem, hbm],
        out_specs=[vmem, vmem, vmem],
        out_shape=[
            half_conv,
            jax.ShapeDtypeStruct((3, channels), F32),
            jax.ShapeDtypeStruct((rows + 2 * BLOCK, channels), BF16),
        ],
        scratch_shapes=scratch,
        compiler_params=params(LIMIT),
        cost_estimate=cost(work / 2, moved),
        name="conv_outer",
    )(occupancy, odd_flag, map_rows, features, even, other, inner, in_hbm(weights))

    window_mate = swap(window, 1)
    stats = exchanged(stats, stacked_moments)

    block_out, sums = pl.pallas_call(
        norm_kernel,
        in_specs=[smem] + [vmem] * 10,
        out_shape=[
            jax.ShapeDtypeStruct((rows, channels), BF16),
            jax.ShapeDtypeStruct((2, channels), F32),
        ],
        compiler_params=params(LIMIT),
        cost_estimate=cost(rows * channels * 20, rows * channels * 10),
        name="norm",
    )(occupancy, inner, outer, gain, shift, cotangent, features, *stats)

    grads = exchanged(sums, jnp.add)

    grad_conv, sums = pl.pallas_call(
        functools.partial(grad_conv_kernel, len(stats)),
        in_specs=[smem] + [vmem] * 13,
        out_shape=[
            jax.ShapeDtypeStruct((rows, channels), BF16),
            jax.ShapeDtypeStruct((2, channels), F32),
        ],
        compiler_params=params(LIMIT),
        cost_estimate=cost(rows * channels * 20, rows * channels * 8),
        name="grad_conv",
    )(occupancy, inner, outer, gain, shift, cotangent, *stats, *grads)
    grad_mate = swap(grad_conv, 1)

    core, lane, depth = me & 1, (me >> 1) & 1, (me >> 2) & 3
    places = jnp.stack([core, lane * 4 + depth, depth * 2 + lane])
    size = channels // 8
    rows_one, rows_two = K_ONE * size, (HALF - K_ONE) * size + size // 2
    shapes = [((4, rows_one, channels), F32), ((4, rows_one, channels), BF16)]
    shapes += [((2, rows_two, channels), F32)] + [((2, rows_two, channels), BF16)] * 3
    keep_one, send_one, keep_two, *sends_two = pl.pallas_call(
        gradient_kernel,
        in_specs=[smem] + [vmem] * 6,
        out_specs=[anywhere] * 6,
        out_shape=[jax.ShapeDtypeStruct(*shape) for shape in shapes],
        scratch_shapes=[
            pltpu.VMEM((2, rows, BLOCK), jnp.int32),
            pltpu.VMEM((K_ONE, 2 * rows, channels), BF16),
            pltpu.VMEM((2 * rows, channels), BF16),
            pltpu.VMEM((K_ONE, channels, channels), F32),
        ]
        + [pltpu.VMEM(*shape) for shape in shapes]
        + [pltpu.SemaphoreType.DMA((6,))],
        compiler_params=params(LIMIT),
        cost_estimate=cost(work, K * channels * channels * 6),
        name="weight_gradient",
    )(places, grad_conv, grad_mate, map_rows, map_mate, window, window_mate)
    one, two = (keep_one, [send_one]), (keep_two, sends_two)

    weight_spec = pl.BlockSpec((GROUP, channels, channels), lambda s: (s, 0, 0))

    push_grid = dict(
        grid=(groups,),
        compiler_params=params(LIMIT),
        cost_estimate=cost(1000, 1000),
    )

    def edge_push(grad_conv):
        edges = jnp.concatenate([grad_conv[:BLOCK], grad_conv[rows - BLOCK :]], axis=0)
        edge = jax.ShapeDtypeStruct((BLOCK, channels), BF16)
        before, after = pl.pallas_call(
            edge_push_kernel,
            in_specs=[full((2 * BLOCK, channels)), full((K, rows)), weight_spec],
            out_specs=[full((BLOCK, channels))] * 2,
            out_shape=[edge, edge],
            scratch_shapes=[pltpu.VMEM((BLOCK, channels), F32)] * 2,
            name="push_edges",
            **push_grid,
        )(edges, map_rows, weights)
        return before, after

    def push(grad_conv):
        return pl.pallas_call(
            push_kernel,
            in_specs=[full((rows, channels)), full((K, rows)), weight_spec],
            out_specs=full((rows, channels)),
            out_shape=jax.ShapeDtypeStruct((rows, channels), F32),
            name="push",
            **push_grid,
        )(grad_conv, map_rows, weights)

    def finish(sink, halo):
        even, other = halo
        from_prev = jnp.where(odd == 1, even, other).astype(F32)
        from_next = jnp.where(odd == 1, other, even).astype(F32)
        occupied = occupied_rows(occupancy[0], rows)
        received = jnp.concatenate(
            [
                sink[:BLOCK] + from_prev,
                sink[BLOCK : rows - BLOCK],
                sink[rows - BLOCK :] + from_next,
            ],
            axis=0,
        )
        total = jnp.where(occupied, cotangent.astype(F32), 0.0) + received
        return total.astype(BF16), sums[0], sums[1]


    def placed(layout, sources, *into):
        count = sum(one.shape[0] + two.shape[0] * (HALF - K_ONE + 1) for one, two in sources)
        operands = []
        for one, two in sources:
            operands += [one.reshape(one.shape[0], K_ONE, size, channels), two]
        return pl.pallas_call(
            functools.partial(place_kernel, layout),
            in_specs=[smem] + [anywhere] * len(operands) + [hbm] * len(into),
            out_specs=hbm,
            out_shape=jax.ShapeDtypeStruct(weights.shape, BF16),
            scratch_shapes=[pltpu.SemaphoreType.DMA((count,))],
            input_output_aliases={len(operands) + 1: 0} if into else {},
            compiler_params=params(LIMIT),
            cost_estimate=cost(0, K * channels * channels * 2),
            name="place",
        )(places, *operands, *into)

    def place_early(own, other):
        return placed(((0, 0, 0), (1, 0, 0)), (own, other))

    late, late_other, results = summed_over_devices(
        one, two, grad_conv, edge_push, push, neighbours_swap, finish, place_early
    )
    (grad_features, grad_gain, grad_shift), grad_weights = results
    first_late = (8 - late[0].shape[0], 8 - late[1].shape[0])
    grad_weights = placed(((0, *first_late),), (late,), grad_weights)
    grad_weights = placed(((1, *first_late),), (late_other,), grad_weights)
    return block_out, grad_features, grad_weights, grad_gain, grad_shift


def solution(mesh):
    in_specs = (
        P(("parts", "dp"), None),
        P(("parts", "dp"), None),
        P(("parts", "dp")),
        P(),
        P(),
        P(),
        P(("parts", "dp"), None),
    )
    out_specs = (
        P(("parts", "dp"), None),
        P(("parts", "dp"), None),
        P("parts", None, None),
        P("parts"),
        P("parts"),
    )
    return jax.shard_map(
        per_device, mesh=mesh, in_specs=in_specs, out_specs=out_specs, check_vma=False
    )
```

```python
import functools

import jax
import jax.numpy as jnp
from jax import lax
from jax.experimental import pallas as pl
from jax.experimental.pallas import tpu as pltpu
from jax.sharding import PartitionSpec as P

K = 27
BLOCK = 128
GROUP = 9
HALF = 13
K_ONE = 9
EPSILON = 1e-05
F32 = jnp.float32
BF16 = jnp.bfloat16
LIMIT = 24 * 1024 * 1024


def merged(merge, values):
    return merge(merge(values[0], values[1]), merge(values[2], values[3]))


def merged_moments(one, two):
    (sum_one, square_one, count_one), (sum_two, square_two, count_two) = one, two
    away = sum_one / count_one - sum_two / count_two
    count = count_one + count_two
    square = (square_one + square_two) + away * away * (count_one * count_two / count)
    return sum_one + sum_two, square, count


def dot(a, b, contract):
    return lax.dot_general(a, b, ((contract[0], contract[1]), ((), ())), preferred_element_type=F32)


def full(shape):
    return pl.BlockSpec(shape, lambda *_: (0,) * len(shape))


def params(limit):
    return pltpu.CompilerParams(vmem_limit_bytes=limit)


def cost(flops, moved):
    return pl.CostEstimate(flops=int(flops), bytes_accessed=int(moved), transcendentals=0)


def occupied_rows(filled, rows):
    position = lax.broadcasted_iota(jnp.int32, (rows, 1), 0)
    return (position < filled - BLOCK) | (position >= rows - BLOCK)


def chosen_slots(slot, slots):
    return jnp.where(slot == slots, 1.0, 0.0).astype(BF16)


def transposed_map(map_ref):
    spare = jnp.zeros((BLOCK - K, map_ref.shape[1]), jnp.int32)
    return jnp.transpose(jnp.concatenate([map_ref[...], spare], axis=0))


def convolve(map_ref, tiles, first_slots, weight_hbm, conv_ref, scratch):
    weight, picked, index, weight_sem = scratch
    groups = K // GROUP

    def fetch(g):
        here = pl.ds(g * GROUP, GROUP)
        return pltpu.make_async_copy(weight_hbm.at[here], weight.at[here], weight_sem.at[g])

    for g in range(groups):
        fetch(g).start()
    index[...] = transposed_map(map_ref)
    conv_ref[...] = jnp.zeros_like(conv_ref)
    slots = lax.broadcasted_iota(jnp.int32, (BLOCK, 3 * BLOCK), 1)

    def group(g, carry):
        local = pltpu.roll(index[...], lax.rem(BLOCK - g * GROUP, BLOCK), 1)
        for b, tile in enumerate(tiles):
            here = slice(b * BLOCK, (b + 1) * BLOCK)
            slot = local[here] - first_slots[b]
            for j in range(GROUP):
                chosen = chosen_slots(slot[:, j : j + 1], slots)
                picked[j, here, :] = dot(chosen, tile[...], ((1,), (0,))).astype(BF16)
        fetch(g).wait()
        total = conv_ref[...]
        for j in range(GROUP):
            total = total + dot(picked[j], weight[g * GROUP + j], ((1,), (0,)))
        conv_ref[...] = total
        return carry

    lax.fori_loop(0, groups, group, 0)


def inner_kernel(map_ref, own_ref, weight_hbm, conv_ref, chosen_map, *scratch):
    rows = own_ref.shape[0]
    chosen_map[...] = map_ref[:, BLOCK : rows - BLOCK]
    blocks = range(1, rows // BLOCK - 1)
    tiles = [own_ref.at[(b - 1) * BLOCK : (b + 2) * BLOCK] for b in blocks]
    first_slots = [rows - BLOCK + b * BLOCK for b in blocks]
    convolve(chosen_map, tiles, first_slots, weight_hbm, conv_ref, scratch)


def outer_kernel(
    filled_ref, odd_ref, map_ref, own_ref, even_ref, other_ref, inner_ref, weight_hbm,
    conv_ref, stats_ref, window_ref, chosen_map, *scratch,
):
    rows = own_ref.shape[0]
    odd = odd_ref[0] == 1
    window_ref[0:BLOCK, :] = jnp.where(odd, even_ref[...], other_ref[...])
    window_ref[BLOCK : rows + BLOCK, :] = own_ref[...]
    window_ref[rows + BLOCK :, :] = jnp.where(odd, other_ref[...], even_ref[...])
    chosen_map[:, 0:BLOCK] = map_ref[:, 0:BLOCK]
    chosen_map[:, BLOCK:] = map_ref[:, rows - BLOCK :]
    tiles = [window_ref.at[0 : 3 * BLOCK], window_ref.at[rows - BLOCK :]]
    first_slots = [rows - BLOCK, 2 * rows - 2 * BLOCK]
    convolve(chosen_map, tiles, first_slots, weight_hbm, conv_ref, scratch)
    filled = filled_ref[0]
    count = filled.astype(F32)
    conv = whole(inner_ref, conv_ref)
    occupied = occupied_rows(filled, rows)
    sums = jnp.sum(jnp.where(occupied, conv, 0.0), axis=0, keepdims=True)
    off = jnp.where(occupied, conv - sums / count, 0.0)
    squares = jnp.sum(off * off, axis=0, keepdims=True)
    stats_ref[...] = jnp.concatenate([sums, squares, jnp.full_like(sums, count)], axis=0)


def whole(inner_ref, outer_ref):
    return jnp.concatenate([outer_ref[0:BLOCK, :], inner_ref[...], outer_ref[BLOCK:, :]], axis=0)


def normalised(filled, inner_ref, outer_ref, stats_refs, gain_ref, shift_ref, cotangent_ref):
    conv = whole(inner_ref, outer_ref)
    sums, squares, total = merged(
        merged_moments, [[ref[i : i + 1, :] for i in range(3)] for ref in stats_refs]
    )
    center = sums / total
    inverse = lax.rsqrt(squares / total + EPSILON)
    occupied = occupied_rows(filled, conv.shape[0])
    normed = (conv - center) * inverse
    affine = gain_ref[...] * normed + shift_ref[...]
    upstream = jnp.where(occupied & (affine > 0.0), cotangent_ref[...].astype(F32), 0.0)
    return occupied, normed, affine, upstream, inverse, total


def norm_kernel(
    filled_ref, inner_ref, outer_ref, gain_ref, shift_ref, cotangent_ref, feature_ref, *refs
):
    *stats_refs, out_ref, sums_ref = refs
    occupied, normed, affine, upstream, _, _ = normalised(
        filled_ref[0], inner_ref, outer_ref, stats_refs, gain_ref, shift_ref, cotangent_ref
    )
    out = jnp.maximum(affine, 0.0) + feature_ref[...].astype(F32)
    out_ref[...] = jnp.where(occupied, out, 0.0).astype(BF16)
    sums_ref[...] = jnp.concatenate(
        [jnp.sum(upstream * normed, axis=0, keepdims=True), jnp.sum(upstream, axis=0, keepdims=True)],
        axis=0,
    )


def grad_conv_kernel(
    parts, filled_ref, inner_ref, outer_ref, gain_ref, shift_ref, cotangent_ref, *refs
):
    stats_refs, grads_refs, (grad_ref, sums_ref) = refs[:parts], refs[parts:-2], refs[-2:]
    occupied, normed, _, upstream, inverse, total = normalised(
        filled_ref[0], inner_ref, outer_ref, stats_refs, gain_ref, shift_ref, cotangent_ref
    )
    sums = merged(jnp.add, [ref[...] for ref in grads_refs])
    sums_ref[...] = sums
    grad_conv = gain_ref[...] * inverse * (
        upstream - sums[1:2, :] / total - normed * sums[0:1, :] / total
    )
    grad_ref[...] = jnp.where(occupied, grad_conv, 0.0).astype(BF16)


def gradient_kernel(
    place_ref, grad_own, grad_mate, map_own, map_mate, window_own, window_mate, *refs
):
    outs, scratch = refs[:6], refs[6:]
    index, picked, grad, product, *staged, out_sem = scratch
    keep_one, send_one, keep_two, *sends_two = staged
    rows, channels = grad_own.shape
    core = place_ref[0]
    slots = lax.broadcasted_iota(jnp.int32, (BLOCK, 3 * BLOCK), 1)
    sides = ((map_own, window_own), (map_mate, window_mate))
    grad[0:rows, :] = grad_own[...]
    grad[rows:, :] = grad_mate[...]
    for side, (map_ref, _) in enumerate(sides):
        index[side] = transposed_map(map_ref)

    def gradient(j, slot_of):
        for side, (_, window) in enumerate(sides):
            for b in range(rows // BLOCK):
                here = slice(b * BLOCK, (b + 1) * BLOCK)
                chosen = chosen_slots(slot_of(side)[here] - (rows + (b - 1) * BLOCK), slots)
                tile = window[b * BLOCK : (b + 3) * BLOCK, :]
                at = slice(side * rows + b * BLOCK, side * rows + (b + 1) * BLOCK)
                picked[j, at, :] = dot(chosen, tile, ((1,), (0,))).astype(BF16)
        product[j] = dot(picked[j], grad[...], ((0,), (0,)))

    def stored(staged, out, n):
        return pltpu.make_async_copy(staged, out, out_sem.at[n])

    shift = lax.rem(BLOCK - core * (HALF + 1), BLOCK)
    local = [pltpu.roll(index[side], shift, 1) for side in range(2)]
    size = channels // 8

    def rows_of(piece, place, size, first):
        at = lax.bitwise_xor(jnp.int32(piece), place) * size + first
        return pl.ds(pl.multiple_of(at, 16), size)

    for j in range(K_ONE):
        gradient(j, lambda side: local[side][:, j : j + 1])
        here = slice(j * size, (j + 1) * size)
        for piece in range(8):
            value = product[j, rows_of(piece, place_ref[1], size, 0), :]
            if piece < 4:
                keep_one[piece, here, :] = value
            else:
                send_one[piece - 4, here, :] = value.astype(BF16)
    copies = [stored(keep_one, outs[0], 0), stored(send_one, outs[1], 1)]
    for copy in copies:
        copy.start()
    for j in range(HALF - K_ONE + 1):
        whole_offset = j < HALF - K_ONE
        if whole_offset:
            gradient(j, lambda side: local[side][:, K_ONE + j : K_ONE + j + 1])
        else:
            gradient(j, lambda side: index[side][:, HALF : HALF + 1])
        count = size if whole_offset else size // 2
        first = 0 if whole_offset else core * (channels // 2)
        here = slice(j * size, j * size + count)
        for piece in range(8):
            value = product[j, rows_of(piece, place_ref[2], count, first), :]
            if piece < 2:
                keep_two[piece, here, :] = value
            else:
                sends_two[piece // 2 - 1][piece % 2, here, :] = value.astype(BF16)
    late = [stored(keep_two, outs[2], 2)]
    late += [stored(sends_two[n], outs[3 + n], 3 + n) for n in range(3)]
    for copy in late:
        copy.start()
    for copy in copies + late:
        copy.wait()


def scatter(step, grad_ref, first_row, map_ref, weight_ref, windows):
    pushed = [dot(grad_ref[...], weight_ref[j], ((1,), (1,))).astype(BF16) for j in range(GROUP)]
    named = [map_ref[step * GROUP + j, :][None] for j in range(GROUP)]
    for b, first_slot, sink in windows:
        rows = slice(b * BLOCK, (b + 1) * BLOCK)
        at = slice(first_row(b), first_row(b) + BLOCK)
        slots = lax.broadcasted_iota(jnp.int32, (sink.shape[0], BLOCK), 0) + first_slot
        chosen = jnp.concatenate(
            [chosen_slots(named[j][:, at], slots) for j in range(GROUP)],
            axis=1,
        )
        stacked = jnp.concatenate([pushed[j][rows] for j in range(GROUP)], axis=0)
        sink[...] = sink[...] + dot(chosen, stacked, ((1,), (0,)))


def edge_push_kernel(grad_ref, map_ref, weight_ref, before_ref, after_ref, before, after):
    step = pl.program_id(0)
    rows = map_ref.shape[1]

    @pl.when(step == 0)
    def _():
        before[...] = jnp.zeros_like(before)
        after[...] = jnp.zeros_like(after)

    def first_row(b):
        return b * (rows - BLOCK)

    windows = [(0, rows - BLOCK, before), (1, 2 * rows, after)]
    scatter(step, grad_ref, first_row, map_ref, weight_ref, windows)

    @pl.when(step == pl.num_programs(0) - 1)
    def _():
        before_ref[...] = before[...].astype(BF16)
        after_ref[...] = after[...].astype(BF16)


def push_kernel(grad_ref, map_ref, weight_ref, own_ref):
    step = pl.program_id(0)
    rows = map_ref.shape[1]

    @pl.when(step == 0)
    def _():
        own_ref[...] = jnp.zeros_like(own_ref)

    windows = []
    for b in range(rows // BLOCK):
        start, stop = max(b - 1, 0) * BLOCK, min((b + 2) * BLOCK, rows)
        windows.append((b, rows + start, own_ref.at[start:stop]))
    scatter(step, grad_ref, lambda b: b * BLOCK, map_ref, weight_ref, windows)


def place_kernel(layout, places_ref, *refs):
    out_ref, sems = refs[-2:]
    size = out_ref.shape[1] // 8
    copies = []

    def put(source, out, part, piece, count, base):
        at = lax.bitwise_xor(jnp.int32(piece), places_ref[part]) * count + base
        here = pl.ds(pl.multiple_of(at, 16), count)
        copies.append(pltpu.make_async_copy(source, out.at[:, here, :], sems.at[len(copies)]))

    for n, (other, first_one, first_two) in enumerate(layout):
        one, two = refs[2 * n : 2 * n + 2]
        core = lax.bitwise_xor(places_ref[0], jnp.int32(other))
        first = core * (HALF + 1)
        for i in range(one.shape[0]):
            put(one.at[i], out_ref.at[pl.ds(first, K_ONE)], 1, first_one + i, size, 0)
        for i in range(two.shape[0]):
            piece = first_two + i
            for j in range(HALF - K_ONE):
                source = two.at[pl.ds(i, 1), pl.ds(j * size, size)]
                put(source, out_ref.at[pl.ds(first + K_ONE + j, 1)], 2, piece, size, 0)
            source = two.at[pl.ds(i, 1), pl.ds((HALF - K_ONE) * size, size // 2)]
            base = core * (out_ref.shape[1] // 2)
            put(source, out_ref.at[pl.ds(HALF, 1)], 2, piece, size // 2, base)
    for copy in copies:
        copy.start()
    for copy in copies:
        copy.wait()


def swap(value, by):
    peers = lax.axis_size("dp")
    return lax.ppermute(value, "dp", [(i, i ^ by) for i in range(peers)])


STAGES = {"c": (1,), "x": (2,), "z": (4, 8, 12)}


def part(terms, first, size):
    return functools.reduce(
        jnp.add, [term[first : first + size].astype(F32) for term in terms]
    )


def split(terms, stage):
    partners = STAGES[stage]
    size = terms[0].shape[0] // (len(partners) + 1)
    sends = [part(terms, (i + 1) * size, size).astype(BF16) for i in range(len(partners))]
    return part(terms, 0, size), sends


def swapped(sends, stage):
    return [swap(send, by) for send, by in zip(sends, STAGES[stage])]


def gather_start(piece, stage):
    return [swap(piece, by) for by in STAGES[stage]]


def summed_over_devices(one, two, grad_conv, edge_push, push, spread, finish, place):
    parts, grad_conv = lax.optimization_barrier(((one, two), grad_conv))
    received = [swapped(sends, stage) for (_, sends), stage in zip(parts, "xz")]
    edges, sink = edge_push(grad_conv), push(grad_conv)
    received, edges, sink = lax.optimization_barrier((received, edges, sink))
    parts = [
        split([kept] + got, stage) for (kept, _), got, stage in zip(parts, received, "zx")
    ]
    parts, edges = lax.optimization_barrier((parts, edges))
    received = [swapped(sends, stage) for (_, sends), stage in zip(parts, "zx")]
    halo = spread(*edges)
    received, sink = lax.optimization_barrier((received, sink))
    pieces = [part([kept] + got, 0, 1) for (kept, _), got in zip(parts, received)]
    by = 16
    while by < lax.axis_size("dp"):
        pieces = [piece + swap(piece, by) for piece in pieces]
        by *= 2
    pieces = [piece.astype(BF16) for piece in pieces]
    pieces, sink = lax.optimization_barrier((pieces, sink))
    results = finish(sink, halo)
    received = [gather_start(piece, stage) for piece, stage in zip(pieces, "zx")]
    received, pieces, results = lax.optimization_barrier((received, pieces, results))
    early = [jnp.concatenate([piece] + got, axis=0) for piece, got in zip(pieces, received)]
    early_other = [swap(piece, 1) for piece in early]
    received = [gather_start(piece, stage) for piece, stage in zip(early, "xz")]
    received, results = lax.optimization_barrier((received, (results, place(early, early_other))))
    late = [jnp.concatenate(got, axis=0) for got in received]
    late_other = [swap(piece, 1) for piece in late]
    return late, late_other, results


def exchanged(value, merge):
    received = [swap(value, by) for by in (1, 2, 3)]
    value = merged(merge, [value] + received)
    by = 16
    while by < lax.axis_size("dp"):
        value = merge(value, swap(value, by))
        by *= 2
    return [value] + [swap(value, by) for by in (4, 8, 12)]


def stacked_moments(one, two):
    return jnp.stack(merged_moments(one, two))


def per_device(features, kernel_map, occupancy, weights, bn_gain, bn_shift, cotangent):
    rows, channels = features.shape
    peers = lax.axis_size("dp")
    me = lax.axis_index("dp")
    blocks = rows // BLOCK
    inner_rows = rows - 2 * BLOCK
    steps = K // GROUP

    odd = me & 1
    even_pairs = [(i, i ^ 1) for i in range(peers)]
    other_pairs = [(i, ((i + 1) ^ 1) - 1) for i in range(1, peers - 1)]

    def neighbours_swap(to_before, to_after):
        even = lax.ppermute(jnp.where(odd == 1, to_before, to_after), "dp", even_pairs)
        other = lax.ppermute(jnp.where(odd == 1, to_after, to_before), "dp", other_pairs)
        return even, other

    even, other = neighbours_swap(features[:BLOCK], features[rows - BLOCK :])
    map_rows = jnp.transpose(kernel_map)
    map_mate = swap(map_rows, 1)
    odd_flag = odd.reshape(1)

    gain = bn_gain.reshape(1, channels)
    shift = bn_shift.reshape(1, channels)
    smem = pl.BlockSpec(memory_space=pltpu.SMEM)
    vmem = pl.BlockSpec(memory_space=pltpu.VMEM)
    hbm = pl.BlockSpec(memory_space=pltpu.HBM)
    anywhere = pl.BlockSpec(memory_space=pl.ANY)
    groups = K // GROUP
    work = K * rows * channels * 2 * (3 * BLOCK + channels)
    moved = K * channels * channels * 2 * 3

    half_conv = jax.ShapeDtypeStruct((2 * BLOCK, channels), F32)
    scratch = [
        pltpu.VMEM((K, 2 * BLOCK), jnp.int32),
        pltpu.VMEM((K, channels, channels), BF16),
        pltpu.VMEM((GROUP, 2 * BLOCK, channels), BF16),
        pltpu.VMEM((2 * BLOCK, BLOCK), jnp.int32),
        pltpu.SemaphoreType.DMA((groups,)),
    ]

    def in_hbm(value):
        return pltpu.with_memory_space_constraint(value, pltpu.HBM)

    inner = pl.pallas_call(
        inner_kernel,
        in_specs=[vmem, vmem, hbm],
        out_specs=vmem,
        out_shape=half_conv,
        scratch_shapes=scratch,
        compiler_params=params(LIMIT),
        cost_estimate=cost(work / 2, moved),
        name="conv_inner",
    )(in_hbm(map_rows), in_hbm(features), in_hbm(weights))

    outer, stats, window = pl.pallas_call(
        outer_kernel,
        in_specs=[smem, smem, vmem, vmem, vmem, vmem, vmem, hbm],
        out_specs=[vmem, vmem, vmem],
        out_shape=[
            half_conv,
            jax.ShapeDtypeStruct((3, channels), F32),
            jax.ShapeDtypeStruct((rows + 2 * BLOCK, channels), BF16),
        ],
        scratch_shapes=scratch,
        compiler_params=params(LIMIT),
        cost_estimate=cost(work / 2, moved),
        name="conv_outer",
    )(occupancy, odd_flag, map_rows, features, even, other, inner, in_hbm(weights))

    window_mate = swap(window, 1)
    stats = exchanged(stats, stacked_moments)

    block_out, sums = pl.pallas_call(
        norm_kernel,
        in_specs=[smem] + [vmem] * 10,
        out_shape=[
            jax.ShapeDtypeStruct((rows, channels), BF16),
            jax.ShapeDtypeStruct((2, channels), F32),
        ],
        compiler_params=params(LIMIT),
        cost_estimate=cost(rows * channels * 20, rows * channels * 10),
        name="norm",
    )(occupancy, inner, outer, gain, shift, cotangent, features, *stats)

    grads = exchanged(sums, jnp.add)

    grad_conv, sums = pl.pallas_call(
        functools.partial(grad_conv_kernel, len(stats)),
        in_specs=[smem] + [vmem] * 13,
        out_shape=[
            jax.ShapeDtypeStruct((rows, channels), BF16),
            jax.ShapeDtypeStruct((2, channels), F32),
        ],
        compiler_params=params(LIMIT),
        cost_estimate=cost(rows * channels * 20, rows * channels * 8),
        name="grad_conv",
    )(occupancy, inner, outer, gain, shift, cotangent, *stats, *grads)
    grad_mate = swap(grad_conv, 1)

    core, lane, depth = me & 1, (me >> 1) & 1, (me >> 2) & 3
    places = jnp.stack([core, lane * 4 + depth, depth * 2 + lane])
    size = channels // 8
    rows_one, rows_two = K_ONE * size, (HALF - K_ONE) * size + size // 2
    shapes = [((4, rows_one, channels), F32), ((4, rows_one, channels), BF16)]
    shapes += [((2, rows_two, channels), F32)] + [((2, rows_two, channels), BF16)] * 3
    keep_one, send_one, keep_two, *sends_two = pl.pallas_call(
        gradient_kernel,
        in_specs=[smem] + [vmem] * 6,
        out_specs=[anywhere] * 6,
        out_shape=[jax.ShapeDtypeStruct(*shape) for shape in shapes],
        scratch_shapes=[
            pltpu.VMEM((2, rows, BLOCK), jnp.int32),
            pltpu.VMEM((K_ONE, 2 * rows, channels), BF16),
            pltpu.VMEM((2 * rows, channels), BF16),
            pltpu.VMEM((K_ONE, channels, channels), F32),
        ]
        + [pltpu.VMEM(*shape) for shape in shapes]
        + [pltpu.SemaphoreType.DMA((6,))],
        compiler_params=params(LIMIT),
        cost_estimate=cost(work, K * channels * channels * 6),
        name="weight_gradient",
    )(places, grad_conv, grad_mate, map_rows, map_mate, window, window_mate)
    one, two = (keep_one, [send_one]), (keep_two, sends_two)

    weight_spec = pl.BlockSpec((GROUP, channels, channels), lambda s: (s, 0, 0))

    push_grid = dict(
        grid=(groups,),
        compiler_params=params(LIMIT),
        cost_estimate=cost(1000, 1000),
    )

    def edge_push(grad_conv):
        edges = jnp.concatenate([grad_conv[:BLOCK], grad_conv[rows - BLOCK :]], axis=0)
        edge = jax.ShapeDtypeStruct((BLOCK, channels), BF16)
        before, after = pl.pallas_call(
            edge_push_kernel,
            in_specs=[full((2 * BLOCK, channels)), full((K, rows)), weight_spec],
            out_specs=[full((BLOCK, channels))] * 2,
            out_shape=[edge, edge],
            scratch_shapes=[pltpu.VMEM((BLOCK, channels), F32)] * 2,
            name="push_edges",
            **push_grid,
        )(edges, map_rows, weights)
        return before, after

    def push(grad_conv):
        return pl.pallas_call(
            push_kernel,
            in_specs=[full((rows, channels)), full((K, rows)), weight_spec],
            out_specs=full((rows, channels)),
            out_shape=jax.ShapeDtypeStruct((rows, channels), F32),
            name="push",
            **push_grid,
        )(grad_conv, map_rows, weights)

    def finish(sink, halo):
        even, other = halo
        from_prev = jnp.where(odd == 1, even, other).astype(F32)
        from_next = jnp.where(odd == 1, other, even).astype(F32)
        occupied = occupied_rows(occupancy[0], rows)
        received = jnp.concatenate(
            [
                sink[:BLOCK] + from_prev,
                sink[BLOCK : rows - BLOCK],
                sink[rows - BLOCK :] + from_next,
            ],
            axis=0,
        )
        total = jnp.where(occupied, cotangent.astype(F32), 0.0) + received
        return total.astype(BF16), sums[0], sums[1]


    def placed(layout, sources, *into):
        count = sum(one.shape[0] + two.shape[0] * (HALF - K_ONE + 1) for one, two in sources)
        operands = []
        for one, two in sources:
            operands += [one.reshape(one.shape[0], K_ONE, size, channels), two]
        return pl.pallas_call(
            functools.partial(place_kernel, layout),
            in_specs=[smem] + [anywhere] * len(operands) + [hbm] * len(into),
            out_specs=hbm,
            out_shape=jax.ShapeDtypeStruct(weights.shape, BF16),
            scratch_shapes=[pltpu.SemaphoreType.DMA((count,))],
            input_output_aliases={len(operands) + 1: 0} if into else {},
            compiler_params=params(LIMIT),
            cost_estimate=cost(0, K * channels * channels * 2),
            name="place",
        )(places, *operands, *into)

    def place_early(own, other):
        return placed(((0, 0, 0), (1, 0, 0)), (own, other))

    late, late_other, results = summed_over_devices(
        one, two, grad_conv, edge_push, push, neighbours_swap, finish, place_early
    )
    (grad_features, grad_gain, grad_shift), grad_weights = results
    first_late = (8 - late[0].shape[0], 8 - late[1].shape[0])
    grad_weights = placed(((0, *first_late),), (late,), grad_weights)
    grad_weights = placed(((1, *first_late),), (late_other,), grad_weights)
    return block_out, grad_features, grad_weights, grad_gain, grad_shift


def solution(mesh):
    in_specs = (
        P(("parts", "dp"), None),
        P(("parts", "dp"), None),
        P(("parts", "dp")),
        P(),
        P(),
        P(),
        P(("parts", "dp"), None),
    )
    out_specs = (
        P(("parts", "dp"), None),
        P(("parts", "dp"), None),
        P("parts", None, None),
        P("parts"),
        P("parts"),
    )
    return jax.shard_map(
        per_device, mesh=mesh, in_specs=in_specs, out_specs=out_specs, check_vma=False
    )
```

```python
import functools

import jax
import jax.numpy as jnp
from jax import lax
from jax.experimental import pallas as pl
from jax.experimental.pallas import tpu as pltpu
from jax.sharding import PartitionSpec as P

K = 27
BLOCK = 128
GROUP = 9
HALF = 13
K_ONE = 9
EPSILON = 1e-05
F32 = jnp.float32
BF16 = jnp.bfloat16
LIMIT = 24 * 1024 * 1024


def merged(merge, values):
    return merge(merge(values[0], values[1]), merge(values[2], values[3]))


def merged_moments(one, two):
    (sum_one, square_one, count_one), (sum_two, square_two, count_two) = one, two
    away = sum_one / count_one - sum_two / count_two
    count = count_one + count_two
    square = (square_one + square_two) + away * away * (count_one * count_two / count)
    return sum_one + sum_two, square, count


def dot(a, b, contract):
    return lax.dot_general(a, b, ((contract[0], contract[1]), ((), ())), preferred_element_type=F32)


def full(shape):
    return pl.BlockSpec(shape, lambda *_: (0,) * len(shape))


def params(limit):
    return pltpu.CompilerParams(vmem_limit_bytes=limit)


def cost(flops, moved):
    return pl.CostEstimate(flops=int(flops), bytes_accessed=int(moved), transcendentals=0)


def occupied_rows(filled, rows):
    position = lax.broadcasted_iota(jnp.int32, (rows, 1), 0)
    return (position < filled - BLOCK) | (position >= rows - BLOCK)


def chosen_slots(slot, slots):
    return jnp.where(slot == slots, 1.0, 0.0).astype(BF16)


def transposed_map(map_ref):
    spare = jnp.zeros((BLOCK - K, map_ref.shape[1]), jnp.int32)
    return jnp.transpose(jnp.concatenate([map_ref[...], spare], axis=0))


def convolve(map_ref, tiles, first_slots, weight_hbm, conv_ref, scratch):
    weight, picked, index, weight_sem = scratch
    groups = K // GROUP

    def fetch(g):
        here = pl.ds(g * GROUP, GROUP)
        return pltpu.make_async_copy(weight_hbm.at[here], weight.at[here], weight_sem.at[g])

    for g in range(groups):
        fetch(g).start()
    index[...] = transposed_map(map_ref)
    conv_ref[...] = jnp.zeros_like(conv_ref)
    slots = lax.broadcasted_iota(jnp.int32, (BLOCK, 3 * BLOCK), 1)

    def group(g, carry):
        local = pltpu.roll(index[...], lax.rem(BLOCK - g * GROUP, BLOCK), 1)
        for b, tile in enumerate(tiles):
            here = slice(b * BLOCK, (b + 1) * BLOCK)
            slot = local[here] - first_slots[b]
            for j in range(GROUP):
                chosen = chosen_slots(slot[:, j : j + 1], slots)
                picked[j, here, :] = dot(chosen, tile[...], ((1,), (0,))).astype(BF16)
        fetch(g).wait()
        total = conv_ref[...]
        for j in range(GROUP):
            total = total + dot(picked[j], weight[g * GROUP + j], ((1,), (0,)))
        conv_ref[...] = total
        return carry

    lax.fori_loop(0, groups, group, 0)


def inner_kernel(map_ref, own_ref, weight_hbm, conv_ref, chosen_map, *scratch):
    rows = own_ref.shape[0]
    chosen_map[...] = map_ref[:, BLOCK : rows - BLOCK]
    blocks = range(1, rows // BLOCK - 1)
    tiles = [own_ref.at[(b - 1) * BLOCK : (b + 2) * BLOCK] for b in blocks]
    first_slots = [rows - BLOCK + b * BLOCK for b in blocks]
    convolve(chosen_map, tiles, first_slots, weight_hbm, conv_ref, scratch)


def outer_kernel(
    filled_ref, odd_ref, map_ref, own_ref, even_ref, other_ref, inner_ref, weight_hbm,
    conv_ref, stats_ref, window_ref, chosen_map, *scratch,
):
    rows = own_ref.shape[0]
    odd = odd_ref[0] == 1
    window_ref[0:BLOCK, :] = jnp.where(odd, even_ref[...], other_ref[...])
    window_ref[BLOCK : rows + BLOCK, :] = own_ref[...]
    window_ref[rows + BLOCK :, :] = jnp.where(odd, other_ref[...], even_ref[...])
    chosen_map[:, 0:BLOCK] = map_ref[:, 0:BLOCK]
    chosen_map[:, BLOCK:] = map_ref[:, rows - BLOCK :]
    tiles = [window_ref.at[0 : 3 * BLOCK], window_ref.at[rows - BLOCK :]]
    first_slots = [rows - BLOCK, 2 * rows - 2 * BLOCK]
    convolve(chosen_map, tiles, first_slots, weight_hbm, conv_ref, scratch)
    filled = filled_ref[0]
    count = filled.astype(F32)
    conv = whole(inner_ref, conv_ref)
    occupied = occupied_rows(filled, rows)
    sums = jnp.sum(jnp.where(occupied, conv, 0.0), axis=0, keepdims=True)
    off = jnp.where(occupied, conv - sums / count, 0.0)
    squares = jnp.sum(off * off, axis=0, keepdims=True)
    stats_ref[...] = jnp.concatenate([sums, squares, jnp.full_like(sums, count)], axis=0)


def whole(inner_ref, outer_ref):
    return jnp.concatenate([outer_ref[0:BLOCK, :], inner_ref[...], outer_ref[BLOCK:, :]], axis=0)


def normalised(filled, inner_ref, outer_ref, stats_refs, gain_ref, shift_ref, cotangent_ref):
    conv = whole(inner_ref, outer_ref)
    sums, squares, total = merged(
        merged_moments, [[ref[i : i + 1, :] for i in range(3)] for ref in stats_refs]
    )
    center = sums / total
    inverse = lax.rsqrt(squares / total + EPSILON)
    occupied = occupied_rows(filled, conv.shape[0])
    normed = (conv - center) * inverse
    affine = gain_ref[...] * normed + shift_ref[...]
    upstream = jnp.where(occupied & (affine > 0.0), cotangent_ref[...].astype(F32), 0.0)
    return occupied, normed, affine, upstream, inverse, total


def norm_kernel(
    filled_ref, inner_ref, outer_ref, gain_ref, shift_ref, cotangent_ref, feature_ref, *refs
):
    *stats_refs, out_ref, sums_ref = refs
    occupied, normed, affine, upstream, _, _ = normalised(
        filled_ref[0], inner_ref, outer_ref, stats_refs, gain_ref, shift_ref, cotangent_ref
    )
    out = jnp.maximum(affine, 0.0) + feature_ref[...].astype(F32)
    out_ref[...] = jnp.where(occupied, out, 0.0).astype(BF16)
    sums_ref[...] = jnp.concatenate(
        [jnp.sum(upstream * normed, axis=0, keepdims=True), jnp.sum(upstream, axis=0, keepdims=True)],
        axis=0,
    )


def grad_conv_kernel(
    parts, filled_ref, inner_ref, outer_ref, gain_ref, shift_ref, cotangent_ref, *refs
):
    stats_refs, grads_refs, (grad_ref, sums_ref) = refs[:parts], refs[parts:-2], refs[-2:]
    occupied, normed, _, upstream, inverse, total = normalised(
        filled_ref[0], inner_ref, outer_ref, stats_refs, gain_ref, shift_ref, cotangent_ref
    )
    sums = merged(jnp.add, [ref[...] for ref in grads_refs])
    sums_ref[...] = sums
    grad_conv = gain_ref[...] * inverse * (
        upstream - sums[1:2, :] / total - normed * sums[0:1, :] / total
    )
    grad_ref[...] = jnp.where(occupied, grad_conv, 0.0).astype(BF16)


def gradient_kernel(
    place_ref, grad_own, grad_mate, map_own, map_mate, window_own, window_mate, *refs
):
    outs, scratch = refs[:6], refs[6:]
    index, picked, grad, product, *staged, out_sem = scratch
    keep_one, send_one, keep_two, *sends_two = staged
    rows, channels = grad_own.shape
    core = place_ref[0]
    slots = lax.broadcasted_iota(jnp.int32, (BLOCK, 3 * BLOCK), 1)
    sides = ((map_own, window_own), (map_mate, window_mate))
    grad[0:rows, :] = grad_own[...]
    grad[rows:, :] = grad_mate[...]
    for side, (map_ref, _) in enumerate(sides):
        index[side] = transposed_map(map_ref)

    def gradient(j, slot_of):
        for side, (_, window) in enumerate(sides):
            for b in range(rows // BLOCK):
                here = slice(b * BLOCK, (b + 1) * BLOCK)
                chosen = chosen_slots(slot_of(side)[here] - (rows + (b - 1) * BLOCK), slots)
                tile = window[b * BLOCK : (b + 3) * BLOCK, :]
                at = slice(side * rows + b * BLOCK, side * rows + (b + 1) * BLOCK)
                picked[j, at, :] = dot(chosen, tile, ((1,), (0,))).astype(BF16)
        product[j] = dot(picked[j], grad[...], ((0,), (0,)))

    def stored(staged, out, n):
        return pltpu.make_async_copy(staged, out, out_sem.at[n])

    shift = lax.rem(BLOCK - core * (HALF + 1), BLOCK)
    local = [pltpu.roll(index[side], shift, 1) for side in range(2)]
    size = channels // 8

    def rows_of(piece, place, size, first):
        at = lax.bitwise_xor(jnp.int32(piece), place) * size + first
        return pl.ds(pl.multiple_of(at, 16), size)

    for j in range(K_ONE):
        gradient(j, lambda side: local[side][:, j : j + 1])
        here = slice(j * size, (j + 1) * size)
        for piece in range(8):
            value = product[j, rows_of(piece, place_ref[1], size, 0), :]
            if piece < 4:
                keep_one[piece, here, :] = value
            else:
                send_one[piece - 4, here, :] = value.astype(BF16)
    copies = [stored(keep_one, outs[0], 0), stored(send_one, outs[1], 1)]
    for copy in copies:
        copy.start()
    for j in range(HALF - K_ONE + 1):
        whole_offset = j < HALF - K_ONE
        if whole_offset:
            gradient(j, lambda side: local[side][:, K_ONE + j : K_ONE + j + 1])
        else:
            gradient(j, lambda side: index[side][:, HALF : HALF + 1])
        count = size if whole_offset else size // 2
        first = 0 if whole_offset else core * (channels // 2)
        here = slice(j * size, j * size + count)
        for piece in range(8):
            value = product[j, rows_of(piece, place_ref[2], count, first), :]
            if piece < 2:
                keep_two[piece, here, :] = value
            else:
                sends_two[piece // 2 - 1][piece % 2, here, :] = value.astype(BF16)
    late = [stored(keep_two, outs[2], 2)]
    late += [stored(sends_two[n], outs[3 + n], 3 + n) for n in range(3)]
    for copy in late:
        copy.start()
    for copy in copies + late:
        copy.wait()


def scatter(step, grad, first_row, map_ref, weight_ref, windows):
    pushed = [dot(grad, weight_ref[j], ((1,), (1,))).astype(BF16) for j in range(GROUP)]
    named = [map_ref[step * GROUP + j, :][None] for j in range(GROUP)]
    for b, first_slot, sink in windows:
        rows = slice(b * BLOCK, (b + 1) * BLOCK)
        at = slice(first_row(b), first_row(b) + BLOCK)
        slots = lax.broadcasted_iota(jnp.int32, (sink.shape[0], BLOCK), 0) + first_slot
        chosen = jnp.concatenate(
            [chosen_slots(named[j][:, at], slots) for j in range(GROUP)],
            axis=1,
        )
        stacked = jnp.concatenate([pushed[j][rows] for j in range(GROUP)], axis=0)
        sink[...] = sink[...] + dot(chosen, stacked, ((1,), (0,)))


def edge_push_kernel(grad_ref, map_ref, weight_ref, before_ref, after_ref, before, after):
    step = pl.program_id(0)
    rows = map_ref.shape[1]

    @pl.when(step == 0)
    def _():
        before[...] = jnp.zeros_like(before)
        after[...] = jnp.zeros_like(after)

    def first_row(b):
        return b * (rows - BLOCK)

    windows = [(0, rows - BLOCK, before), (1, 2 * rows, after)]
    grad = jnp.concatenate([grad_ref[0:BLOCK, :], grad_ref[rows - BLOCK :, :]], axis=0)
    scatter(step, grad, first_row, map_ref, weight_ref, windows)

    @pl.when(step == pl.num_programs(0) - 1)
    def _():
        before_ref[...] = before[...].astype(BF16)
        after_ref[...] = after[...].astype(BF16)


def push_kernel(grad_ref, map_ref, weight_ref, own_ref):
    step = pl.program_id(0)
    rows = map_ref.shape[1]

    @pl.when(step == 0)
    def _():
        own_ref[...] = jnp.zeros_like(own_ref)

    windows = []
    for b in range(rows // BLOCK):
        start, stop = max(b - 1, 0) * BLOCK, min((b + 2) * BLOCK, rows)
        windows.append((b, rows + start, own_ref.at[start:stop]))
    scatter(step, grad_ref[...], lambda b: b * BLOCK, map_ref, weight_ref, windows)


def place_kernel(layout, places_ref, *refs):
    out_ref, sems = refs[-2:]
    size = out_ref.shape[1] // 8
    copies = []

    def put(source, out, part, piece, count, base):
        at = lax.bitwise_xor(jnp.int32(piece), places_ref[part]) * count + base
        here = pl.ds(pl.multiple_of(at, 16), count)
        copies.append(pltpu.make_async_copy(source, out.at[:, here, :], sems.at[len(copies)]))

    for n, (other, first_one, first_two) in enumerate(layout):
        one, two = refs[2 * n : 2 * n + 2]
        core = lax.bitwise_xor(places_ref[0], jnp.int32(other))
        first = core * (HALF + 1)
        for i in range(one.shape[0]):
            put(one.at[i], out_ref.at[pl.ds(first, K_ONE)], 1, first_one + i, size, 0)
        for i in range(two.shape[0]):
            piece = first_two + i
            source = two.at[i, pl.ds(0, (HALF - K_ONE) * size)]
            source = source.reshape(HALF - K_ONE, size, two.shape[2])
            put(source, out_ref.at[pl.ds(first + K_ONE, HALF - K_ONE)], 2, piece, size, 0)
            source = two.at[pl.ds(i, 1), pl.ds((HALF - K_ONE) * size, size // 2)]
            base = core * (out_ref.shape[1] // 2)
            put(source, out_ref.at[pl.ds(HALF, 1)], 2, piece, size // 2, base)
    for copy in copies:
        copy.start()
    for copy in copies:
        copy.wait()


def swap(value, by):
    peers = lax.axis_size("dp")
    return lax.ppermute(value, "dp", [(i, i ^ by) for i in range(peers)])


STAGES = {"c": (1,), "x": (2,), "z": (4, 8, 12)}


def part(terms, first, size):
    return functools.reduce(
        jnp.add, [term[first : first + size].astype(F32) for term in terms]
    )


def split(terms, stage):
    partners = STAGES[stage]
    size = terms[0].shape[0] // (len(partners) + 1)
    sends = [part(terms, (i + 1) * size, size).astype(BF16) for i in range(len(partners))]
    return part(terms, 0, size), sends


def swapped(sends, stage):
    return [swap(send, by) for send, by in zip(sends, STAGES[stage])]


def gather_start(piece, stage):
    return [swap(piece, by) for by in STAGES[stage]]


def summed_over_devices(one, two, grad_conv, edge_push, push, spread, finish, place):
    parts, grad_conv = lax.optimization_barrier(((one, two), grad_conv))
    received = [swapped(sends, stage) for (_, sends), stage in zip(parts, "xz")]
    edges, sink = edge_push(grad_conv), push(grad_conv)
    received, edges, sink = lax.optimization_barrier((received, edges, sink))
    parts = [
        split([kept] + got, stage) for (kept, _), got, stage in zip(parts, received, "zx")
    ]
    parts, edges = lax.optimization_barrier((parts, edges))
    received = [swapped(sends, stage) for (_, sends), stage in zip(parts, "zx")]
    halo = spread(*edges)
    received, sink = lax.optimization_barrier((received, sink))
    pieces = [part([kept] + got, 0, 1) for (kept, _), got in zip(parts, received)]
    by = 16
    while by < lax.axis_size("dp"):
        pieces = [piece + swap(piece, by) for piece in pieces]
        by *= 2
    pieces = [piece.astype(BF16) for piece in pieces]
    pieces, sink = lax.optimization_barrier((pieces, sink))
    results = finish(sink, halo)
    received = [gather_start(piece, stage) for piece, stage in zip(pieces, "zx")]
    received, pieces, results = lax.optimization_barrier((received, pieces, results))
    early = [jnp.concatenate([piece] + got, axis=0) for piece, got in zip(pieces, received)]
    received = [gather_start(piece, stage) for piece, stage in zip(early, "xz")]
    received, results = lax.optimization_barrier((received, (results, place(early))))
    late = [jnp.concatenate(got, axis=0) for got in received]
    other = [swap(jnp.concatenate(pair, axis=0), 1) for pair in zip(early, late)]
    return late, other, results


def exchanged(value, merge):
    received = [swap(value, by) for by in (1, 2, 3)]
    value = merged(merge, [value] + received)
    by = 16
    while by < lax.axis_size("dp"):
        value = merge(value, swap(value, by))
        by *= 2
    return [value] + [swap(value, by) for by in (4, 8, 12)]


def stacked_moments(one, two):
    return jnp.stack(merged_moments(one, two))


def per_device(features, kernel_map, occupancy, weights, bn_gain, bn_shift, cotangent):
    rows, channels = features.shape
    peers = lax.axis_size("dp")
    me = lax.axis_index("dp")
    blocks = rows // BLOCK
    inner_rows = rows - 2 * BLOCK
    steps = K // GROUP

    odd = me & 1
    even_pairs = [(i, i ^ 1) for i in range(peers)]
    other_pairs = [(i, ((i + 1) ^ 1) - 1) for i in range(1, peers - 1)]

    def neighbours_swap(to_before, to_after):
        even = lax.ppermute(jnp.where(odd == 1, to_before, to_after), "dp", even_pairs)
        other = lax.ppermute(jnp.where(odd == 1, to_after, to_before), "dp", other_pairs)
        return even, other

    even, other = neighbours_swap(features[:BLOCK], features[rows - BLOCK :])
    map_rows = jnp.transpose(kernel_map)
    map_mate = swap(map_rows, 1)
    odd_flag = odd.reshape(1)

    gain = bn_gain.reshape(1, channels)
    shift = bn_shift.reshape(1, channels)
    smem = pl.BlockSpec(memory_space=pltpu.SMEM)
    vmem = pl.BlockSpec(memory_space=pltpu.VMEM)
    hbm = pl.BlockSpec(memory_space=pltpu.HBM)
    anywhere = pl.BlockSpec(memory_space=pl.ANY)
    groups = K // GROUP
    work = K * rows * channels * 2 * (3 * BLOCK + channels)
    moved = K * channels * channels * 2 * 3

    half_conv = jax.ShapeDtypeStruct((2 * BLOCK, channels), F32)
    scratch = [
        pltpu.VMEM((K, 2 * BLOCK), jnp.int32),
        pltpu.VMEM((K, channels, channels), BF16),
        pltpu.VMEM((GROUP, 2 * BLOCK, channels), BF16),
        pltpu.VMEM((2 * BLOCK, BLOCK), jnp.int32),
        pltpu.SemaphoreType.DMA((groups,)),
    ]

    def in_hbm(value):
        return pltpu.with_memory_space_constraint(value, pltpu.HBM)

    inner = pl.pallas_call(
        inner_kernel,
        in_specs=[vmem, vmem, hbm],
        out_specs=vmem,
        out_shape=half_conv,
        scratch_shapes=scratch,
        compiler_params=params(LIMIT),
        cost_estimate=cost(work / 2, moved),
        name="conv_inner",
    )(in_hbm(map_rows), in_hbm(features), in_hbm(weights))

    outer, stats, window = pl.pallas_call(
        outer_kernel,
        in_specs=[smem, smem, vmem, vmem, vmem, vmem, vmem, hbm],
        out_specs=[vmem, vmem, vmem],
        out_shape=[
            half_conv,
            jax.ShapeDtypeStruct((3, channels), F32),
            jax.ShapeDtypeStruct((rows + 2 * BLOCK, channels), BF16),
        ],
        scratch_shapes=scratch,
        compiler_params=params(LIMIT),
        cost_estimate=cost(work / 2, moved),
        name="conv_outer",
    )(occupancy, odd_flag, map_rows, features, even, other, inner, in_hbm(weights))

    window_mate = swap(window, 1)
    stats = exchanged(stats, stacked_moments)

    block_out, sums = pl.pallas_call(
        norm_kernel,
        in_specs=[smem] + [vmem] * 10,
        out_shape=[
            jax.ShapeDtypeStruct((rows, channels), BF16),
            jax.ShapeDtypeStruct((2, channels), F32),
        ],
        compiler_params=params(LIMIT),
        cost_estimate=cost(rows * channels * 20, rows * channels * 10),
        name="norm",
    )(occupancy, inner, outer, gain, shift, cotangent, features, *stats)

    grads = exchanged(sums, jnp.add)

    grad_conv, sums = pl.pallas_call(
        functools.partial(grad_conv_kernel, len(stats)),
        in_specs=[smem] + [vmem] * 13,
        out_shape=[
            jax.ShapeDtypeStruct((rows, channels), BF16),
            jax.ShapeDtypeStruct((2, channels), F32),
        ],
        compiler_params=params(LIMIT),
        cost_estimate=cost(rows * channels * 20, rows * channels * 8),
        name="grad_conv",
    )(occupancy, inner, outer, gain, shift, cotangent, *stats, *grads)
    grad_mate = swap(grad_conv, 1)

    core, lane, depth = me & 1, (me >> 1) & 1, (me >> 2) & 3
    places = jnp.stack([core, lane * 4 + depth, depth * 2 + lane])
    size = channels // 8
    rows_one, rows_two = K_ONE * size, (HALF - K_ONE) * size + size // 2
    shapes = [((4, rows_one, channels), F32), ((4, rows_one, channels), BF16)]
    shapes += [((2, rows_two, channels), F32)] + [((2, rows_two, channels), BF16)] * 3
    keep_one, send_one, keep_two, *sends_two = pl.pallas_call(
        gradient_kernel,
        in_specs=[smem] + [vmem] * 6,
        out_specs=[anywhere] * 6,
        out_shape=[jax.ShapeDtypeStruct(*shape) for shape in shapes],
        scratch_shapes=[
            pltpu.VMEM((2, rows, BLOCK), jnp.int32),
            pltpu.VMEM((K_ONE, 2 * rows, channels), BF16),
            pltpu.VMEM((2 * rows, channels), BF16),
            pltpu.VMEM((K_ONE, channels, channels), F32),
        ]
        + [pltpu.VMEM(*shape) for shape in shapes]
        + [pltpu.SemaphoreType.DMA((6,))],
        compiler_params=params(LIMIT),
        cost_estimate=cost(work, K * channels * channels * 6),
        name="weight_gradient",
    )(places, grad_conv, grad_mate, map_rows, map_mate, window, window_mate)
    one, two = (keep_one, [send_one]), (keep_two, sends_two)

    weight_spec = pl.BlockSpec((GROUP, channels, channels), lambda s: (s, 0, 0))

    push_grid = dict(
        grid=(groups,),
        compiler_params=params(LIMIT),
        cost_estimate=cost(1000, 1000),
    )

    def edge_push(grad_conv):
        edge = jax.ShapeDtypeStruct((BLOCK, channels), BF16)
        before, after = pl.pallas_call(
            edge_push_kernel,
            in_specs=[full((rows, channels)), full((K, rows)), weight_spec],
            out_specs=[full((BLOCK, channels))] * 2,
            out_shape=[edge, edge],
            scratch_shapes=[pltpu.VMEM((BLOCK, channels), F32)] * 2,
            name="push_edges",
            **push_grid,
        )(grad_conv, map_rows, weights)
        return before, after

    def push(grad_conv):
        return pl.pallas_call(
            push_kernel,
            in_specs=[full((rows, channels)), full((K, rows)), weight_spec],
            out_specs=full((rows, channels)),
            out_shape=jax.ShapeDtypeStruct((rows, channels), F32),
            name="push",
            **push_grid,
        )(grad_conv, map_rows, weights)

    def finish(sink, halo):
        even, other = halo
        from_prev = jnp.where(odd == 1, even, other).astype(F32)
        from_next = jnp.where(odd == 1, other, even).astype(F32)
        occupied = occupied_rows(occupancy[0], rows)
        received = jnp.concatenate(
            [
                sink[:BLOCK] + from_prev,
                sink[BLOCK : rows - BLOCK],
                sink[rows - BLOCK :] + from_next,
            ],
            axis=0,
        )
        total = jnp.where(occupied, cotangent.astype(F32), 0.0) + received
        return total.astype(BF16), sums[0], sums[1]


    def placed(layout, sources, *into):
        count = sum(one.shape[0] + two.shape[0] * 2 for one, two in sources)
        operands = []
        for one, two in sources:
            operands += [one.reshape(one.shape[0], K_ONE, size, channels), two]
        return pl.pallas_call(
            functools.partial(place_kernel, layout),
            in_specs=[smem] + [anywhere] * len(operands) + [hbm] * len(into),
            out_specs=hbm,
            out_shape=jax.ShapeDtypeStruct(weights.shape, BF16),
            scratch_shapes=[pltpu.SemaphoreType.DMA((count,))],
            input_output_aliases={len(operands) + 1: 0} if into else {},
            compiler_params=params(LIMIT),
            cost_estimate=cost(0, K * channels * channels * 2),
            name="place",
        )(places, *operands, *into)

    def place_early(own):
        return placed(((0, 0, 0),), (own,))

    late, other_pieces, results = summed_over_devices(
        one, two, grad_conv, edge_push, push, neighbours_swap, finish, place_early
    )
    (grad_features, grad_gain, grad_shift), grad_weights = results
    first_late = (8 - late[0].shape[0], 8 - late[1].shape[0])
    grad_weights = placed(((0, *first_late),), (late,), grad_weights)
    grad_weights = placed(((1, 0, 0),), (other_pieces,), grad_weights)
    return block_out, grad_features, grad_weights, grad_gain, grad_shift


def solution(mesh):
    in_specs = (
        P(("parts", "dp"), None),
        P(("parts", "dp"), None),
        P(("parts", "dp")),
        P(),
        P(),
        P(),
        P(("parts", "dp"), None),
    )
    out_specs = (
        P(("parts", "dp"), None),
        P(("parts", "dp"), None),
        P("parts", None, None),
        P("parts"),
        P("parts"),
    )
    return jax.shard_map(
        per_device, mesh=mesh, in_specs=in_specs, out_specs=out_specs, check_vma=False
    )
```

```python
import functools

import jax
import jax.numpy as jnp
from jax import lax
from jax.experimental import pallas as pl
from jax.experimental.pallas import tpu as pltpu
from jax.sharding import PartitionSpec as P

K = 27
BLOCK = 128
GROUP = 9
HALF = 13
K_ONE = 9
EPSILON = 1e-05
F32 = jnp.float32
BF16 = jnp.bfloat16
LIMIT = 24 * 1024 * 1024


def merged(merge, values):
    return merge(merge(values[0], values[1]), merge(values[2], values[3]))


def merged_moments(one, two):
    (sum_one, square_one, count_one), (sum_two, square_two, count_two) = one, two
    away = sum_one / count_one - sum_two / count_two
    count = count_one + count_two
    square = (square_one + square_two) + away * away * (count_one * count_two / count)
    return sum_one + sum_two, square, count


def dot(a, b, contract):
    return lax.dot_general(a, b, ((contract[0], contract[1]), ((), ())), preferred_element_type=F32)


def full(shape):
    return pl.BlockSpec(shape, lambda *_: (0,) * len(shape))


def params(limit):
    return pltpu.CompilerParams(vmem_limit_bytes=limit)


def cost(flops, moved):
    return pl.CostEstimate(flops=int(flops), bytes_accessed=int(moved), transcendentals=0)


def occupied_rows(filled, rows):
    position = lax.broadcasted_iota(jnp.int32, (rows, 1), 0)
    return (position < filled - BLOCK) | (position >= rows - BLOCK)


def chosen_slots(slot, slots):
    return jnp.where(slot == slots, 1.0, 0.0).astype(BF16)


def transposed_map(map_ref):
    spare = jnp.zeros((BLOCK - K, map_ref.shape[1]), jnp.int32)
    return jnp.transpose(jnp.concatenate([map_ref[...], spare], axis=0))


def convolve(map_ref, tiles, first_slots, weight_hbm, conv_ref, scratch):
    weight, picked, index, weight_sem = scratch
    groups = K // GROUP

    def fetch(g):
        here = pl.ds(g * GROUP, GROUP)
        return pltpu.make_async_copy(weight_hbm.at[here], weight.at[here], weight_sem.at[g])

    for g in range(groups):
        fetch(g).start()
    index[...] = transposed_map(map_ref)
    conv_ref[...] = jnp.zeros_like(conv_ref)
    slots = lax.broadcasted_iota(jnp.int32, (BLOCK, 3 * BLOCK), 1)

    def group(g, carry):
        local = pltpu.roll(index[...], lax.rem(BLOCK - g * GROUP, BLOCK), 1)
        for b, tile in enumerate(tiles):
            here = slice(b * BLOCK, (b + 1) * BLOCK)
            slot = local[here] - first_slots[b]
            for j in range(GROUP):
                chosen = chosen_slots(slot[:, j : j + 1], slots)
                picked[j, here, :] = dot(chosen, tile[...], ((1,), (0,))).astype(BF16)
        fetch(g).wait()
        total = conv_ref[...]
        for j in range(GROUP):
            total = total + dot(picked[j], weight[g * GROUP + j], ((1,), (0,)))
        conv_ref[...] = total
        return carry

    lax.fori_loop(0, groups, group, 0)


def inner_kernel(map_ref, own_ref, weight_hbm, conv_ref, chosen_map, *scratch):
    rows = own_ref.shape[0]
    chosen_map[...] = map_ref[:, BLOCK : rows - BLOCK]
    blocks = range(1, rows // BLOCK - 1)
    tiles = [own_ref.at[(b - 1) * BLOCK : (b + 2) * BLOCK] for b in blocks]
    first_slots = [rows - BLOCK + b * BLOCK for b in blocks]
    convolve(chosen_map, tiles, first_slots, weight_hbm, conv_ref, scratch)


def outer_kernel(
    filled_ref, odd_ref, map_ref, own_ref, even_ref, other_ref, inner_ref, weight_hbm,
    conv_ref, stats_ref, window_ref, chosen_map, *scratch,
):
    rows = own_ref.shape[0]
    odd = odd_ref[0] == 1
    window_ref[0:BLOCK, :] = jnp.where(odd, even_ref[...], other_ref[...])
    window_ref[BLOCK : rows + BLOCK, :] = own_ref[...]
    window_ref[rows + BLOCK :, :] = jnp.where(odd, other_ref[...], even_ref[...])
    chosen_map[:, 0:BLOCK] = map_ref[:, 0:BLOCK]
    chosen_map[:, BLOCK:] = map_ref[:, rows - BLOCK :]
    tiles = [window_ref.at[0 : 3 * BLOCK], window_ref.at[rows - BLOCK :]]
    first_slots = [rows - BLOCK, 2 * rows - 2 * BLOCK]
    convolve(chosen_map, tiles, first_slots, weight_hbm, conv_ref, scratch)
    filled = filled_ref[0]
    count = filled.astype(F32)
    conv = whole(inner_ref, conv_ref)
    occupied = occupied_rows(filled, rows)
    sums = jnp.sum(jnp.where(occupied, conv, 0.0), axis=0, keepdims=True)
    off = jnp.where(occupied, conv - sums / count, 0.0)
    squares = jnp.sum(off * off, axis=0, keepdims=True)
    stats_ref[...] = jnp.concatenate([sums, squares, jnp.full_like(sums, count)], axis=0)


def whole(inner_ref, outer_ref):
    return jnp.concatenate([outer_ref[0:BLOCK, :], inner_ref[...], outer_ref[BLOCK:, :]], axis=0)


def normalised(filled, inner_ref, outer_ref, stats_refs, gain_ref, shift_ref, cotangent_ref):
    conv = whole(inner_ref, outer_ref)
    sums, squares, total = merged(
        merged_moments, [[ref[i : i + 1, :] for i in range(3)] for ref in stats_refs]
    )
    center = sums / total
    inverse = lax.rsqrt(squares / total + EPSILON)
    occupied = occupied_rows(filled, conv.shape[0])
    normed = (conv - center) * inverse
    affine = gain_ref[...] * normed + shift_ref[...]
    upstream = jnp.where(occupied & (affine > 0.0), cotangent_ref[...].astype(F32), 0.0)
    return occupied, normed, affine, upstream, inverse, total


def norm_kernel(
    filled_ref, inner_ref, outer_ref, gain_ref, shift_ref, cotangent_ref, feature_ref, *refs
):
    *stats_refs, out_ref, sums_ref = refs
    occupied, normed, affine, upstream, _, _ = normalised(
        filled_ref[0], inner_ref, outer_ref, stats_refs, gain_ref, shift_ref, cotangent_ref
    )
    out = jnp.maximum(affine, 0.0) + feature_ref[...].astype(F32)
    out_ref[...] = jnp.where(occupied, out, 0.0).astype(BF16)
    sums_ref[...] = jnp.concatenate(
        [jnp.sum(upstream * normed, axis=0, keepdims=True), jnp.sum(upstream, axis=0, keepdims=True)],
        axis=0,
    )


def grad_conv_kernel(
    parts, filled_ref, inner_ref, outer_ref, gain_ref, shift_ref, cotangent_ref, *refs
):
    stats_refs, grads_refs, (grad_ref, sums_ref) = refs[:parts], refs[parts:-2], refs[-2:]
    occupied, normed, _, upstream, inverse, total = normalised(
        filled_ref[0], inner_ref, outer_ref, stats_refs, gain_ref, shift_ref, cotangent_ref
    )
    sums = merged(jnp.add, [ref[...] for ref in grads_refs])
    sums_ref[...] = sums
    grad_conv = gain_ref[...] * inverse * (
        upstream - sums[1:2, :] / total - normed * sums[0:1, :] / total
    )
    grad_ref[...] = jnp.where(occupied, grad_conv, 0.0).astype(BF16)


def gradient_kernel(
    place_ref, grad_own, grad_mate, map_own, map_mate, window_own, window_mate, *refs
):
    outs, scratch = refs[:6], refs[6:]
    index, picked, grad, turned, product, *staged, out_sem = scratch
    keep_one, send_one, keep_two, *sends_two = staged
    rows, channels = grad_own.shape
    core = place_ref[0]
    slots = lax.broadcasted_iota(jnp.int32, (BLOCK, 3 * BLOCK), 1)
    sides = ((map_own, window_own), (map_mate, window_mate))
    grad[0:rows, :] = grad_own[...]
    grad[rows:, :] = grad_mate[...]
    turned[...] = jnp.transpose(grad[...].astype(F32)).astype(BF16)
    for side, (map_ref, _) in enumerate(sides):
        index[side] = transposed_map(map_ref)

    def gradient(j, slot_of):
        for side, (_, window) in enumerate(sides):
            for b in range(rows // BLOCK):
                here = slice(b * BLOCK, (b + 1) * BLOCK)
                chosen = chosen_slots(slot_of(side)[here] - (rows + (b - 1) * BLOCK), slots)
                tile = window[b * BLOCK : (b + 3) * BLOCK, :]
                at = slice(side * rows + b * BLOCK, side * rows + (b + 1) * BLOCK)
                picked[j, at, :] = dot(chosen, tile, ((1,), (0,))).astype(BF16)
        product[j] = jnp.transpose(dot(turned[...], picked[j], ((1,), (0,))))

    def stored(staged, out, n):
        return pltpu.make_async_copy(staged, out, out_sem.at[n])

    shift = lax.rem(BLOCK - core * (HALF + 1), BLOCK)
    local = [pltpu.roll(index[side], shift, 1) for side in range(2)]
    size = channels // 8

    def rows_of(piece, place, size, first):
        at = lax.bitwise_xor(jnp.int32(piece), place) * size + first
        return pl.ds(pl.multiple_of(at, 16), size)

    for j in range(K_ONE):
        gradient(j, lambda side: local[side][:, j : j + 1])
        here = slice(j * size, (j + 1) * size)
        for piece in range(8):
            value = product[j, rows_of(piece, place_ref[1], size, 0), :]
            if piece < 4:
                keep_one[piece, here, :] = value
            else:
                send_one[piece - 4, here, :] = value.astype(BF16)
    copies = [stored(keep_one, outs[0], 0), stored(send_one, outs[1], 1)]
    for copy in copies:
        copy.start()
    for j in range(HALF - K_ONE + 1):
        whole_offset = j < HALF - K_ONE
        if whole_offset:
            gradient(j, lambda side: local[side][:, K_ONE + j : K_ONE + j + 1])
        else:
            gradient(j, lambda side: index[side][:, HALF : HALF + 1])
        count = size if whole_offset else size // 2
        first = 0 if whole_offset else core * (channels // 2)
        here = slice(j * size, j * size + count)
        for piece in range(8):
            value = product[j, rows_of(piece, place_ref[2], count, first), :]
            if piece < 2:
                keep_two[piece, here, :] = value
            else:
                sends_two[piece // 2 - 1][piece % 2, here, :] = value.astype(BF16)
    late = [stored(keep_two, outs[2], 2)]
    late += [stored(sends_two[n], outs[3 + n], 3 + n) for n in range(3)]
    for copy in late:
        copy.start()
    for copy in copies + late:
        copy.wait()


def scatter(step, grad, first_row, map_ref, weight_ref, windows):
    pushed = [dot(grad, weight_ref[j], ((1,), (1,))).astype(BF16) for j in range(GROUP)]
    named = [map_ref[step * GROUP + j, :][None] for j in range(GROUP)]
    for b, first_slot, sink in windows:
        rows = slice(b * BLOCK, (b + 1) * BLOCK)
        at = slice(first_row(b), first_row(b) + BLOCK)
        slots = lax.broadcasted_iota(jnp.int32, (sink.shape[0], BLOCK), 0) + first_slot
        chosen = jnp.concatenate(
            [chosen_slots(named[j][:, at], slots) for j in range(GROUP)],
            axis=1,
        )
        stacked = jnp.concatenate([pushed[j][rows] for j in range(GROUP)], axis=0)
        sink[...] = sink[...] + dot(chosen, stacked, ((1,), (0,)))


def edge_push_kernel(grad_ref, map_ref, weight_ref, before_ref, after_ref, before, after):
    step = pl.program_id(0)
    rows = map_ref.shape[1]

    @pl.when(step == 0)
    def _():
        before[...] = jnp.zeros_like(before)
        after[...] = jnp.zeros_like(after)

    def first_row(b):
        return b * (rows - BLOCK)

    windows = [(0, rows - BLOCK, before), (1, 2 * rows, after)]
    grad = jnp.concatenate([grad_ref[0:BLOCK, :], grad_ref[rows - BLOCK :, :]], axis=0)
    scatter(step, grad, first_row, map_ref, weight_ref, windows)

    @pl.when(step == pl.num_programs(0) - 1)
    def _():
        before_ref[...] = before[...].astype(BF16)
        after_ref[...] = after[...].astype(BF16)


def push_kernel(grad_ref, map_ref, weight_ref, own_ref):
    step = pl.program_id(0)
    rows = map_ref.shape[1]

    @pl.when(step == 0)
    def _():
        own_ref[...] = jnp.zeros_like(own_ref)

    windows = []
    for b in range(rows // BLOCK):
        start, stop = max(b - 1, 0) * BLOCK, min((b + 2) * BLOCK, rows)
        windows.append((b, rows + start, own_ref.at[start:stop]))
    scatter(step, grad_ref[...], lambda b: b * BLOCK, map_ref, weight_ref, windows)


def place_kernel(layout, places_ref, *refs):
    out_ref, sems = refs[-2:]
    size = out_ref.shape[1] // 8
    copies = []

    def put(source, out, part, piece, count, base):
        at = lax.bitwise_xor(jnp.int32(piece), places_ref[part]) * count + base
        here = pl.ds(pl.multiple_of(at, 16), count)
        copies.append(pltpu.make_async_copy(source, out.at[:, here, :], sems.at[len(copies)]))

    for n, (other, first_one, first_two) in enumerate(layout):
        one, two = refs[2 * n : 2 * n + 2]
        core = lax.bitwise_xor(places_ref[0], jnp.int32(other))
        first = core * (HALF + 1)
        for i in range(one.shape[0]):
            put(one.at[i], out_ref.at[pl.ds(first, K_ONE)], 1, first_one + i, size, 0)
        for i in range(two.shape[0]):
            piece = first_two + i
            source = two.at[i, pl.ds(0, (HALF - K_ONE) * size)]
            source = source.reshape(HALF - K_ONE, size, two.shape[2])
            put(source, out_ref.at[pl.ds(first + K_ONE, HALF - K_ONE)], 2, piece, size, 0)
            source = two.at[pl.ds(i, 1), pl.ds((HALF - K_ONE) * size, size // 2)]
            base = core * (out_ref.shape[1] // 2)
            put(source, out_ref.at[pl.ds(HALF, 1)], 2, piece, size // 2, base)
    for copy in copies:
        copy.start()
    for copy in copies:
        copy.wait()


def swap(value, by):
    peers = lax.axis_size("dp")
    return lax.ppermute(value, "dp", [(i, i ^ by) for i in range(peers)])


STAGES = {"c": (1,), "x": (2,), "z": (4, 8, 12)}


def part(terms, first, size):
    return functools.reduce(
        jnp.add, [term[first : first + size].astype(F32) for term in terms]
    )


def split(terms, stage):
    partners = STAGES[stage]
    size = terms[0].shape[0] // (len(partners) + 1)
    sends = [part(terms, (i + 1) * size, size).astype(BF16) for i in range(len(partners))]
    return part(terms, 0, size), sends


def swapped(sends, stage):
    return [swap(send, by) for send, by in zip(sends, STAGES[stage])]


def gather_start(piece, stage):
    return [swap(piece, by) for by in STAGES[stage]]


def summed_over_devices(one, two, grad_conv, edge_push, push, spread, finish, place):
    parts, grad_conv = lax.optimization_barrier(((one, two), grad_conv))
    received = [swapped(sends, stage) for (_, sends), stage in zip(parts, "xz")]
    edges, sink = edge_push(grad_conv), push(grad_conv)
    received, edges, sink = lax.optimization_barrier((received, edges, sink))
    parts = [
        split([kept] + got, stage) for (kept, _), got, stage in zip(parts, received, "zx")
    ]
    parts, edges = lax.optimization_barrier((parts, edges))
    received = [swapped(sends, stage) for (_, sends), stage in zip(parts, "zx")]
    halo = spread(*edges)
    received, sink = lax.optimization_barrier((received, sink))
    pieces = [part([kept] + got, 0, 1) for (kept, _), got in zip(parts, received)]
    by = 16
    while by < lax.axis_size("dp"):
        pieces = [piece + swap(piece, by) for piece in pieces]
        by *= 2
    pieces = [piece.astype(BF16) for piece in pieces]
    pieces, sink = lax.optimization_barrier((pieces, sink))
    results = finish(sink, halo)
    received = [gather_start(piece, stage) for piece, stage in zip(pieces, "zx")]
    received, pieces, results = lax.optimization_barrier((received, pieces, results))
    early = [jnp.concatenate([piece] + got, axis=0) for piece, got in zip(pieces, received)]
    received = [gather_start(piece, stage) for piece, stage in zip(early, "xz")]
    received, results = lax.optimization_barrier((received, (results, place(early))))
    late = [jnp.concatenate(got, axis=0) for got in received]
    other = [swap(jnp.concatenate(pair, axis=0), 1) for pair in zip(early, late)]
    return late, other, results


def exchanged(value, merge):
    received = [swap(value, by) for by in (1, 2, 3)]
    value = merged(merge, [value] + received)
    by = 16
    while by < lax.axis_size("dp"):
        value = merge(value, swap(value, by))
        by *= 2
    return [value] + [swap(value, by) for by in (4, 8, 12)]


def stacked_moments(one, two):
    return jnp.stack(merged_moments(one, two))


def per_device(features, kernel_map, occupancy, weights, bn_gain, bn_shift, cotangent):
    rows, channels = features.shape
    peers = lax.axis_size("dp")
    me = lax.axis_index("dp")
    blocks = rows // BLOCK
    inner_rows = rows - 2 * BLOCK
    steps = K // GROUP

    odd = me & 1
    even_pairs = [(i, i ^ 1) for i in range(peers)]
    other_pairs = [(i, ((i + 1) ^ 1) - 1) for i in range(1, peers - 1)]

    def neighbours_swap(to_before, to_after):
        even = lax.ppermute(jnp.where(odd == 1, to_before, to_after), "dp", even_pairs)
        other = lax.ppermute(jnp.where(odd == 1, to_after, to_before), "dp", other_pairs)
        return even, other

    even, other = neighbours_swap(features[:BLOCK], features[rows - BLOCK :])
    map_rows = jnp.transpose(kernel_map)
    map_mate = swap(map_rows, 1)
    odd_flag = odd.reshape(1)

    gain = bn_gain.reshape(1, channels)
    shift = bn_shift.reshape(1, channels)
    smem = pl.BlockSpec(memory_space=pltpu.SMEM)
    vmem = pl.BlockSpec(memory_space=pltpu.VMEM)
    hbm = pl.BlockSpec(memory_space=pltpu.HBM)
    anywhere = pl.BlockSpec(memory_space=pl.ANY)
    groups = K // GROUP
    work = K * rows * channels * 2 * (3 * BLOCK + channels)
    moved = K * channels * channels * 2 * 3

    half_conv = jax.ShapeDtypeStruct((2 * BLOCK, channels), F32)
    scratch = [
        pltpu.VMEM((K, 2 * BLOCK), jnp.int32),
        pltpu.VMEM((K, channels, channels), BF16),
        pltpu.VMEM((GROUP, 2 * BLOCK, channels), BF16),
        pltpu.VMEM((2 * BLOCK, BLOCK), jnp.int32),
        pltpu.SemaphoreType.DMA((groups,)),
    ]

    def in_hbm(value):
        return pltpu.with_memory_space_constraint(value, pltpu.HBM)

    inner = pl.pallas_call(
        inner_kernel,
        in_specs=[vmem, vmem, hbm],
        out_specs=vmem,
        out_shape=half_conv,
        scratch_shapes=scratch,
        compiler_params=params(LIMIT),
        cost_estimate=cost(work / 2, moved),
        name="conv_inner",
    )(in_hbm(map_rows), in_hbm(features), in_hbm(weights))

    outer, stats, window = pl.pallas_call(
        outer_kernel,
        in_specs=[smem, smem, vmem, vmem, vmem, vmem, vmem, hbm],
        out_specs=[vmem, vmem, vmem],
        out_shape=[
            half_conv,
            jax.ShapeDtypeStruct((3, channels), F32),
            jax.ShapeDtypeStruct((rows + 2 * BLOCK, channels), BF16),
        ],
        scratch_shapes=scratch,
        compiler_params=params(LIMIT),
        cost_estimate=cost(work / 2, moved),
        name="conv_outer",
    )(occupancy, odd_flag, map_rows, features, even, other, inner, in_hbm(weights))

    window_mate = swap(window, 1)
    stats = exchanged(stats, stacked_moments)

    block_out, sums = pl.pallas_call(
        norm_kernel,
        in_specs=[smem] + [vmem] * 10,
        out_shape=[
            jax.ShapeDtypeStruct((rows, channels), BF16),
            jax.ShapeDtypeStruct((2, channels), F32),
        ],
        compiler_params=params(LIMIT),
        cost_estimate=cost(rows * channels * 20, rows * channels * 10),
        name="norm",
    )(occupancy, inner, outer, gain, shift, cotangent, features, *stats)

    grads = exchanged(sums, jnp.add)

    grad_conv, sums = pl.pallas_call(
        functools.partial(grad_conv_kernel, len(stats)),
        in_specs=[smem] + [vmem] * 13,
        out_shape=[
            jax.ShapeDtypeStruct((rows, channels), BF16),
            jax.ShapeDtypeStruct((2, channels), F32),
        ],
        compiler_params=params(LIMIT),
        cost_estimate=cost(rows * channels * 20, rows * channels * 8),
        name="grad_conv",
    )(occupancy, inner, outer, gain, shift, cotangent, *stats, *grads)
    grad_mate = swap(grad_conv, 1)

    core, lane, depth = me & 1, (me >> 1) & 1, (me >> 2) & 3
    places = jnp.stack([core, lane * 4 + depth, depth * 2 + lane])
    size = channels // 8
    rows_one, rows_two = K_ONE * size, (HALF - K_ONE) * size + size // 2
    shapes = [((4, rows_one, channels), F32), ((4, rows_one, channels), BF16)]
    shapes += [((2, rows_two, channels), F32)] + [((2, rows_two, channels), BF16)] * 3
    keep_one, send_one, keep_two, *sends_two = pl.pallas_call(
        gradient_kernel,
        in_specs=[smem] + [vmem] * 6,
        out_specs=[anywhere] * 6,
        out_shape=[jax.ShapeDtypeStruct(*shape) for shape in shapes],
        scratch_shapes=[
            pltpu.VMEM((2, rows, BLOCK), jnp.int32),
            pltpu.VMEM((K_ONE, 2 * rows, channels), BF16),
            pltpu.VMEM((2 * rows, channels), BF16),
            pltpu.VMEM((channels, 2 * rows), BF16),
            pltpu.VMEM((K_ONE, channels, channels), F32),
        ]
        + [pltpu.VMEM(*shape) for shape in shapes]
        + [pltpu.SemaphoreType.DMA((6,))],
        compiler_params=params(LIMIT),
        cost_estimate=cost(work, K * channels * channels * 6),
        name="weight_gradient",
    )(places, grad_conv, grad_mate, map_rows, map_mate, window, window_mate)
    one, two = (keep_one, [send_one]), (keep_two, sends_two)

    weight_spec = pl.BlockSpec((GROUP, channels, channels), lambda s: (s, 0, 0))

    push_grid = dict(
        grid=(groups,),
        compiler_params=params(LIMIT),
        cost_estimate=cost(1000, 1000),
    )

    def edge_push(grad_conv):
        edge = jax.ShapeDtypeStruct((BLOCK, channels), BF16)
        before, after = pl.pallas_call(
            edge_push_kernel,
            in_specs=[full((rows, channels)), full((K, rows)), weight_spec],
            out_specs=[full((BLOCK, channels))] * 2,
            out_shape=[edge, edge],
            scratch_shapes=[pltpu.VMEM((BLOCK, channels), F32)] * 2,
            name="push_edges",
            **push_grid,
        )(grad_conv, map_rows, weights)
        return before, after

    def push(grad_conv):
        return pl.pallas_call(
            push_kernel,
            in_specs=[full((rows, channels)), full((K, rows)), weight_spec],
            out_specs=full((rows, channels)),
            out_shape=jax.ShapeDtypeStruct((rows, channels), F32),
            name="push",
            **push_grid,
        )(grad_conv, map_rows, weights)

    def finish(sink, halo):
        even, other = halo
        from_prev = jnp.where(odd == 1, even, other).astype(F32)
        from_next = jnp.where(odd == 1, other, even).astype(F32)
        occupied = occupied_rows(occupancy[0], rows)
        received = jnp.concatenate(
            [
                sink[:BLOCK] + from_prev,
                sink[BLOCK : rows - BLOCK],
                sink[rows - BLOCK :] + from_next,
            ],
            axis=0,
        )
        total = jnp.where(occupied, cotangent.astype(F32), 0.0) + received
        return total.astype(BF16), sums[0], sums[1]


    def placed(layout, sources, *into):
        count = sum(one.shape[0] + two.shape[0] * 2 for one, two in sources)
        operands = []
        for one, two in sources:
            operands += [one.reshape(one.shape[0], K_ONE, size, channels), two]
        return pl.pallas_call(
            functools.partial(place_kernel, layout),
            in_specs=[smem] + [anywhere] * len(operands) + [hbm] * len(into),
            out_specs=hbm,
            out_shape=jax.ShapeDtypeStruct(weights.shape, BF16),
            scratch_shapes=[pltpu.SemaphoreType.DMA((count,))],
            input_output_aliases={len(operands) + 1: 0} if into else {},
            compiler_params=params(LIMIT),
            cost_estimate=cost(0, K * channels * channels * 2),
            name="place",
        )(places, *operands, *into)

    def place_early(own):
        return placed(((0, 0, 0),), (own,))

    late, other_pieces, results = summed_over_devices(
        one, two, grad_conv, edge_push, push, neighbours_swap, finish, place_early
    )
    (grad_features, grad_gain, grad_shift), grad_weights = results
    first_late = (8 - late[0].shape[0], 8 - late[1].shape[0])
    grad_weights = placed(((0, *first_late),), (late,), grad_weights)
    grad_weights = placed(((1, 0, 0),), (other_pieces,), grad_weights)
    return block_out, grad_features, grad_weights, grad_gain, grad_shift


def solution(mesh):
    in_specs = (
        P(("parts", "dp"), None),
        P(("parts", "dp"), None),
        P(("parts", "dp")),
        P(),
        P(),
        P(),
        P(("parts", "dp"), None),
    )
    out_specs = (
        P(("parts", "dp"), None),
        P(("parts", "dp"), None),
        P("parts", None, None),
        P("parts"),
        P("parts"),
    )
    return jax.shard_map(
        per_device, mesh=mesh, in_specs=in_specs, out_specs=out_specs, check_vma=False
    )
```

```python
import functools

import jax
import jax.numpy as jnp
from jax import lax
from jax.experimental import pallas as pl
from jax.experimental.pallas import tpu as pltpu
from jax.sharding import PartitionSpec as P

K = 27
BLOCK = 128
GROUP = 9
HALF = 13
K_ONE = 9
EPSILON = 1e-05
F32 = jnp.float32
BF16 = jnp.bfloat16
LIMIT = 24 * 1024 * 1024


def merged(merge, values):
    return merge(merge(values[0], values[1]), merge(values[2], values[3]))


def merged_moments(one, two):
    (sum_one, square_one, count_one), (sum_two, square_two, count_two) = one, two
    away = sum_one / count_one - sum_two / count_two
    count = count_one + count_two
    square = (square_one + square_two) + away * away * (count_one * count_two / count)
    return sum_one + sum_two, square, count


def dot(a, b, contract):
    return lax.dot_general(a, b, ((contract[0], contract[1]), ((), ())), preferred_element_type=F32)


def full(shape):
    return pl.BlockSpec(shape, lambda *_: (0,) * len(shape))


def params(limit):
    return pltpu.CompilerParams(vmem_limit_bytes=limit)


def cost(flops, moved):
    return pl.CostEstimate(flops=int(flops), bytes_accessed=int(moved), transcendentals=0)


def occupied_rows(filled, rows):
    position = lax.broadcasted_iota(jnp.int32, (rows, 1), 0)
    return (position < filled - BLOCK) | (position >= rows - BLOCK)


def chosen_slots(slot, slots):
    one = jnp.ones((), BF16 if slots.dtype == jnp.int16 else F32)
    return jnp.where(slot == slots, one, jnp.zeros_like(one)).astype(BF16)


def transposed_map(map_ref):
    spare = jnp.zeros((BLOCK - K, map_ref.shape[1]), jnp.int32)
    return jnp.transpose(jnp.concatenate([map_ref[...], spare], axis=0))


def convolve(map_ref, tiles, first_slots, weight_hbm, conv_ref, scratch):
    weight, picked, index, weight_sem = scratch
    groups = K // GROUP

    def fetch(g):
        here = pl.ds(g * GROUP, GROUP)
        return pltpu.make_async_copy(weight_hbm.at[here], weight.at[here], weight_sem.at[g])

    for g in range(groups):
        fetch(g).start()
    index[...] = transposed_map(map_ref)
    conv_ref[...] = jnp.zeros_like(conv_ref)
    slots = lax.broadcasted_iota(jnp.int32, (BLOCK, 3 * BLOCK), 1)

    def group(g, carry):
        local = pltpu.roll(index[...], lax.rem(BLOCK - g * GROUP, BLOCK), 1)
        for b, tile in enumerate(tiles):
            here = slice(b * BLOCK, (b + 1) * BLOCK)
            slot = local[here] - first_slots[b]
            for j in range(GROUP):
                chosen = chosen_slots(slot[:, j : j + 1], slots)
                picked[j, here, :] = dot(chosen, tile[...], ((1,), (0,))).astype(BF16)
        fetch(g).wait()
        total = conv_ref[...]
        for j in range(GROUP):
            total = total + dot(picked[j], weight[g * GROUP + j], ((1,), (0,)))
        conv_ref[...] = total
        return carry

    lax.fori_loop(0, groups, group, 0)


def inner_kernel(map_ref, own_ref, weight_hbm, conv_ref, chosen_map, *scratch):
    rows = own_ref.shape[0]
    chosen_map[...] = map_ref[:, BLOCK : rows - BLOCK]
    blocks = range(1, rows // BLOCK - 1)
    tiles = [own_ref.at[(b - 1) * BLOCK : (b + 2) * BLOCK] for b in blocks]
    first_slots = [rows - BLOCK + b * BLOCK for b in blocks]
    convolve(chosen_map, tiles, first_slots, weight_hbm, conv_ref, scratch)


def outer_kernel(
    filled_ref, odd_ref, map_ref, own_ref, even_ref, other_ref, inner_ref, weight_hbm,
    conv_ref, stats_ref, window_ref, chosen_map, *scratch,
):
    rows = own_ref.shape[0]
    odd = odd_ref[0] == 1
    window_ref[0:BLOCK, :] = jnp.where(odd, even_ref[...], other_ref[...])
    window_ref[BLOCK : rows + BLOCK, :] = own_ref[...]
    window_ref[rows + BLOCK :, :] = jnp.where(odd, other_ref[...], even_ref[...])
    chosen_map[:, 0:BLOCK] = map_ref[:, 0:BLOCK]
    chosen_map[:, BLOCK:] = map_ref[:, rows - BLOCK :]
    tiles = [window_ref.at[0 : 3 * BLOCK], window_ref.at[rows - BLOCK :]]
    first_slots = [rows - BLOCK, 2 * rows - 2 * BLOCK]
    convolve(chosen_map, tiles, first_slots, weight_hbm, conv_ref, scratch)
    filled = filled_ref[0]
    count = filled.astype(F32)
    conv = whole(inner_ref, conv_ref)
    occupied = occupied_rows(filled, rows)
    sums = jnp.sum(jnp.where(occupied, conv, 0.0), axis=0, keepdims=True)
    off = jnp.where(occupied, conv - sums / count, 0.0)
    squares = jnp.sum(off * off, axis=0, keepdims=True)
    stats_ref[...] = jnp.concatenate([sums, squares, jnp.full_like(sums, count)], axis=0)


def whole(inner_ref, outer_ref):
    return jnp.concatenate([outer_ref[0:BLOCK, :], inner_ref[...], outer_ref[BLOCK:, :]], axis=0)


def normalised(filled, inner_ref, outer_ref, stats_refs, gain_ref, shift_ref, cotangent_ref):
    conv = whole(inner_ref, outer_ref)
    sums, squares, total = merged(
        merged_moments, [[ref[i : i + 1, :] for i in range(3)] for ref in stats_refs]
    )
    center = sums / total
    inverse = lax.rsqrt(squares / total + EPSILON)
    occupied = occupied_rows(filled, conv.shape[0])
    normed = (conv - center) * inverse
    affine = gain_ref[...] * normed + shift_ref[...]
    upstream = jnp.where(occupied & (affine > 0.0), cotangent_ref[...].astype(F32), 0.0)
    return occupied, normed, affine, upstream, inverse, total


def norm_kernel(
    filled_ref, inner_ref, outer_ref, gain_ref, shift_ref, cotangent_ref, feature_ref, *refs
):
    *stats_refs, out_ref, sums_ref = refs
    occupied, normed, affine, upstream, _, _ = normalised(
        filled_ref[0], inner_ref, outer_ref, stats_refs, gain_ref, shift_ref, cotangent_ref
    )
    out = jnp.maximum(affine, 0.0) + feature_ref[...].astype(F32)
    out_ref[...] = jnp.where(occupied, out, 0.0).astype(BF16)
    sums_ref[...] = jnp.concatenate(
        [jnp.sum(upstream * normed, axis=0, keepdims=True), jnp.sum(upstream, axis=0, keepdims=True)],
        axis=0,
    )


def grad_conv_kernel(
    parts, filled_ref, inner_ref, outer_ref, gain_ref, shift_ref, cotangent_ref, *refs
):
    stats_refs, grads_refs, (grad_ref, sums_ref) = refs[:parts], refs[parts:-2], refs[-2:]
    occupied, normed, _, upstream, inverse, total = normalised(
        filled_ref[0], inner_ref, outer_ref, stats_refs, gain_ref, shift_ref, cotangent_ref
    )
    sums = merged(jnp.add, [ref[...] for ref in grads_refs])
    sums_ref[...] = sums
    grad_conv = gain_ref[...] * inverse * (
        upstream - sums[1:2, :] / total - normed * sums[0:1, :] / total
    )
    grad_ref[...] = jnp.where(occupied, grad_conv, 0.0).astype(BF16)


def gradient_kernel(
    place_ref, grad_own, grad_mate, map_own, map_mate, window_own, window_mate, *refs
):
    outs, scratch = refs[:6], refs[6:]
    index, picked, grad, turned, product, *staged, out_sem = scratch
    keep_one, send_one, keep_two, *sends_two = staged
    rows, channels = grad_own.shape
    core = place_ref[0]
    slots = lax.broadcasted_iota(jnp.int32, (BLOCK, 3 * BLOCK), 1).astype(jnp.int16)
    sides = ((map_own, window_own), (map_mate, window_mate))
    grad[0:rows, :] = grad_own[...]
    grad[rows:, :] = grad_mate[...]
    turned[...] = jnp.transpose(grad[...].astype(F32)).astype(BF16)
    for side, (map_ref, _) in enumerate(sides):
        index[side] = transposed_map(map_ref)

    def gradient(j, slot_of):
        for side, (_, window) in enumerate(sides):
            for b in range(rows // BLOCK):
                here = slice(b * BLOCK, (b + 1) * BLOCK)
                slot = slot_of(side)[here] - (rows + (b - 1) * BLOCK)
                chosen = chosen_slots(slot.astype(jnp.int16), slots)
                tile = window[b * BLOCK : (b + 3) * BLOCK, :]
                at = slice(side * rows + b * BLOCK, side * rows + (b + 1) * BLOCK)
                picked[j, at, :] = dot(chosen, tile, ((1,), (0,))).astype(BF16)
        product[j] = jnp.transpose(dot(turned[...], picked[j], ((1,), (0,))))

    def stored(staged, out, n):
        return pltpu.make_async_copy(staged, out, out_sem.at[n])

    shift = lax.rem(BLOCK - core * (HALF + 1), BLOCK)
    local = [pltpu.roll(index[side], shift, 1) for side in range(2)]
    size = channels // 8

    def rows_of(piece, place, size, first):
        at = lax.bitwise_xor(jnp.int32(piece), place) * size + first
        return pl.ds(pl.multiple_of(at, 16), size)

    for j in range(K_ONE):
        gradient(j, lambda side: local[side][:, j : j + 1])
        here = slice(j * size, (j + 1) * size)
        for piece in range(8):
            value = product[j, rows_of(piece, place_ref[1], size, 0), :]
            if piece < 4:
                keep_one[piece, here, :] = value
            else:
                send_one[piece - 4, here, :] = value.astype(BF16)
    copies = [stored(keep_one, outs[0], 0), stored(send_one, outs[1], 1)]
    for copy in copies:
        copy.start()
    for j in range(HALF - K_ONE + 1):
        whole_offset = j < HALF - K_ONE
        if whole_offset:
            gradient(j, lambda side: local[side][:, K_ONE + j : K_ONE + j + 1])
        else:
            gradient(j, lambda side: index[side][:, HALF : HALF + 1])
        count = size if whole_offset else size // 2
        first = 0 if whole_offset else core * (channels // 2)
        here = slice(j * size, j * size + count)
        for piece in range(8):
            value = product[j, rows_of(piece, place_ref[2], count, first), :]
            if piece < 2:
                keep_two[piece, here, :] = value
            else:
                sends_two[piece // 2 - 1][piece % 2, here, :] = value.astype(BF16)
    late = [stored(keep_two, outs[2], 2)]
    late += [stored(sends_two[n], outs[3 + n], 3 + n) for n in range(3)]
    for copy in late:
        copy.start()
    for copy in copies + late:
        copy.wait()


def scatter(step, grad, first_row, map_ref, weight_ref, windows):
    pushed = [dot(grad, weight_ref[j], ((1,), (1,))).astype(BF16) for j in range(GROUP)]
    named = [map_ref[step * GROUP + j, :][None] for j in range(GROUP)]
    for b, first_slot, sink in windows:
        rows = slice(b * BLOCK, (b + 1) * BLOCK)
        at = slice(first_row(b), first_row(b) + BLOCK)
        slots = lax.broadcasted_iota(jnp.int32, (sink.shape[0], BLOCK), 0) + first_slot
        chosen = jnp.concatenate(
            [chosen_slots(named[j][:, at], slots) for j in range(GROUP)],
            axis=1,
        )
        stacked = jnp.concatenate([pushed[j][rows] for j in range(GROUP)], axis=0)
        sink[...] = sink[...] + dot(chosen, stacked, ((1,), (0,)))


def edge_push_kernel(grad_ref, map_ref, weight_ref, before_ref, after_ref, before, after):
    step = pl.program_id(0)
    rows = map_ref.shape[1]

    @pl.when(step == 0)
    def _():
        before[...] = jnp.zeros_like(before)
        after[...] = jnp.zeros_like(after)

    def first_row(b):
        return b * (rows - BLOCK)

    windows = [(0, rows - BLOCK, before), (1, 2 * rows, after)]
    grad = jnp.concatenate([grad_ref[0:BLOCK, :], grad_ref[rows - BLOCK :, :]], axis=0)
    scatter(step, grad, first_row, map_ref, weight_ref, windows)

    @pl.when(step == pl.num_programs(0) - 1)
    def _():
        before_ref[...] = before[...].astype(BF16)
        after_ref[...] = after[...].astype(BF16)


def push_kernel(grad_ref, map_ref, weight_ref, own_ref):
    step = pl.program_id(0)
    rows = map_ref.shape[1]

    @pl.when(step == 0)
    def _():
        own_ref[...] = jnp.zeros_like(own_ref)

    windows = []
    for b in range(rows // BLOCK):
        start, stop = max(b - 1, 0) * BLOCK, min((b + 2) * BLOCK, rows)
        windows.append((b, rows + start, own_ref.at[start:stop]))
    scatter(step, grad_ref[...], lambda b: b * BLOCK, map_ref, weight_ref, windows)


def place_kernel(layout, places_ref, *refs):
    out_ref, sems = refs[-2:]
    size = out_ref.shape[1] // 8
    copies = []

    def put(source, out, part, piece, count, base):
        at = lax.bitwise_xor(jnp.int32(piece), places_ref[part]) * count + base
        here = pl.ds(pl.multiple_of(at, 16), count)
        copies.append(pltpu.make_async_copy(source, out.at[:, here, :], sems.at[len(copies)]))

    for n, (other, first_one, first_two) in enumerate(layout):
        one, two = refs[2 * n : 2 * n + 2]
        core = lax.bitwise_xor(places_ref[0], jnp.int32(other))
        first = core * (HALF + 1)
        for i in range(one.shape[0]):
            put(one.at[i], out_ref.at[pl.ds(first, K_ONE)], 1, first_one + i, size, 0)
        for i in range(two.shape[0]):
            piece = first_two + i
            source = two.at[i, pl.ds(0, (HALF - K_ONE) * size)]
            source = source.reshape(HALF - K_ONE, size, two.shape[2])
            put(source, out_ref.at[pl.ds(first + K_ONE, HALF - K_ONE)], 2, piece, size, 0)
            source = two.at[pl.ds(i, 1), pl.ds((HALF - K_ONE) * size, size // 2)]
            base = core * (out_ref.shape[1] // 2)
            put(source, out_ref.at[pl.ds(HALF, 1)], 2, piece, size // 2, base)
    for copy in copies:
        copy.start()
    for copy in copies:
        copy.wait()


def swap(value, by):
    peers = lax.axis_size("dp")
    return lax.ppermute(value, "dp", [(i, i ^ by) for i in range(peers)])


STAGES = {"c": (1,), "x": (2,), "z": (4, 8, 12)}


def part(terms, first, size):
    return functools.reduce(
        jnp.add, [term[first : first + size].astype(F32) for term in terms]
    )


def split(terms, stage):
    partners = STAGES[stage]
    size = terms[0].shape[0] // (len(partners) + 1)
    sends = [part(terms, (i + 1) * size, size).astype(BF16) for i in range(len(partners))]
    return part(terms, 0, size), sends


def swapped(sends, stage):
    return [swap(send, by) for send, by in zip(sends, STAGES[stage])]


def gather_start(piece, stage):
    return [swap(piece, by) for by in STAGES[stage]]


def summed_over_devices(one, two, grad_conv, sums, edge_push, push, spread, finish, place):
    parts, grad_conv = lax.optimization_barrier(((one, two), grad_conv))
    received = [swapped(sends, stage) for (_, sends), stage in zip(parts, "xz")]
    edges, sink = edge_push(grad_conv), push(grad_conv)
    received, edges, sink = lax.optimization_barrier((received, edges, sink))
    parts = [
        split([kept] + got, stage) for (kept, _), got, stage in zip(parts, received, "zx")
    ]
    parts, edges = lax.optimization_barrier((parts, edges))
    received = [swapped(sends, stage) for (_, sends), stage in zip(parts, "zx")]
    halo = spread(*edges)
    received, sink, sums = lax.optimization_barrier((received, sink, sums))
    pieces = [part([kept] + got, 0, 1) for (kept, _), got in zip(parts, received)]
    by = 16
    while by < lax.axis_size("dp"):
        pieces = [piece + swap(piece, by) for piece in pieces]
        by *= 2
    pieces = [piece.astype(BF16) for piece in pieces]
    pieces, sink = lax.optimization_barrier((pieces, sink))
    results = finish(sink, halo, sums)
    received = [gather_start(piece, stage) for piece, stage in zip(pieces, "zx")]
    received, pieces, results = lax.optimization_barrier((received, pieces, results))
    early = [jnp.concatenate([piece] + got, axis=0) for piece, got in zip(pieces, received)]
    received = [gather_start(piece, stage) for piece, stage in zip(early, "xz")]
    received, results = lax.optimization_barrier((received, (results, place(early))))
    late = [jnp.concatenate(got, axis=0) for got in received]
    other = [swap(jnp.concatenate(pair, axis=0), 1) for pair in zip(early, late)]
    return late, other, results


def exchanged(value, merge):
    received = [swap(value, by) for by in (1, 2, 3)]
    value = merged(merge, [value] + received)
    by = 16
    while by < lax.axis_size("dp"):
        value = merge(value, swap(value, by))
        by *= 2
    return [value] + [swap(value, by) for by in (4, 8, 12)]


def stacked_moments(one, two):
    return jnp.stack(merged_moments(one, two))


def per_device(features, kernel_map, occupancy, weights, bn_gain, bn_shift, cotangent):
    rows, channels = features.shape
    peers = lax.axis_size("dp")
    me = lax.axis_index("dp")
    blocks = rows // BLOCK
    inner_rows = rows - 2 * BLOCK
    steps = K // GROUP

    odd = me & 1
    even_pairs = [(i, i ^ 1) for i in range(peers)]
    other_pairs = [(i, ((i + 1) ^ 1) - 1) for i in range(1, peers - 1)]

    def neighbours_swap(to_before, to_after):
        even = lax.ppermute(jnp.where(odd == 1, to_before, to_after), "dp", even_pairs)
        other = lax.ppermute(jnp.where(odd == 1, to_after, to_before), "dp", other_pairs)
        return even, other

    even, other = neighbours_swap(features[:BLOCK], features[rows - BLOCK :])
    map_rows = jnp.transpose(kernel_map)
    map_mate = swap(map_rows, 1)
    odd_flag = odd.reshape(1)

    gain = bn_gain.reshape(1, channels)
    shift = bn_shift.reshape(1, channels)
    smem = pl.BlockSpec(memory_space=pltpu.SMEM)
    vmem = pl.BlockSpec(memory_space=pltpu.VMEM)
    hbm = pl.BlockSpec(memory_space=pltpu.HBM)
    anywhere = pl.BlockSpec(memory_space=pl.ANY)
    groups = K // GROUP
    work = K * rows * channels * 2 * (3 * BLOCK + channels)
    moved = K * channels * channels * 2 * 3

    half_conv = jax.ShapeDtypeStruct((2 * BLOCK, channels), F32)
    scratch = [
        pltpu.VMEM((K, 2 * BLOCK), jnp.int32),
        pltpu.VMEM((K, channels, channels), BF16),
        pltpu.VMEM((GROUP, 2 * BLOCK, channels), BF16),
        pltpu.VMEM((2 * BLOCK, BLOCK), jnp.int32),
        pltpu.SemaphoreType.DMA((groups,)),
    ]

    def in_hbm(value):
        return pltpu.with_memory_space_constraint(value, pltpu.HBM)

    inner = pl.pallas_call(
        inner_kernel,
        in_specs=[vmem, vmem, hbm],
        out_specs=vmem,
        out_shape=half_conv,
        scratch_shapes=scratch,
        compiler_params=params(LIMIT),
        cost_estimate=cost(work / 2, moved),
        name="conv_inner",
    )(in_hbm(map_rows), in_hbm(features), in_hbm(weights))

    outer, stats, window = pl.pallas_call(
        outer_kernel,
        in_specs=[smem, smem, vmem, vmem, vmem, vmem, vmem, hbm],
        out_specs=[vmem, vmem, vmem],
        out_shape=[
            half_conv,
            jax.ShapeDtypeStruct((3, channels), F32),
            jax.ShapeDtypeStruct((rows + 2 * BLOCK, channels), BF16),
        ],
        scratch_shapes=scratch,
        compiler_params=params(LIMIT),
        cost_estimate=cost(work / 2, moved),
        name="conv_outer",
    )(occupancy, odd_flag, map_rows, features, even, other, inner, in_hbm(weights))

    window_mate = swap(window, 1)
    stats = exchanged(stats, stacked_moments)

    block_out, sums = pl.pallas_call(
        norm_kernel,
        in_specs=[smem] + [vmem] * 10,
        out_shape=[
            jax.ShapeDtypeStruct((rows, channels), BF16),
            jax.ShapeDtypeStruct((2, channels), F32),
        ],
        compiler_params=params(LIMIT),
        cost_estimate=cost(rows * channels * 20, rows * channels * 10),
        name="norm",
    )(occupancy, inner, outer, gain, shift, cotangent, features, *stats)

    grads = exchanged(sums, jnp.add)

    grad_conv, sums = pl.pallas_call(
        functools.partial(grad_conv_kernel, len(stats)),
        in_specs=[smem] + [vmem] * 13,
        out_shape=[
            jax.ShapeDtypeStruct((rows, channels), BF16),
            jax.ShapeDtypeStruct((2, channels), F32),
        ],
        compiler_params=params(LIMIT),
        cost_estimate=cost(rows * channels * 20, rows * channels * 8),
        name="grad_conv",
    )(occupancy, inner, outer, gain, shift, cotangent, *stats, *grads)
    grad_mate = swap(grad_conv, 1)

    core, lane, depth = me & 1, (me >> 1) & 1, (me >> 2) & 3
    places = jnp.stack([core, lane * 4 + depth, depth * 2 + lane])
    size = channels // 8
    rows_one, rows_two = K_ONE * size, (HALF - K_ONE) * size + size // 2
    shapes = [((4, rows_one, channels), F32), ((4, rows_one, channels), BF16)]
    shapes += [((2, rows_two, channels), F32)] + [((2, rows_two, channels), BF16)] * 3
    keep_one, send_one, keep_two, *sends_two = pl.pallas_call(
        gradient_kernel,
        in_specs=[smem] + [vmem] * 6,
        out_specs=[anywhere] * 6,
        out_shape=[jax.ShapeDtypeStruct(*shape) for shape in shapes],
        scratch_shapes=[
            pltpu.VMEM((2, rows, BLOCK), jnp.int32),
            pltpu.VMEM((K_ONE, 2 * rows, channels), BF16),
            pltpu.VMEM((2 * rows, channels), BF16),
            pltpu.VMEM((channels, 2 * rows), BF16),
            pltpu.VMEM((K_ONE, channels, channels), F32),
        ]
        + [pltpu.VMEM(*shape) for shape in shapes]
        + [pltpu.SemaphoreType.DMA((6,))],
        compiler_params=params(LIMIT),
        cost_estimate=cost(work, K * channels * channels * 6),
        name="weight_gradient",
    )(places, grad_conv, grad_mate, map_rows, map_mate, window, window_mate)
    one, two = (keep_one, [send_one]), (keep_two, sends_two)

    weight_spec = pl.BlockSpec((GROUP, channels, channels), lambda s: (s, 0, 0))

    push_grid = dict(
        grid=(groups,),
        compiler_params=params(LIMIT),
        cost_estimate=cost(1000, 1000),
    )

    def edge_push(grad_conv):
        edge = jax.ShapeDtypeStruct((BLOCK, channels), BF16)
        before, after = pl.pallas_call(
            edge_push_kernel,
            in_specs=[full((rows, channels)), full((K, rows)), weight_spec],
            out_specs=[full((BLOCK, channels))] * 2,
            out_shape=[edge, edge],
            scratch_shapes=[pltpu.VMEM((BLOCK, channels), F32)] * 2,
            name="push_edges",
            **push_grid,
        )(grad_conv, map_rows, weights)
        return before, after

    def push(grad_conv):
        return pl.pallas_call(
            push_kernel,
            in_specs=[full((rows, channels)), full((K, rows)), weight_spec],
            out_specs=full((rows, channels)),
            out_shape=jax.ShapeDtypeStruct((rows, channels), F32),
            name="push",
            **push_grid,
        )(grad_conv, map_rows, weights)

    def finish(sink, halo, sums):
        even, other = halo
        from_prev = jnp.where(odd == 1, even, other).astype(F32)
        from_next = jnp.where(odd == 1, other, even).astype(F32)
        occupied = occupied_rows(occupancy[0], rows)
        received = jnp.concatenate(
            [
                sink[:BLOCK] + from_prev,
                sink[BLOCK : rows - BLOCK],
                sink[rows - BLOCK :] + from_next,
            ],
            axis=0,
        )
        total = jnp.where(occupied, cotangent.astype(F32), 0.0) + received
        return total.astype(BF16), sums[0], sums[1]


    def placed(layout, sources, *into):
        count = sum(one.shape[0] + two.shape[0] * 2 for one, two in sources)
        operands = []
        for one, two in sources:
            operands += [one.reshape(one.shape[0], K_ONE, size, channels), two]
        return pl.pallas_call(
            functools.partial(place_kernel, layout),
            in_specs=[smem] + [anywhere] * len(operands) + [hbm] * len(into),
            out_specs=hbm,
            out_shape=jax.ShapeDtypeStruct(weights.shape, BF16),
            scratch_shapes=[pltpu.SemaphoreType.DMA((count,))],
            input_output_aliases={len(operands) + 1: 0} if into else {},
            compiler_params=params(LIMIT),
            cost_estimate=cost(0, K * channels * channels * 2),
            name="place",
        )(places, *operands, *into)

    def place_early(own):
        return placed(((0, 0, 0),), (own,))

    late, other_pieces, results = summed_over_devices(
        one, two, grad_conv, sums, edge_push, push, neighbours_swap, finish, place_early
    )
    (grad_features, grad_gain, grad_shift), grad_weights = results
    first_late = (8 - late[0].shape[0], 8 - late[1].shape[0])
    grad_weights = placed(((0, *first_late),), (late,), grad_weights)
    grad_weights = placed(((1, 0, 0),), (other_pieces,), grad_weights)
    return block_out, grad_features, grad_weights, grad_gain, grad_shift


def solution(mesh):
    in_specs = (
        P(("parts", "dp"), None),
        P(("parts", "dp"), None),
        P(("parts", "dp")),
        P(),
        P(),
        P(),
        P(("parts", "dp"), None),
    )
    out_specs = (
        P(("parts", "dp"), None),
        P(("parts", "dp"), None),
        P("parts", None, None),
        P("parts"),
        P("parts"),
    )
    return jax.shard_map(
        per_device, mesh=mesh, in_specs=in_specs, out_specs=out_specs, check_vma=False
    )
```
